32 devices in a mesh: dp: 4 (over y, core), expert: 8 (over z, x).
Axes of the slice: x: 2, y: 2, z: 4, core: 2. Of those that a mesh axis runs over, the one named last changes fastest.
Arguments:
- frames_in: bfloat16 [32, 256, 1024], P(('dp', 'expert')), may hold values from -6 to 6
- pit_order: int32 [16, 2], replicated, may hold values from 0 to 1, each once within a row
- expert_ids: int32 [32, 256, 2], P(('dp', 'expert')), may hold values from 0 to 7, all different within a row; in each aligned block of 256 rows (0 to 255, 256 to 511, ..., all dimensions but the last counted through in order) at most 80 rows name the same one
- norm_gains: float32 [2, 1024], replicated, may hold values from 0.25 to 1.75
- attn_qkv: bfloat16 [3, 1024, 1024], P(None, 'expert'), may hold values from -6 to 6
- attn_out: bfloat16 [1024, 1024], P('expert'), may hold values from -0.1875 to 0.1875
- router: float32 [1024, 8], replicated, may hold values from -0.046875 to 0.046875
- expert_in: bfloat16 [8, 1024, 4096], P('expert', None, 'dp'), may hold values from -0.1875 to 0.1875
- expert_out: bfloat16 [8, 4096, 1024], P('expert', 'dp'), may hold values from -0.09375 to 0.09375
Outputs:
- layer_out: bfloat16 [32, 256, 1024], P(('dp', 'expert'))
The draws below stay inside these ranges and needn't reach their ends.
Inputs may be any that keep to these rules, and one draw needn't show every extreme that they name: `expert_ids`: at most 80 frames of one stream name the same expert, and in every draw some stream names some expert exactly 80 times; each frame names 2 different experts.
All inputs are finite; a program needn't handle non-finite values.
Results may differ from the reference program's by a relative error of at most 0.011.
Values may be sent and summed in bfloat16 or wider, within the bound.
No kernel may reach another device: no remote copies, remote signals or barrier semaphores. Data moves between devices by JAX's collectives and lax.ppermute only.
A program may use at most 128 MiB of HBM per device.

```python
import math
import jax
import jax.numpy as jnp
import numpy as np
from jax import lax

D = 1024
FF = 4096
HEADS = 16
HEAD_DIM = 64
TOP = 2
FRAMES = 256
EXPERTS = 8
CAP = 80
STREAMS = 32
MEETINGS = 16
N_DP = 4


def draw_attn_qkv(key, part):
    base = jnp.clip(jax.random.normal(key, (3, D, D), jnp.float32), -6.0, 6.0) * D ** (-0.5)
    return jnp.clip(base, -6.0, 6.0).astype(jnp.bfloat16)


def shard_levels(own_key, extent, split, smallest, top_value):
    level, own = 1.0, jax.random.fold_in(own_key, 6)
    for axis_at, blocks in split:
        draws = jnp.exp(jax.random.uniform(jax.random.fold_in(own, axis_at), (blocks,), jnp.float32, smallest / len(split), top_value / len(split)))
        level = level * jnp.repeat(draws, extent[axis_at] // blocks).reshape([-1 if axis == axis_at else 1 for axis in range(len(extent))])
    return level


def shared_out(rng, own, number, rows, amount, top, most, skew):
    ranking = jax.random.permutation(rng, amount)
    crowded, common = portions_of(amount, rows * top, most, skew, True), portions_of(amount, rows * top, most, skew, False)
    places = jnp.arange(amount)

    def named(sizes, turn):
        used = int((sizes > 0).sum())
        fixed = max(1, used // 4)
        shifted = fixed + (places - fixed + turn * (used - fixed)) % max(1, amount - fixed)
        return jnp.zeros((amount,), jnp.int32).at[ranking[jnp.where(places < fixed, places, shifted)]].set(jnp.asarray(sizes, jnp.int32))

    sizes = jnp.where(number % 4 == 0, named(crowded, number // 4), named(common, number - number // 4 - 1))
    mixed = jax.random.permutation(jax.random.fold_in(own, 3), amount)
    source_of, taker = mixed[0:amount // 2 * 2:2], mixed[1:amount // 2 * 2:2]
    slack = jnp.minimum(sizes[source_of] - 1, most - sizes[taker]) // 2
    slack = jnp.where((source_of == ranking[0]) | (taker == ranking[0]) | (sizes[taker] == 0), 0, jnp.maximum(slack, 0))
    shifted = jax.random.randint(jax.random.fold_in(own, 4), (amount // 2,), 0, 1 << 20) % (slack + 1)
    sizes = sizes.at[source_of].add(-shifted).at[taker].add(shifted)
    labels = jnp.searchsorted(jnp.cumsum(sizes), jnp.arange(rows * top), side="right").astype(jnp.int32)
    table = labels.reshape(top, rows).T
    table = table[jax.random.permutation(jax.random.fold_in(own, 1), rows)]
    turn = jax.random.randint(jax.random.fold_in(own, 2), (rows, 1), 0, top)
    return jnp.take_along_axis(table, (jnp.arange(top)[None, :] + turn) % top, axis=1)


def portions_of(count, total, limit, lean, full):
    weights = [(1 << 20) // math.isqrt(standing ** lean) + 1 for standing in range(1, count + 1)]
    largest = limit if full else min(limit, max(-(-total // count), total * weights[0] // sum(weights)))
    least = 1 if total - largest >= count - 1 else 0
    counts, spare = [largest] + [least] * (count - 1), total - largest - least * (count - 1)
    while spare > 0:
        movable = [i for i in range(1, count) if counts[i] < largest] or [i for i in range(1, count) if counts[i] < limit]
        whole, budget = sum([weights[i] for i in movable]), spare
        for i in movable:
            extra = min(limit - counts[i], max(1, budget * weights[i] // whole), spare)
            counts[i] = counts[i] + extra
            spare = spare - extra
    return np.array(counts)


def scatter_about(stream_key, dims, scale, bound, cuts=(), kind=jnp.bfloat16):
    values = jax.random.normal(stream_key, dims, jnp.float32) * scale
    if len(cuts) > 0:
        values = shard_levels(stream_key, dims, cuts, -0.22, 0.18) * values
    return jnp.clip(values, min=-bound, max=bound).astype(kind)


def setup_inputs(seed: int = 0) -> dict:
    key_list = jax.random.split(jax.random.key(seed), 10)
    frames_in = scatter_about(key_list[0], (STREAMS, FRAMES, D), 1.0, 6.0, ((0, 32),))
    pit_order = jax.vmap(lambda own: jax.random.permutation(own, 2))(jax.random.split(key_list[1], MEETINGS)).reshape((MEETINGS, 2)).astype(jnp.int32)
    expert_ids_keys = jax.random.split(jax.random.fold_in(key_list[2], 1), STREAMS * FRAMES // FRAMES)
    expert_ids_turns = jax.random.permutation(jax.random.fold_in(key_list[2], 3), STREAMS * FRAMES // FRAMES)
    expert_ids = jax.vmap(lambda own, number: shared_out(jax.random.fold_in(key_list[2], 2), own, number, FRAMES, EXPERTS, TOP, CAP, 2))(expert_ids_keys, expert_ids_turns).reshape((STREAMS, FRAMES, TOP))
    norm_gains = jnp.clip(1.0 + 0.15 * jax.random.normal(key_list[3], (2, D), jnp.float32), 0.25, 1.75)
    attn_qkv = draw_attn_qkv(jax.random.fold_in(key_list[9], 71), 0)
    attn_out = scatter_about(key_list[5], (D, D), D ** -0.5, 0.1875, ((0, 8),))
    router = scatter_about(key_list[6], (D, EXPERTS), (16 * D) ** -0.5, 0.046875, (), jnp.float32)
    expert_in = scatter_about(key_list[7], (EXPERTS, D, FF), D ** -0.5, 0.1875, ((0, 8), (2, 4)))
    expert_out = scatter_about(key_list[8], (EXPERTS, FF, D), FF ** -0.5, 0.09375, ((0, 8), (1, 4)))
    return {"frames_in": frames_in, "pit_order": pit_order, "expert_ids": expert_ids, "norm_gains": norm_gains, "attn_qkv": attn_qkv, "attn_out": attn_out, "router": router, "expert_in": expert_in, "expert_out": expert_out}


epsilon = 1e-05

def layer_norm(values, gain):
    mean = lax.optimization_barrier(jnp.mean(values, axis=-1, keepdims=True))
    centred = values - mean
    spread = lax.optimization_barrier(jnp.mean(centred * centred, axis=-1, keepdims=True))
    return centred * lax.rsqrt(spread + epsilon) * gain

def attend(stream, norm_gains, attn_qkv, attn_out):
    resid = stream.astype(jnp.float32)
    normed = layer_norm(resid, norm_gains[0]).astype(jnp.bfloat16)
    query = jnp.dot(normed, attn_qkv[0], preferred_element_type=jnp.float32).astype(jnp.bfloat16)
    keys = jnp.dot(normed, attn_qkv[1], preferred_element_type=jnp.float32).astype(jnp.bfloat16)
    values = jnp.dot(normed, attn_qkv[2], preferred_element_type=jnp.float32).astype(jnp.bfloat16)
    query = query.reshape(FRAMES, HEADS, HEAD_DIM).astype(jnp.float32)
    keys = keys.reshape(FRAMES, HEADS, HEAD_DIM).astype(jnp.float32)
    values = values.reshape(FRAMES, HEADS, HEAD_DIM).astype(jnp.float32)
    scores = jnp.einsum('qhd,khd->hqk', query, keys) / HEAD_DIM ** 0.5
    top = lax.optimization_barrier(jnp.max(scores, axis=-1, keepdims=True))
    weights = jnp.exp(scores - top)
    probs = (weights / lax.optimization_barrier(jnp.sum(weights, axis=-1, keepdims=True))).astype(jnp.bfloat16)
    context = jnp.einsum('hqk,khd->qhd', probs.astype(jnp.float32), values)
    context = context.reshape(FRAMES, D).astype(jnp.bfloat16)
    attended = jnp.dot(context, attn_out, preferred_element_type=jnp.float32)
    mixed = (resid + attended).astype(jnp.bfloat16)
    normed2 = layer_norm(mixed.astype(jnp.float32), norm_gains[1]).astype(jnp.bfloat16)
    return (mixed, normed2)

def slot_positions(ids):
    flat = ids.reshape(-1).astype(jnp.int32)
    onehot = (flat[:, None] == jnp.arange(EXPERTS, dtype=jnp.int32)[None, :]).astype(jnp.int32)
    ranks = lax.optimization_barrier(jnp.sum(onehot * (jnp.cumsum(onehot, axis=0) - 1), axis=1)).astype(jnp.int32)
    return (flat * CAP + ranks).astype(jnp.int32)

def fill_slots(rows, positions):
    return jnp.zeros((EXPERTS * CAP, D), jnp.bfloat16).at[positions].set(rows)

def run_expert(inputs):
    rows, first, second = inputs
    hidden = jax.nn.silu(jnp.dot(rows, first, preferred_element_type=jnp.float32)).astype(jnp.bfloat16)
    width = FF // N_DP
    total = jnp.zeros((rows.shape[0], D), jnp.float32)
    for index in range(N_DP):
        part = jnp.dot(hidden[:, index * width:(index + 1) * width], second[index * width:(index + 1) * width], preferred_element_type=jnp.float32).astype(jnp.bfloat16)
        part = lax.optimization_barrier(part)
        total = total + part.astype(jnp.float32)
    return total.astype(jnp.bfloat16)

def reference(frames_in, pit_order, expert_ids, norm_gains, attn_qkv, attn_out, router, expert_in, expert_out):
    pairs = frames_in.reshape(2, MEETINGS, FRAMES, D)
    first = jnp.where((pit_order[:, 0] == 0)[:, None, None], pairs[0], pairs[1])
    second = jnp.where((pit_order[:, 1] == 0)[:, None, None], pairs[0], pairs[1])
    streams = jnp.concatenate([first, second], axis=0)
    mixed, normed2 = lax.map(lambda one: attend(one, norm_gains, attn_qkv, attn_out), streams)
    logits = jnp.dot(normed2.reshape(STREAMS * FRAMES, D).astype(jnp.float32), router, precision=lax.Precision.HIGHEST)
    logits = logits.reshape(STREAMS, FRAMES, EXPERTS)
    picked = jnp.take_along_axis(logits, expert_ids, axis=2)
    gate0 = jax.nn.sigmoid(picked[:, :, 0] - picked[:, :, 1])
    gate1 = 1.0 - gate0
    positions = jax.vmap(slot_positions)(expert_ids)
    rows = jnp.repeat(normed2, TOP, axis=1)
    slots = jax.vmap(fill_slots)(rows, positions)
    slots = slots.reshape(STREAMS, EXPERTS, CAP, D).transpose(1, 0, 2, 3).reshape(EXPERTS, STREAMS * CAP, D)
    answer = lax.map(run_expert, (slots, expert_in, expert_out))
    answer = answer.reshape(EXPERTS, STREAMS, CAP, D).transpose(1, 0, 2, 3).reshape(STREAMS, EXPERTS * CAP, D)
    back = jax.vmap(lambda table, where: table[where])(answer, positions)
    back = back.reshape(STREAMS, FRAMES, TOP, D).astype(jnp.float32)
    result = mixed.astype(jnp.float32) + gate0[:, :, None] * back[:, :, 0] + gate1[:, :, None] * back[:, :, 1]
    return result.astype(jnp.bfloat16)
```

```python
import functools

import jax
import jax.numpy as jnp
from jax import lax
from jax.experimental import pallas as pl
from jax.experimental.pallas import tpu as pltpu
from jax.sharding import PartitionSpec as P

HEAD_DIM = 64
epsilon = 1e-05
BF16 = jnp.bfloat16
F32 = jnp.float32
VMEM = pl.BlockSpec(memory_space=pltpu.VMEM)
SMEM = pl.BlockSpec(memory_space=pltpu.SMEM)
ANY = pl.BlockSpec(memory_space=pl.ANY)


def params(mib):
    return pltpu.CompilerParams(vmem_limit_bytes=mib << 20)


def cost(flops, moved, special=0):
    return pl.CostEstimate(flops=flops, bytes_accessed=moved, transcendentals=special)


def swap(block, axis, mask):
    count = lax.axis_size(axis)
    return lax.ppermute(block, axis, [(i, i ^ mask) for i in range(count)])


def layer_norm(values, gain):
    mean = jnp.mean(values, axis=-1, keepdims=True)
    centred = values - mean
    spread = jnp.mean(centred * centred, axis=-1, keepdims=True)
    return centred * lax.rsqrt(spread + epsilon) * gain


def norm_kernel(count, place_ref, gain_ref, *refs):
    raw, (normed_ref, own_ref) = refs[:count], refs[count:]
    gain = gain_ref[0:1, :]
    for k in range(count):
        where = place_ref[k]
        block = raw[k][0]
        normed_ref[where] = layer_norm(block.astype(F32), gain).astype(BF16)

        @pl.when(where == 0)
        def _():
            own_ref[...] = block


def attention_kernel(count, shards, me_ref, normed_ref, *refs):
    pieces, outs = refs[:shards], refs[shards : shards + count]
    weights, sems = refs[shards + count :]
    depth, cols = pieces[0].shape[1:]
    me = me_ref[0]
    copies = []
    for k in range(shards):
        rows = pl.ds(pl.multiple_of((me ^ k) * depth, depth), depth)
        copy = pltpu.make_async_copy(pieces[k], weights.at[:, rows, :], sems.at[k])
        copy.start()
        copies.append(copy)
    for copy in copies:
        copy.wait()
    frames = normed_ref.shape[1]
    head = lax.broadcasted_iota(jnp.int32, (frames, cols), 1) // HEAD_DIM
    scale = HEAD_DIM**-0.5
    for k in range(count):
        x = normed_ref[k]
        q, key, val = [
            jnp.dot(x, weights[i], preferred_element_type=F32).astype(BF16) for i in range(3)
        ]
        q = q * jnp.asarray(scale, BF16)
        total = jnp.zeros((frames, cols), F32)
        for h in range(cols // HEAD_DIM):
            mine = head == h
            scores = lax.dot_general(
                jnp.where(mine, q, jnp.zeros_like(q)),
                key,
                (((1,), (1,)), ((), ())),
                preferred_element_type=F32,
            )
            exps = jnp.exp(scores - jnp.max(scores, axis=-1, keepdims=True))
            norm = 1.0 / jnp.sum(exps, axis=-1, keepdims=True)
            probs = (exps * norm).astype(BF16)
            total = jnp.where(mine, jnp.dot(probs, val, preferred_element_type=F32), total)
        outs[k][...] = total.astype(BF16)


def mix_kernel(count, experts, capacity, me_ref, own_ref, proj_ref, gain_ref, router_ref, rows_ref, cols_ref, *refs):
    blocks, (slots_ref, mixed_ref, gate_ref) = refs[:count], refs[count:]
    frames, depth = blocks[0].shape
    me = me_ref[0]
    total = own_ref[...].astype(F32)
    for k in range(count):
        rows = pl.ds(pl.multiple_of((me ^ k) * depth, depth), depth)
        total += jnp.dot(blocks[k][...], proj_ref[rows, :], preferred_element_type=F32)
    mixed = total.astype(BF16)
    mixed_ref[...] = mixed
    normed = layer_norm(mixed.astype(F32), gain_ref[1:2, :]).astype(BF16)
    first, second = rows_ref[0:1, :], rows_ref[1:2, :]
    which = lax.broadcasted_iota(jnp.int32, (experts, frames), 0)
    named = ((which == first) | (which == second)).astype(F32)
    before = (
        lax.broadcasted_iota(jnp.int32, (frames, frames), 0)
        < lax.broadcasted_iota(jnp.int32, (frames, frames), 1)
    ).astype(F32)
    rank = jnp.dot(named, before, preferred_element_type=F32) + (which * capacity).astype(F32)
    slot = lax.broadcasted_iota(jnp.int32, (experts * capacity, frames), 0).astype(F32)
    place0 = jnp.sum(jnp.where(which == first, rank, 0.0), axis=0, keepdims=True)
    place1 = jnp.sum(jnp.where(which == second, rank, 0.0), axis=0, keepdims=True)
    spread = ((slot == place0) | (slot == place1)).astype(F32).astype(BF16)
    slots_ref[...] = jnp.dot(spread, normed, preferred_element_type=F32).astype(BF16)
    high = router_ref[...].astype(BF16)
    rest = router_ref[...] - high.astype(F32)
    middle = rest.astype(BF16)
    low = (rest - middle.astype(F32)).astype(BF16)
    logits = (
        jnp.dot(normed, low, preferred_element_type=F32)
        + jnp.dot(normed, middle, preferred_element_type=F32)
    ) + jnp.dot(normed, high, preferred_element_type=F32)
    lane = lax.broadcasted_iota(jnp.int32, (frames, experts), 1)
    ahead = jnp.sum(jnp.where(lane == cols_ref[:, 0:1], logits, 0.0), axis=1, keepdims=True)
    behind = jnp.sum(jnp.where(lane == cols_ref[:, 1:2], logits, 0.0), axis=1, keepdims=True)
    gate_ref[...] = jnp.broadcast_to(jax.nn.sigmoid(ahead - behind), gate_ref.shape)


def expert_kernel(count, order, slots_ref, *refs):
    firsts, seconds, answer_ref = refs[:count], refs[count : 2 * count], refs[2 * count]
    first_buf, second_buf, total, sems = refs[2 * count + 1 :]
    copies = []
    for at, k in enumerate(order):
        pair = (
            pltpu.make_async_copy(firsts[k].at[0], first_buf.at[at], sems.at[0, at]),
            pltpu.make_async_copy(seconds[k].at[0], second_buf.at[at], sems.at[1, at]),
        )
        pair[0].start()
        pair[1].start()
        copies.append(pair)
    width = first_buf.shape[2]
    step = min(512, width)
    for at in range(count):
        copies[at][0].wait()
        copies[at][1].wait()
        for part in range(0, width, step):
            up = jnp.dot(
                slots_ref[...], first_buf[at, :, part : part + step], preferred_element_type=F32
            )
            half = 0.5 * up
            hidden = (half + half * jnp.tanh(half)).astype(BF16)
            down = jnp.dot(
                hidden, second_buf[at, part : part + step, :], preferred_element_type=F32
            )
            if at == 0 and part == 0:
                total[...] = down
            elif at == count - 1 and part + step == width:
                answer_ref[...] = (total[...] + down).astype(BF16)
            else:
                total[...] += down


def combine_kernel(experts, capacity, answer_ref, mixed_ref, gate_ref, cols_ref, out_ref):
    frames = mixed_ref.shape[0]
    first, second = cols_ref[:, 0:1], cols_ref[:, 1:2]
    lane = lax.broadcasted_iota(jnp.int32, (frames, experts), 1)
    named = ((lane == first) | (lane == second)).astype(F32)
    before = (
        lax.broadcasted_iota(jnp.int32, (frames, frames), 1)
        < lax.broadcasted_iota(jnp.int32, (frames, frames), 0)
    ).astype(F32)
    rank = jnp.dot(before, named, preferred_element_type=F32) + (lane * capacity).astype(F32)
    slot = lax.broadcasted_iota(jnp.int32, (frames, experts * capacity), 1).astype(F32)
    back = []
    for chosen in (first, second):
        place = jnp.sum(jnp.where(lane == chosen, rank, 0.0), axis=1, keepdims=True)
        pick = (slot == place).astype(F32).astype(BF16)
        back.append(jnp.dot(pick, answer_ref[...], preferred_element_type=F32))
    gate = gate_ref[:, 0:1]
    result = mixed_ref[...].astype(F32) + gate * back[0] + (1.0 - gate) * back[1]
    out_ref[0] = result.astype(BF16)


def body(
    frames_in, pit_order, expert_ids, norm_gains, attn_qkv, attn_out, router, expert_in, expert_out
):
    dp_count = lax.axis_size("dp")
    exp_count = lax.axis_size("expert")
    me = lax.axis_index("dp").astype(jnp.int32)
    exp_index = lax.axis_index("expert").astype(jnp.int32)
    frames, width = frames_in.shape[1:]
    top = expert_ids.shape[2]
    capacity = frames * top * 5 // (4 * exp_count)
    slots_count = exp_count * capacity
    half = dp_count // 2
    share = width // dp_count
    me_arr = me[None]

    own_cols = lax.dynamic_slice_in_dim(attn_qkv, me * share, share, axis=2)
    qkv = {0: own_cols}
    for far in range(2, exp_count, 2):
        qkv[far] = swap(own_cols, "expert", far)
    for far in range(0, exp_count, 2):
        qkv[far | 1] = swap(qkv[far], "expert", 1)

    raw = {0: frames_in}
    bit = half
    while bit:
        for k in list(raw):
            raw[k | bit] = swap(raw[k], "dp", bit)
        bit //= 2

    proj_rows = attn_out.shape[0] // dp_count
    proj = lax.all_gather(
        lax.dynamic_slice_in_dim(attn_out, me * proj_rows, proj_rows, axis=0),
        ("expert", "dp"),
        axis=0,
        tiled=True,
    )

    expert_in, expert_out, raw[half] = lax.optimization_barrier((expert_in, expert_out, raw[half]))
    firsts, seconds = {0: expert_in}, {0: expert_out}
    bit = half
    while bit:
        for held in (firsts, seconds):
            for k in list(held):
                held[k | bit] = swap(held[k], "dp", bit)
        bit //= 2

    member = jnp.arange(dp_count, dtype=jnp.int32)
    meeting = ((me ^ member) % half) * exp_count + exp_index
    place = jnp.where(pit_order[meeting, 0] == 0, member, member ^ half)

    normed, stream = pl.pallas_call(
        functools.partial(norm_kernel, dp_count),
        out_shape=(
            jax.ShapeDtypeStruct((dp_count, frames, width), BF16),
            jax.ShapeDtypeStruct((frames, width), BF16),
        ),
        in_specs=[SMEM, VMEM] + [VMEM] * dp_count,
        out_specs=(VMEM, VMEM),
        compiler_params=params(32),
        cost_estimate=cost(dp_count * frames * width * 8, dp_count * frames * width * 4),
        name="norm",
    )(place, norm_gains, *[raw[k] for k in range(dp_count)])

    contexts = pl.pallas_call(
        functools.partial(attention_kernel, dp_count, exp_count),
        out_shape=[jax.ShapeDtypeStruct((frames, share), BF16)] * dp_count,
        in_specs=[SMEM, VMEM] + [ANY] * exp_count,
        out_specs=[VMEM] * dp_count,
        scratch_shapes=[
            pltpu.VMEM((3, width, share), BF16),
            pltpu.SemaphoreType.DMA((exp_count,)),
        ],
        compiler_params=params(32),
        cost_estimate=cost(
            2 * frames * width * width * 3 + 16 * frames * frames * width, 5 << 20, frames * frames * 16
        ),
        name="attention",
    )(exp_index[None], normed, *[qkv[k] for k in range(exp_count)])

    blocks = [contexts[0]] + [swap(contexts[k], "dp", k) for k in range(1, dp_count)]

    cols = expert_ids[0]
    rows = cols.T
    slots, mixed, gate = pl.pallas_call(
        functools.partial(mix_kernel, dp_count, exp_count, capacity),
        out_shape=(
            jax.ShapeDtypeStruct((slots_count, width), BF16),
            jax.ShapeDtypeStruct((frames, width), BF16),
            jax.ShapeDtypeStruct((frames, 128), F32),
        ),
        in_specs=[SMEM] + [VMEM] * (6 + dp_count),
        out_specs=(VMEM, VMEM, VMEM),
        compiler_params=params(32),
        cost_estimate=cost(2 * frames * width * (width + slots_count), 5 << 20),
        name="mix",
    )(me_arr, stream, proj, norm_gains, router, rows, cols, *blocks)

    arrived = lax.all_to_all(
        slots.reshape(exp_count, capacity, width), "expert", split_axis=0, concat_axis=0, tiled=True
    ).reshape(slots_count, width)

    order = sorted(range(dp_count), key=lambda k: (k & half, k))
    inner = expert_in.shape[2]
    answer = pl.pallas_call(
        functools.partial(expert_kernel, dp_count, order),
        out_shape=jax.ShapeDtypeStruct((slots_count, width), BF16),
        in_specs=[VMEM] + [ANY] * (2 * dp_count),
        out_specs=VMEM,
        scratch_shapes=[
            pltpu.VMEM((dp_count, width, inner), BF16),
            pltpu.VMEM((dp_count, inner, width), BF16),
            pltpu.VMEM((slots_count, width), F32),
            pltpu.SemaphoreType.DMA((2, dp_count)),
        ],
        compiler_params=params(48),
        cost_estimate=cost(4 * slots_count * width * inner * dp_count, 18 << 20),
        name="experts",
    )(arrived, *[firsts[k] for k in range(dp_count)], *[seconds[k] for k in range(dp_count)])

    returned = lax.all_to_all(
        answer.reshape(exp_count, capacity, width), "expert", split_axis=0, concat_axis=0, tiled=True
    ).reshape(slots_count, width)

    return pl.pallas_call(
        functools.partial(combine_kernel, exp_count, capacity),
        out_shape=jax.ShapeDtypeStruct((1, frames, width), BF16),
        in_specs=[VMEM] * 4,
        out_specs=VMEM,
        compiler_params=params(32),
        cost_estimate=cost(4 * frames * slots_count * width, 3 << 20),
        name="combine",
    )(returned, mixed, gate, cols)


def solution(mesh):
    return jax.shard_map(
        body,
        mesh=mesh,
        in_specs=(
            P(("dp", "expert"), None, None),
            P(),
            P(("dp", "expert"), None, None),
            P(),
            P(None, "expert", None),
            P("expert", None),
            P(),
            P("expert", None, "dp"),
            P("expert", "dp", None),
        ),
        out_specs=P(("dp", "expert"), None, None),
        check_vma=False,
    )
```

```python
import functools

import jax
import jax.numpy as jnp
from jax import lax
from jax.experimental import pallas as pl
from jax.experimental.pallas import tpu as pltpu
from jax.sharding import PartitionSpec as P

HEAD_DIM = 64
epsilon = 1e-05
BF16 = jnp.bfloat16
F32 = jnp.float32
VMEM = pl.BlockSpec(memory_space=pltpu.VMEM)
SMEM = pl.BlockSpec(memory_space=pltpu.SMEM)
ANY = pl.BlockSpec(memory_space=pl.ANY)


def params(mib):
    return pltpu.CompilerParams(vmem_limit_bytes=mib << 20)


def cost(flops, moved, special=0):
    return pl.CostEstimate(flops=flops >> 8, bytes_accessed=moved >> 8, transcendentals=special >> 8)


def swap(block, axis, mask):
    count = lax.axis_size(axis)
    return lax.ppermute(block, axis, [(i, i ^ mask) for i in range(count)])


def layer_norm(values, gain):
    mean = jnp.mean(values, axis=-1, keepdims=True)
    centred = values - mean
    spread = jnp.mean(centred * centred, axis=-1, keepdims=True)
    return centred * lax.rsqrt(spread + epsilon) * gain


def norm_kernel(count, place_ref, gain_ref, *refs):
    raw, (normed_ref, own_ref) = refs[:count], refs[count:]
    gain = gain_ref[0:1, :]
    for k in range(count):
        where = place_ref[k]
        block = raw[k][0]
        normed_ref[where] = layer_norm(block.astype(F32), gain).astype(BF16)

        @pl.when(where == 0)
        def _():
            own_ref[...] = block


def attention_kernel(count, shards, me_ref, near_ref, far_ref, *refs):
    pieces, outs = refs[:shards], refs[shards : shards + count]
    weights, sems = refs[shards + count :]
    depth, cols = pieces[0].shape[1:]
    me = me_ref[0]
    copies = []
    for k in range(shards):
        rows = pl.ds(pl.multiple_of((me ^ k) * depth, depth), depth)
        copy = pltpu.make_async_copy(pieces[k], weights.at[:, rows, :], sems.at[k])
        copy.start()
        copies.append(copy)
    for copy in copies:
        copy.wait()
    frames = near_ref.shape[1]
    head = lax.broadcasted_iota(jnp.int32, (frames, cols), 1) // HEAD_DIM
    scale = HEAD_DIM**-0.5
    for k in range(count):
        x = (far_ref if k & 1 else near_ref)[k >> 1]
        q, key, val = [
            jnp.dot(x, weights[i], preferred_element_type=F32).astype(BF16) for i in range(3)
        ]
        q = q * jnp.asarray(scale, BF16)
        total = jnp.zeros((frames, cols), F32)
        for h in range(cols // HEAD_DIM):
            mine = head == h
            scores = lax.dot_general(
                jnp.where(mine, q, jnp.zeros_like(q)),
                key,
                (((1,), (1,)), ((), ())),
                preferred_element_type=F32,
            )
            exps = jnp.exp(scores - jnp.max(scores, axis=-1, keepdims=True))
            norm = 1.0 / jnp.sum(exps, axis=-1, keepdims=True)
            probs = (exps * norm).astype(BF16)
            total = jnp.where(mine, jnp.dot(probs, val, preferred_element_type=F32), total)
        outs[k][...] = total.astype(BF16)


def mix_kernel(
    count, experts, capacity, me_ref, own_ref, near_ref, far_ref, gain_ref, router_ref, rows_ref, cols_ref, *refs
):
    blocks, (slots_ref, mixed_ref, gate_ref), (wide,) = refs[:count], refs[count : count + 3], refs[count + 3 :]
    frames, depth = blocks[0].shape
    me = me_ref[0]
    part = near_ref.shape[1]
    for held, side in ((near_ref, me & 1), (far_ref, 1 - (me & 1))):
        total = jnp.zeros((frames, part), F32)
        for k in range(count):
            rows = pl.ds(pl.multiple_of((me ^ k) * depth, depth), depth)
            total += jnp.dot(blocks[k][...], held[rows, :], preferred_element_type=F32)
        wide[:, pl.ds(pl.multiple_of(side * part, part), part)] = total
    mixed = (own_ref[...].astype(F32) + wide[...]).astype(BF16)
    mixed_ref[...] = mixed
    normed = layer_norm(mixed.astype(F32), gain_ref[1:2, :]).astype(BF16)
    first, second = rows_ref[0:1, :], rows_ref[1:2, :]
    which = lax.broadcasted_iota(jnp.int32, (experts, frames), 0)
    named = ((which == first) | (which == second)).astype(F32)
    before = (
        lax.broadcasted_iota(jnp.int32, (frames, frames), 0)
        < lax.broadcasted_iota(jnp.int32, (frames, frames), 1)
    ).astype(F32)
    rank = jnp.dot(named, before, preferred_element_type=F32) + (which * capacity).astype(F32)
    slot = lax.broadcasted_iota(jnp.int32, (experts * capacity, frames), 0).astype(F32)
    place0 = jnp.sum(jnp.where(which == first, rank, 0.0), axis=0, keepdims=True)
    place1 = jnp.sum(jnp.where(which == second, rank, 0.0), axis=0, keepdims=True)
    spread = ((slot == place0) | (slot == place1)).astype(F32).astype(BF16)
    slots_ref[...] = jnp.dot(spread, normed, preferred_element_type=F32).astype(BF16)
    high = router_ref[...].astype(BF16)
    rest = router_ref[...] - high.astype(F32)
    middle = rest.astype(BF16)
    low = (rest - middle.astype(F32)).astype(BF16)
    logits = (
        jnp.dot(normed, low, preferred_element_type=F32)
        + jnp.dot(normed, middle, preferred_element_type=F32)
    ) + jnp.dot(normed, high, preferred_element_type=F32)
    lane = lax.broadcasted_iota(jnp.int32, (frames, experts), 1)
    ahead = jnp.sum(jnp.where(lane == cols_ref[:, 0:1], logits, 0.0), axis=1, keepdims=True)
    behind = jnp.sum(jnp.where(lane == cols_ref[:, 1:2], logits, 0.0), axis=1, keepdims=True)
    gate_ref[...] = jnp.broadcast_to(jax.nn.sigmoid(ahead - behind), gate_ref.shape)


def fetch(plan, refs, buf, sems):
    copies = []
    for at, pieces in enumerate(plan):
        started = []
        for p, (source, view, place) in enumerate(pieces):
            copy = pltpu.make_async_copy(
                refs[source].at[(0, *view)], buf.at[(at, *place)], sems.at[at, p]
            )
            copy.start()
            started.append(copy)
        copies.append(started)
    return copies


def hidden_kernel(plan, sources, slots_ref, *refs):
    hidden_ref, buf, sems = refs[sources:]
    inner = buf.shape[2]
    copies = fetch(plan, refs[:sources], buf, sems)
    step = min(512, inner)
    for at in range(len(plan)):
        for copy in copies[at]:
            copy.wait()
        for part in range(0, inner, step):
            half = 0.5 * jnp.dot(
                slots_ref[...], buf[at, :, part : part + step], preferred_element_type=F32
            )
            hidden_ref[at, :, part : part + step] = (half + half * jnp.tanh(half)).astype(BF16)


def answer_kernel(plan, sources, near_ref, far_ref, *refs):
    answer_ref, buf, total, sems = refs[sources:]
    copies = fetch(plan, refs[:sources], buf, sems)
    near = near_ref.shape[0]
    for at in range(len(plan)):
        for copy in copies[at]:
            copy.wait()
        hidden = near_ref[at] if at < near else far_ref[at - near]
        down = jnp.dot(hidden, buf[at], preferred_element_type=F32)
        if at == 0:
            total[...] = down
        elif at < len(plan) - 1:
            total[...] += down
        else:
            answer_ref[...] = (total[...] + down).astype(BF16)


def combine_kernel(experts, capacity, count, mixed_ref, gate_ref, cols_ref, *refs):
    answers, out_ref = refs[:count], refs[count]
    frames = mixed_ref.shape[0]
    first, second = cols_ref[:, 0:1], cols_ref[:, 1:2]
    lane = lax.broadcasted_iota(jnp.int32, (frames, experts), 1)
    named = ((lane == first) | (lane == second)).astype(F32)
    before = (
        lax.broadcasted_iota(jnp.int32, (frames, frames), 1)
        < lax.broadcasted_iota(jnp.int32, (frames, frames), 0)
    ).astype(F32)
    rank = jnp.dot(before, named, preferred_element_type=F32) + (lane * capacity).astype(F32)
    slot = lax.broadcasted_iota(jnp.int32, (frames, experts * capacity), 1).astype(F32)
    picks = []
    for chosen in (first, second):
        place = jnp.sum(jnp.where(lane == chosen, rank, 0.0), axis=1, keepdims=True)
        picks.append((slot == place).astype(F32).astype(BF16))
    gate = gate_ref[:, 0:1]
    cols = mixed_ref.shape[1] // count
    for c in range(count):
        where = slice(c * cols, (c + 1) * cols)
        back = [jnp.dot(pick, answers[c][...], preferred_element_type=F32) for pick in picks]
        result = mixed_ref[:, where].astype(F32) + gate * back[0] + (1.0 - gate) * back[1]
        out_ref[0, :, where] = result.astype(BF16)


def spread_over(block, axis, low):
    held = {0: block}
    bit = lax.axis_size(axis) // 2
    while bit >= low:
        for k in list(held):
            held[k | bit] = swap(held[k], axis, bit)
        bit //= 2
    return held


def swap_all(held):
    return {k: swap(block, "dp", 1) for k, block in held.items() if k}


def after(values, earlier):
    return lax.optimization_barrier((values, earlier))[0]


def body(
    frames_in, pit_order, expert_ids, norm_gains, attn_qkv, attn_out, router, expert_in, expert_out
):
    dp_count = lax.axis_size("dp")
    exp_count = lax.axis_size("expert")
    me = lax.axis_index("dp").astype(jnp.int32)
    exp_index = lax.axis_index("expert").astype(jnp.int32)
    frames, width = frames_in.shape[1:]
    top = expert_ids.shape[2]
    capacity = frames * top * 5 // (4 * exp_count)
    slots_count = exp_count * capacity
    half = dp_count // 2
    share = width // dp_count
    inner = expert_in.shape[2]

    raw = spread_over(frames_in, "dp", 2)

    qkv = {0: lax.dynamic_slice_in_dim(attn_qkv, me * share, share, axis=2)}
    for far in range(2, exp_count, 2):
        qkv[far] = swap(qkv[0], "expert", far)
    for far in range(0, exp_count, 2):
        qkv[far | 1] = swap(qkv[far], "expert", 1)

    rows = width // 2
    proj_near = lax.all_gather(
        lax.dynamic_slice_in_dim(attn_out, (me % 2) * rows, rows, axis=1),
        "expert",
        axis=0,
        tiled=True,
    )

    in_cuts = [(0, rows // 2), (rows // 2, width - rows // 2)]
    in_chunks = [lax.slice_in_dim(expert_in, a, a + n, axis=1) for a, n in in_cuts]
    out_chunks = [expert_out[:, :, :rows], expert_out[:, :, rows:]]
    in_held = [spread_over(in_chunks[0], "dp", 2)]
    early = [*[qkv[k] for k in range(2, exp_count, 2)], in_held[0]]
    raw[half] = after(raw[half], early)

    groups = len(raw)
    member = jnp.arange(groups, dtype=jnp.int32) * 2
    meeting = ((me ^ member) % half) * exp_count + exp_index
    place = jnp.where(pit_order[meeting, 0] == 0, member, member ^ half) // 2

    near, stream = pl.pallas_call(
        functools.partial(norm_kernel, groups),
        out_shape=(
            jax.ShapeDtypeStruct((groups, frames, width), BF16),
            jax.ShapeDtypeStruct((frames, width), BF16),
        ),
        in_specs=[SMEM, VMEM] + [VMEM] * groups,
        out_specs=(VMEM, VMEM),
        compiler_params=params(32),
        cost_estimate=cost(groups * frames * width * 8, groups * frames * width * 4),
        name="norm",
    )(place, norm_gains, *[raw[2 * k] for k in range(groups)])
    far = swap(near, "dp", 1)
    in_core = swap(after(expert_in, far), "dp", 1)

    contexts = pl.pallas_call(
        functools.partial(attention_kernel, dp_count, exp_count),
        out_shape=[jax.ShapeDtypeStruct((frames, share), BF16)] * dp_count,
        in_specs=[SMEM, VMEM, VMEM] + [ANY] * exp_count,
        out_specs=[VMEM] * dp_count,
        scratch_shapes=[
            pltpu.VMEM((3, width, share), BF16),
            pltpu.SemaphoreType.DMA((exp_count,)),
        ],
        compiler_params=params(32),
        cost_estimate=cost(
            2 * frames * width * width * 3 + 16 * frames * frames * width, 5 << 20, frames * frames * 16
        ),
        name="attention",
    )(exp_index[None], near, far, *[qkv[k] for k in range(exp_count)])

    crossed = [swap(contexts[k], "dp", k) for k in range(1, dp_count)]

    proj_far = swap(after(proj_near, contexts), "dp", 1)

    in_held.append(spread_over(after(in_chunks[1], crossed), "dp", 2))
    in_hop = [swap_all(after(in_held[0], crossed))]
    out_core = swap(after(expert_out, crossed), "dp", 1)
    out_held = [spread_over(after(out_chunks[0], proj_far), "dp", 2)]

    cols = expert_ids[0]
    slots, mixed, gate = pl.pallas_call(
        functools.partial(mix_kernel, dp_count, exp_count, capacity),
        out_shape=(
            jax.ShapeDtypeStruct((slots_count, width), BF16),
            jax.ShapeDtypeStruct((frames, width), BF16),
            jax.ShapeDtypeStruct((frames, 128), F32),
        ),
        in_specs=[SMEM] + [VMEM] * (7 + dp_count),
        out_specs=(VMEM, VMEM, VMEM),
        scratch_shapes=[pltpu.VMEM((frames, width), F32)],
        compiler_params=params(32),
        cost_estimate=cost(2 * frames * width * (width + slots_count), 5 << 20),
        name="mix",
    )(me[None], stream, proj_near, proj_far, norm_gains, router, cols.T, cols, contexts[0], *crossed)

    arrived = lax.all_to_all(
        slots.reshape(exp_count, capacity, width), "expert", split_axis=0, concat_axis=0, tiled=True
    ).reshape(slots_count, width)

    out_held.append(spread_over(after(out_chunks[1], (mixed, in_core, out_core)), "dp", 2))
    in_hop.append(swap_all(after(in_held[1], arrived)))

    whole = (slice(None), slice(None))
    distant = range(2, dp_count)
    places = [(pl.ds(a, n), slice(None)) for a, n in in_cuts]

    def hidden_units(slots_in, plan, sources, name):
        return pl.pallas_call(
            functools.partial(hidden_kernel, plan, len(sources)),
            out_shape=jax.ShapeDtypeStruct((len(plan), slots_count, inner), BF16),
            in_specs=[VMEM] + [ANY] * len(sources),
            out_specs=VMEM,
            scratch_shapes=[
                pltpu.VMEM((len(plan), width, inner), BF16),
                pltpu.SemaphoreType.DMA((len(plan), max(len(pieces) for pieces in plan))),
            ],
            compiler_params=params(32),
            cost_estimate=cost(2 * slots_count * width * inner * len(plan), 8 << 20),
            name=name,
        )(slots_in, *sources)

    hidden_near = hidden_units(
        arrived, [[(k, whole, whole)] for k in range(2)], [expert_in, in_core], "hidden_near"
    )
    hidden_far = hidden_units(
        after(arrived, hidden_near),
        [[(2 * at + p, whole, places[p]) for p in range(2)] for at in range(len(distant))],
        [(in_hop if k & 1 else in_held)[p][k & ~1] for k in distant for p in range(2)],
        "hidden_far",
    )
    out_hop = [swap_all(after(out_held[0], (hidden_near, in_hop)))]

    returned = []
    for c in range(2):
        if c:
            out_hop.append(swap_all(after(out_held[c], answer)))
        piece = (slice(None), pl.ds(c * rows, rows))
        sources = [expert_out, out_core] + [(out_hop if k & 1 else out_held)[c][k & ~1] for k in distant]
        answer = pl.pallas_call(
            functools.partial(
                answer_kernel,
                [[(k, piece if k < 2 else whole, whole)] for k in range(dp_count)],
                len(sources),
            ),
            out_shape=jax.ShapeDtypeStruct((slots_count, rows), BF16),
            in_specs=[VMEM, VMEM] + [ANY] * len(sources),
            out_specs=VMEM,
            scratch_shapes=[
                pltpu.VMEM((dp_count, inner, rows), BF16),
                pltpu.VMEM((slots_count, rows), F32),
                pltpu.SemaphoreType.DMA((dp_count, 1)),
            ],
            compiler_params=params(32),
            cost_estimate=cost(2 * slots_count * rows * inner * dp_count, 10 << 20),
            name="answer",
        )(hidden_near, hidden_far, *sources)
        returned.append(
            lax.all_to_all(
                answer.reshape(exp_count, capacity, rows), "expert", split_axis=0, concat_axis=0, tiled=True
            ).reshape(slots_count, rows)
        )

    return pl.pallas_call(
        functools.partial(combine_kernel, exp_count, capacity, len(returned)),
        out_shape=jax.ShapeDtypeStruct((1, frames, width), BF16),
        in_specs=[VMEM] * (3 + len(returned)),
        out_specs=VMEM,
        compiler_params=params(32),
        cost_estimate=cost(4 * frames * slots_count * width, 3 << 20),
        name="combine",
    )(mixed, gate, cols, *returned)


def solution(mesh):
    return jax.shard_map(
        body,
        mesh=mesh,
        in_specs=(
            P(("dp", "expert"), None, None),
            P(),
            P(("dp", "expert"), None, None),
            P(),
            P(None, "expert", None),
            P("expert", None),
            P(),
            P("expert", None, "dp"),
            P("expert", "dp", None),
        ),
        out_specs=P(("dp", "expert"), None, None),
        check_vma=False,
    )
```

```python
import functools

import jax
import jax.numpy as jnp
from jax import lax
from jax.experimental import pallas as pl
from jax.experimental.pallas import tpu as pltpu
from jax.sharding import PartitionSpec as P

HEAD_DIM = 64
epsilon = 1e-05
BF16 = jnp.bfloat16
F32 = jnp.float32
VMEM = pl.BlockSpec(memory_space=pltpu.VMEM)
SMEM = pl.BlockSpec(memory_space=pltpu.SMEM)
ANY = pl.BlockSpec(memory_space=pl.ANY)


def params(mib):
    return pltpu.CompilerParams(vmem_limit_bytes=mib << 20)


def cost(flops, moved, special=0):
    return pl.CostEstimate(flops=flops >> 8, bytes_accessed=moved >> 8, transcendentals=special >> 8)


def swap(block, axis, mask):
    count = lax.axis_size(axis)
    return lax.ppermute(block, axis, [(i, i ^ mask) for i in range(count)])


def layer_norm(values, gain):
    mean = jnp.mean(values, axis=-1, keepdims=True)
    centred = values - mean
    spread = jnp.mean(centred * centred, axis=-1, keepdims=True)
    return centred * lax.rsqrt(spread + epsilon) * gain


def norm_kernel(count, place_ref, gain_ref, *refs):
    raw, (normed_ref, own_ref) = refs[:count], refs[count:]
    gain = gain_ref[0:1, :]
    for k in range(count):
        where = place_ref[k]
        block = raw[k][0]
        normed_ref[where] = layer_norm(block.astype(F32), gain).astype(BF16)

        @pl.when(where == 0)
        def _():
            own_ref[...] = block


def attention_kernel(count, shards, me_ref, near_ref, far_ref, *refs):
    pieces, outs = refs[:shards], refs[shards : shards + count]
    weights, sems = refs[shards + count :]
    depth, cols = pieces[0].shape[1:]
    me = me_ref[0]
    copies = []
    for k in range(shards):
        rows = pl.ds(pl.multiple_of((me ^ k) * depth, depth), depth)
        copy = pltpu.make_async_copy(pieces[k], weights.at[:, rows, :], sems.at[k])
        copy.start()
        copies.append(copy)
    for copy in copies:
        copy.wait()
    frames = near_ref.shape[1]
    head = lax.broadcasted_iota(jnp.int32, (frames, cols), 1) // HEAD_DIM
    scale = HEAD_DIM**-0.5
    for k in range(count):
        x = (far_ref if k & 1 else near_ref)[k >> 1]
        q, key, val = [
            jnp.dot(x, weights[i], preferred_element_type=F32).astype(BF16) for i in range(3)
        ]
        q = q * jnp.asarray(scale, BF16)
        total = jnp.zeros((frames, cols), F32)
        for h in range(cols // HEAD_DIM):
            mine = head == h
            scores = lax.dot_general(
                jnp.where(mine, q, jnp.zeros_like(q)),
                key,
                (((1,), (1,)), ((), ())),
                preferred_element_type=F32,
            )
            exps = jnp.exp(scores - jnp.max(scores, axis=-1, keepdims=True))
            norm = 1.0 / jnp.sum(exps, axis=-1, keepdims=True)
            probs = (exps * norm).astype(BF16)
            total = jnp.where(mine, jnp.dot(probs, val, preferred_element_type=F32), total)
        outs[k][...] = total.astype(BF16)


def mix_kernel(
    count, experts, capacity, me_ref, own_ref, near_ref, far_ref, gain_ref, router_ref, rows_ref, cols_ref, *refs
):
    blocks, (slots_ref, mixed_ref, gate_ref), (wide,) = refs[:count], refs[count : count + 3], refs[count + 3 :]
    frames, depth = blocks[0].shape
    me = me_ref[0]
    part = near_ref.shape[1]
    for held, side in ((near_ref, me & 1), (far_ref, 1 - (me & 1))):
        total = jnp.zeros((frames, part), F32)
        for k in range(count):
            rows = pl.ds(pl.multiple_of((me ^ k) * depth, depth), depth)
            total += jnp.dot(blocks[k][...], held[rows, :], preferred_element_type=F32)
        wide[:, pl.ds(pl.multiple_of(side * part, part), part)] = total
    mixed = (own_ref[...].astype(F32) + wide[...]).astype(BF16)
    mixed_ref[...] = mixed
    normed = layer_norm(mixed.astype(F32), gain_ref[1:2, :]).astype(BF16)
    first, second = rows_ref[0:1, :], rows_ref[1:2, :]
    which = lax.broadcasted_iota(jnp.int32, (experts, frames), 0)
    named = ((which == first) | (which == second)).astype(F32)
    before = (
        lax.broadcasted_iota(jnp.int32, (frames, frames), 0)
        < lax.broadcasted_iota(jnp.int32, (frames, frames), 1)
    ).astype(F32)
    rank = jnp.dot(named, before, preferred_element_type=F32) + (which * capacity).astype(F32)
    slot = lax.broadcasted_iota(jnp.int32, (experts * capacity, frames), 0).astype(F32)
    place0 = jnp.sum(jnp.where(which == first, rank, 0.0), axis=0, keepdims=True)
    place1 = jnp.sum(jnp.where(which == second, rank, 0.0), axis=0, keepdims=True)
    spread = ((slot == place0) | (slot == place1)).astype(F32).astype(BF16)
    slots_ref[...] = jnp.dot(spread, normed, preferred_element_type=F32).astype(BF16)
    high = router_ref[...].astype(BF16)
    rest = router_ref[...] - high.astype(F32)
    middle = rest.astype(BF16)
    low = (rest - middle.astype(F32)).astype(BF16)
    logits = (
        jnp.dot(normed, low, preferred_element_type=F32)
        + jnp.dot(normed, middle, preferred_element_type=F32)
    ) + jnp.dot(normed, high, preferred_element_type=F32)
    lane = lax.broadcasted_iota(jnp.int32, (frames, experts), 1)
    ahead = jnp.sum(jnp.where(lane == cols_ref[:, 0:1], logits, 0.0), axis=1, keepdims=True)
    behind = jnp.sum(jnp.where(lane == cols_ref[:, 1:2], logits, 0.0), axis=1, keepdims=True)
    gate_ref[...] = jnp.broadcast_to(jax.nn.sigmoid(ahead - behind), gate_ref.shape)


def hidden_kernel(slots_ref, weight_ref, hidden_ref, buf, sems):
    count, _, inner = buf.shape
    copies = [
        pltpu.make_async_copy(weight_ref.at[at], buf.at[at], sems.at[at]) for at in range(count)
    ]
    for copy in copies:
        copy.start()
    step = min(512, inner)
    for at in range(count):
        copies[at].wait()
        for part in range(0, inner, step):
            half = 0.5 * jnp.dot(
                slots_ref[...], buf[at, :, part : part + step], preferred_element_type=F32
            )
            hidden_ref[at, :, part : part + step] = (half + half * jnp.tanh(half)).astype(BF16)


def answer_kernel(near_ref, far_ref, near_weight, far_weight, answer_ref, buf, total, sems):
    count = near_ref.shape[0]
    steps = [(near_ref, near_weight, at) for at in range(count)]
    steps += [(far_ref, far_weight, at) for at in range(count)]
    copies = [
        pltpu.make_async_copy(weight.at[at], buf.at[k], sems.at[k])
        for k, (_, weight, at) in enumerate(steps)
    ]
    for copy in copies:
        copy.start()
    for k, (hidden, _, at) in enumerate(steps):
        copies[k].wait()
        down = jnp.dot(hidden[at], buf[k], preferred_element_type=F32)
        if k == 0:
            total[...] = down
        elif k < len(steps) - 1:
            total[...] += down
        else:
            answer_ref[...] = (total[...] + down).astype(BF16)


def combine_kernel(experts, capacity, count, mixed_ref, gate_ref, cols_ref, *refs):
    answers, out_ref = refs[:count], refs[count]
    frames = mixed_ref.shape[0]
    first, second = cols_ref[:, 0:1], cols_ref[:, 1:2]
    lane = lax.broadcasted_iota(jnp.int32, (frames, experts), 1)
    named = ((lane == first) | (lane == second)).astype(F32)
    before = (
        lax.broadcasted_iota(jnp.int32, (frames, frames), 1)
        < lax.broadcasted_iota(jnp.int32, (frames, frames), 0)
    ).astype(F32)
    rank = jnp.dot(before, named, preferred_element_type=F32) + (lane * capacity).astype(F32)
    slot = lax.broadcasted_iota(jnp.int32, (frames, experts * capacity), 1).astype(F32)
    picks = []
    for chosen in (first, second):
        place = jnp.sum(jnp.where(lane == chosen, rank, 0.0), axis=1, keepdims=True)
        picks.append((slot == place).astype(F32).astype(BF16))
    gate = gate_ref[:, 0:1]
    cols = mixed_ref.shape[1] // count
    for c in range(count):
        where = slice(c * cols, (c + 1) * cols)
        back = [jnp.dot(pick, answers[c][...], preferred_element_type=F32) for pick in picks]
        result = mixed_ref[:, where].astype(F32) + gate * back[0] + (1.0 - gate) * back[1]
        out_ref[0, :, where] = result.astype(BF16)


def spread_over(block, axis, low):
    held = {0: block}
    bit = lax.axis_size(axis) // 2
    while bit >= low:
        for k in list(held):
            held[k | bit] = swap(held[k], axis, bit)
        bit //= 2
    return held


def over_chips(block):
    count = lax.axis_size("dp")
    groups = [list(range(core, count, 2)) for core in range(2)]
    return lax.all_gather(block, "dp", axis=0, tiled=True, axis_index_groups=groups)


def after(values, earlier):
    return lax.optimization_barrier((values, earlier))[0]


def body(
    frames_in, pit_order, expert_ids, norm_gains, attn_qkv, attn_out, router, expert_in, expert_out
):
    dp_count = lax.axis_size("dp")
    exp_count = lax.axis_size("expert")
    me = lax.axis_index("dp").astype(jnp.int32)
    exp_index = lax.axis_index("expert").astype(jnp.int32)
    frames, width = frames_in.shape[1:]
    top = expert_ids.shape[2]
    capacity = frames * top * 5 // (4 * exp_count)
    slots_count = exp_count * capacity
    half = dp_count // 2
    share = width // dp_count
    inner = expert_in.shape[2]

    raw = spread_over(frames_in, "dp", 2)

    qkv = {0: lax.dynamic_slice_in_dim(attn_qkv, me * share, share, axis=2)}
    for far in range(2, exp_count, 2):
        qkv[far] = swap(qkv[0], "expert", far)
    for far in range(0, exp_count, 2):
        qkv[far | 1] = swap(qkv[far], "expert", 1)

    rows = width // 2
    proj_near = lax.all_gather(
        lax.dynamic_slice_in_dim(attn_out, (me % 2) * rows, rows, axis=1),
        "expert",
        axis=0,
        tiled=True,
    )

    early = [qkv[k] for k in range(2, exp_count, 2)]
    raw_half = raw[half]
    raw[half] = after(raw_half, early)

    groups = len(raw)
    member = jnp.arange(groups, dtype=jnp.int32) * 2
    meeting = ((me ^ member) % half) * exp_count + exp_index
    place = jnp.where(pit_order[meeting, 0] == 0, member, member ^ half) // 2

    near, stream = pl.pallas_call(
        functools.partial(norm_kernel, groups),
        out_shape=(
            jax.ShapeDtypeStruct((groups, frames, width), BF16),
            jax.ShapeDtypeStruct((frames, width), BF16),
        ),
        in_specs=[SMEM, VMEM] + [VMEM] * groups,
        out_specs=(VMEM, VMEM),
        compiler_params=params(32),
        cost_estimate=cost(groups * frames * width * 8, groups * frames * width * 4),
        name="norm",
    )(place, norm_gains, *[raw[2 * k] for k in range(groups)])
    far = swap(near, "dp", 1)

    in_near = over_chips(after(expert_in, raw_half))
    out_near = []
    for c, earlier in enumerate((near, far)):
        piece = lax.slice_in_dim(expert_out, c * rows, (c + 1) * rows, axis=2)
        out_near.append(over_chips(after(piece, earlier)))

    contexts = pl.pallas_call(
        functools.partial(attention_kernel, dp_count, exp_count),
        out_shape=[jax.ShapeDtypeStruct((frames, share), BF16)] * dp_count,
        in_specs=[SMEM, VMEM, VMEM] + [ANY] * exp_count,
        out_specs=[VMEM] * dp_count,
        scratch_shapes=[
            pltpu.VMEM((3, width, share), BF16),
            pltpu.SemaphoreType.DMA((exp_count,)),
        ],
        compiler_params=params(32),
        cost_estimate=cost(
            2 * frames * width * width * 3 + 16 * frames * frames * width, 5 << 20, frames * frames * 16
        ),
        name="attention",
    )(exp_index[None], near, far, *[qkv[k] for k in range(exp_count)])

    crossed = [swap(contexts[k], "dp", k) for k in range(1, dp_count)]

    proj_far = swap(after(proj_near, contexts), "dp", 1)

    cols = expert_ids[0]
    slots, mixed, gate = pl.pallas_call(
        functools.partial(mix_kernel, dp_count, exp_count, capacity),
        out_shape=(
            jax.ShapeDtypeStruct((slots_count, width), BF16),
            jax.ShapeDtypeStruct((frames, width), BF16),
            jax.ShapeDtypeStruct((frames, 128), F32),
        ),
        in_specs=[SMEM] + [VMEM] * (7 + dp_count),
        out_specs=(VMEM, VMEM, VMEM),
        scratch_shapes=[pltpu.VMEM((frames, width), F32)],
        compiler_params=params(32),
        cost_estimate=cost(2 * frames * width * (width + slots_count), 5 << 20),
        name="mix",
    )(me[None], stream, proj_near, proj_far, norm_gains, router, cols.T, cols, contexts[0], *crossed)

    arrived = lax.all_to_all(
        slots.reshape(exp_count, capacity, width), "expert", split_axis=0, concat_axis=0, tiled=True
    ).reshape(slots_count, width)


    in_far = swap(after(in_near, arrived), "dp", 1)

    def hidden_units(slots_in, weight, name):
        return pl.pallas_call(
            hidden_kernel,
            out_shape=jax.ShapeDtypeStruct((groups, slots_count, inner), BF16),
            in_specs=[VMEM, ANY],
            out_specs=VMEM,
            scratch_shapes=[
                pltpu.VMEM((groups, width, inner), BF16),
                pltpu.SemaphoreType.DMA((groups,)),
            ],
            compiler_params=params(32),
            cost_estimate=cost(2 * slots_count * width * inner * groups, 8 << 20),
            name=name,
        )(slots_in, weight)

    hidden_near = hidden_units(arrived, in_near, "hidden_near")
    hidden_far = hidden_units(after(arrived, hidden_near), in_far, "hidden_far")

    returned = []
    for c in range(2):
        out_far = swap(after(out_near[c], answer if c else hidden_near), "dp", 1)
        answer = pl.pallas_call(
            answer_kernel,
            out_shape=jax.ShapeDtypeStruct((slots_count, rows), BF16),
            in_specs=[VMEM, VMEM, ANY, ANY],
            out_specs=VMEM,
            scratch_shapes=[
                pltpu.VMEM((dp_count, inner, rows), BF16),
                pltpu.VMEM((slots_count, rows), F32),
                pltpu.SemaphoreType.DMA((dp_count,)),
            ],
            compiler_params=params(32),
            cost_estimate=cost(2 * slots_count * rows * inner * dp_count, 10 << 20),
            name="answer",
        )(hidden_near, hidden_far, out_near[c], out_far)
        returned.append(
            lax.all_to_all(
                answer.reshape(exp_count, capacity, rows), "expert", split_axis=0, concat_axis=0, tiled=True
            ).reshape(slots_count, rows)
        )

    return pl.pallas_call(
        functools.partial(combine_kernel, exp_count, capacity, len(returned)),
        out_shape=jax.ShapeDtypeStruct((1, frames, width), BF16),
        in_specs=[VMEM] * (3 + len(returned)),
        out_specs=VMEM,
        compiler_params=params(32),
        cost_estimate=cost(4 * frames * slots_count * width, 3 << 20),
        name="combine",
    )(mixed, gate, cols, *returned)


def solution(mesh):
    return jax.shard_map(
        body,
        mesh=mesh,
        in_specs=(
            P(("dp", "expert"), None, None),
            P(),
            P(("dp", "expert"), None, None),
            P(),
            P(None, "expert", None),
            P("expert", None),
            P(),
            P("expert", None, "dp"),
            P("expert", "dp", None),
        ),
        out_specs=P(("dp", "expert"), None, None),
        check_vma=False,
    )
```

```python
import functools

import jax
import jax.numpy as jnp
from jax import lax
from jax.experimental import pallas as pl
from jax.experimental.pallas import tpu as pltpu
from jax.sharding import PartitionSpec as P

HEAD_DIM = 64
epsilon = 1e-05
BF16 = jnp.bfloat16
F32 = jnp.float32
VMEM = pl.BlockSpec(memory_space=pltpu.VMEM)
SMEM = pl.BlockSpec(memory_space=pltpu.SMEM)
ANY = pl.BlockSpec(memory_space=pl.ANY)
HBM = pl.BlockSpec(memory_space=pltpu.HBM)


def params(mib):
    return pltpu.CompilerParams(vmem_limit_bytes=mib << 20)


def cost(flops, moved, special=0):
    return pl.CostEstimate(flops=flops >> 8, bytes_accessed=moved >> 8, transcendentals=special >> 8)


def swap(block, axis, mask):
    count = lax.axis_size(axis)
    return lax.ppermute(block, axis, [(i, i ^ mask) for i in range(count)])


def layer_norm(values, gain):
    mean = jnp.mean(values, axis=-1, keepdims=True)
    centred = values - mean
    spread = jnp.mean(centred * centred, axis=-1, keepdims=True)
    return centred * lax.rsqrt(spread + epsilon) * gain


def norm_kernel(count, place_ref, gain_ref, *refs):
    raw, (normed_ref, own_ref) = refs[:count], refs[count:]
    gain = gain_ref[0:1, :]
    for k in range(count):
        where = place_ref[k]
        block = raw[k][0]
        normed_ref[where] = layer_norm(block.astype(F32), gain).astype(BF16)

        @pl.when(where == 0)
        def _():
            own_ref[...] = block


def attention_kernel(count, shards, me_ref, near_ref, far_ref, *refs):
    pieces, outs = refs[:shards], refs[shards : shards + count]
    weights, sems = refs[shards + count :]
    depth, cols = pieces[0].shape[1:]
    me = me_ref[0]
    copies = []
    for k in range(shards):
        rows = pl.ds(pl.multiple_of((me ^ k) * depth, depth), depth)
        copy = pltpu.make_async_copy(pieces[k], weights.at[:, rows, :], sems.at[k])
        copy.start()
        copies.append(copy)
    for copy in copies:
        copy.wait()
    frames = near_ref.shape[1]
    head = lax.broadcasted_iota(jnp.int32, (frames, cols), 1) // HEAD_DIM
    scale = HEAD_DIM**-0.5
    for k in range(count):
        x = (far_ref if k & 1 else near_ref)[k >> 1]
        q, key, val = [
            jnp.dot(x, weights[i], preferred_element_type=F32).astype(BF16) for i in range(3)
        ]
        q = q * jnp.asarray(scale, BF16)
        total = jnp.zeros((frames, cols), F32)
        for h in range(cols // HEAD_DIM):
            mine = head == h
            scores = lax.dot_general(
                jnp.where(mine, q, jnp.zeros_like(q)),
                key,
                (((1,), (1,)), ((), ())),
                preferred_element_type=F32,
            )
            exps = jnp.exp(scores - jnp.max(scores, axis=-1, keepdims=True))
            norm = 1.0 / jnp.sum(exps, axis=-1, keepdims=True)
            probs = (exps * norm).astype(BF16)
            total = jnp.where(mine, jnp.dot(probs, val, preferred_element_type=F32), total)
        outs[k][...] = total.astype(BF16)


def mix_kernel(
    count, experts, capacity, me_ref, own_ref, near_ref, far_ref, gain_ref, router_ref, rows_ref, cols_ref, *refs
):
    blocks, (slots_ref, mixed_ref, gate_ref), (wide,) = refs[:count], refs[count : count + 3], refs[count + 3 :]
    frames, depth = blocks[0].shape
    me = me_ref[0]
    part = near_ref.shape[1]
    for held, side in ((near_ref, me & 1), (far_ref, 1 - (me & 1))):
        total = jnp.zeros((frames, part), F32)
        for k in range(count):
            rows = pl.ds(pl.multiple_of((me ^ k) * depth, depth), depth)
            total += jnp.dot(blocks[k][...], held[rows, :], preferred_element_type=F32)
        wide[:, pl.ds(pl.multiple_of(side * part, part), part)] = total
    mixed = (own_ref[...].astype(F32) + wide[...]).astype(BF16)
    mixed_ref[...] = mixed
    normed = layer_norm(mixed.astype(F32), gain_ref[1:2, :]).astype(BF16)
    first, second = rows_ref[0:1, :], rows_ref[1:2, :]
    which = lax.broadcasted_iota(jnp.int32, (experts, frames), 0)
    named = ((which == first) | (which == second)).astype(F32)
    before = (
        lax.broadcasted_iota(jnp.int32, (frames, frames), 0)
        < lax.broadcasted_iota(jnp.int32, (frames, frames), 1)
    ).astype(F32)
    rank = jnp.dot(named, before, preferred_element_type=F32) + (which * capacity).astype(F32)
    slot = lax.broadcasted_iota(jnp.int32, (experts * capacity, frames), 0).astype(F32)
    place0 = jnp.sum(jnp.where(which == first, rank, 0.0), axis=0, keepdims=True)
    place1 = jnp.sum(jnp.where(which == second, rank, 0.0), axis=0, keepdims=True)
    spread = ((slot == place0) | (slot == place1)).astype(F32).astype(BF16)
    slots_ref[...] = jnp.dot(spread, normed, preferred_element_type=F32).astype(BF16)
    high = router_ref[...].astype(BF16)
    rest = router_ref[...] - high.astype(F32)
    middle = rest.astype(BF16)
    low = (rest - middle.astype(F32)).astype(BF16)
    logits = (
        jnp.dot(normed, low, preferred_element_type=F32)
        + jnp.dot(normed, middle, preferred_element_type=F32)
    ) + jnp.dot(normed, high, preferred_element_type=F32)
    lane = lax.broadcasted_iota(jnp.int32, (frames, experts), 1)
    ahead = jnp.sum(jnp.where(lane == cols_ref[:, 0:1], logits, 0.0), axis=1, keepdims=True)
    behind = jnp.sum(jnp.where(lane == cols_ref[:, 1:2], logits, 0.0), axis=1, keepdims=True)
    gate_ref[...] = jnp.broadcast_to(jax.nn.sigmoid(ahead - behind), gate_ref.shape)


def hidden_kernel(cuts, slots_ref, *refs):
    hidden_ref, buf, sems = refs[len(cuts) :]
    count, _, inner = buf.shape
    copies = [[] for _ in range(count)]
    for k, (at, start, size) in enumerate(cuts):
        copy = pltpu.make_async_copy(
            refs[k].at[0], buf.at[at, pl.ds(start, size), :], sems.at[k]
        )
        copy.start()
        copies[at].append(copy)
    step = min(512, inner)
    for at in range(count):
        for copy in copies[at]:
            copy.wait()
        for part in range(0, inner, step):
            half = 0.5 * jnp.dot(
                slots_ref[...], buf[at, :, part : part + step], preferred_element_type=F32
            )
            hidden_ref[at, :, part : part + step] = (half + half * jnp.tanh(half)).astype(BF16)


def answer_kernel(count, start, near_ref, far_ref, *refs):
    weights, (answer_ref, buf, total, sems) = refs[:count], refs[count:]
    near = near_ref.shape[0]
    cols = buf.shape[2]
    copies = [
        pltpu.make_async_copy(weights[at].at[0, :, pl.ds(start, cols)], buf.at[at], sems.at[at])
        for at in range(count)
    ]
    for copy in copies:
        copy.start()
    for at in range(count):
        copies[at].wait()
        hidden = near_ref[at] if at < near else far_ref[at - near]
        down = jnp.dot(hidden, buf[at], preferred_element_type=F32)
        if at == 0:
            total[...] = down
        elif at < count - 1:
            total[...] += down
        else:
            answer_ref[...] = (total[...] + down).astype(BF16)


def combine_kernel(experts, capacity, count, mixed_ref, gate_ref, cols_ref, *refs):
    answers, out_ref = refs[:count], refs[count]
    frames = mixed_ref.shape[0]
    first, second = cols_ref[:, 0:1], cols_ref[:, 1:2]
    lane = lax.broadcasted_iota(jnp.int32, (frames, experts), 1)
    named = ((lane == first) | (lane == second)).astype(F32)
    before = (
        lax.broadcasted_iota(jnp.int32, (frames, frames), 1)
        < lax.broadcasted_iota(jnp.int32, (frames, frames), 0)
    ).astype(F32)
    rank = jnp.dot(before, named, preferred_element_type=F32) + (lane * capacity).astype(F32)
    slot = lax.broadcasted_iota(jnp.int32, (frames, experts * capacity), 1).astype(F32)
    picks = []
    for chosen in (first, second):
        place = jnp.sum(jnp.where(lane == chosen, rank, 0.0), axis=1, keepdims=True)
        picks.append((slot == place).astype(F32).astype(BF16))
    gate = gate_ref[:, 0:1]
    cols = mixed_ref.shape[1] // count
    for c in range(count):
        where = slice(c * cols, (c + 1) * cols)
        back = [jnp.dot(pick, answers[c][...], preferred_element_type=F32) for pick in picks]
        result = mixed_ref[:, where].astype(F32) + gate * back[0] + (1.0 - gate) * back[1]
        out_ref[0, :, where] = result.astype(BF16)


def spread_over(block, axis, low):
    held = {0: block}
    bit = lax.axis_size(axis) // 2
    while bit >= low:
        for k in list(held):
            held[k | bit] = swap(held[k], axis, bit)
        bit //= 2
    return held


def other_core(held):
    return {k: swap(block, "dp", 1) for k, block in held.items()}


def after(values, earlier):
    return lax.optimization_barrier((values, earlier))[0]


def body(
    frames_in, pit_order, expert_ids, norm_gains, attn_qkv, attn_out, router, expert_in, expert_out
):
    dp_count = lax.axis_size("dp")
    exp_count = lax.axis_size("expert")
    me = lax.axis_index("dp").astype(jnp.int32)
    exp_index = lax.axis_index("expert").astype(jnp.int32)
    frames, width = frames_in.shape[1:]
    top = expert_ids.shape[2]
    capacity = frames * top * 5 // (4 * exp_count)
    slots_count = exp_count * capacity
    half = dp_count // 2
    share = width // dp_count
    inner = expert_in.shape[2]

    raw = spread_over(frames_in, "dp", 2)

    qkv = {0: lax.dynamic_slice_in_dim(attn_qkv, me * share, share, axis=2)}
    for far in range(2, exp_count, 2):
        qkv[far] = swap(qkv[0], "expert", far)
    for far in range(0, exp_count, 2):
        qkv[far | 1] = swap(qkv[far], "expert", 1)

    rows = width // 2
    proj_near = lax.all_gather(
        lax.dynamic_slice_in_dim(attn_out, (me % 2) * rows, rows, axis=1),
        "expert",
        axis=0,
        tiled=True,
    )

    in_cuts = [(0, rows // 2), (rows // 2, width - rows // 2)]
    in_chunks = [lax.slice_in_dim(expert_in, a, a + n, axis=1) for a, n in in_cuts]
    in_held = [spread_over(in_chunks[0], "dp", 2)]

    early = [qkv[1], *[qkv[k] for k in range(2, exp_count, 2)], qkv[3], in_held[0]]
    raw[half] = after(raw[half], early)

    groups = len(raw)
    member = jnp.arange(groups, dtype=jnp.int32) * 2
    meeting = ((me ^ member) % half) * exp_count + exp_index
    place = jnp.where(pit_order[meeting, 0] == 0, member, member ^ half) // 2

    near, stream = pl.pallas_call(
        functools.partial(norm_kernel, groups),
        out_shape=(
            jax.ShapeDtypeStruct((groups, frames, width), BF16),
            jax.ShapeDtypeStruct((frames, width), BF16),
        ),
        in_specs=[SMEM, VMEM] + [VMEM] * groups,
        out_specs=(VMEM, VMEM),
        compiler_params=params(32),
        cost_estimate=cost(groups * frames * width * 8, groups * frames * width * 4),
        name="norm",
    )(place, norm_gains, *[raw[2 * k] for k in range(groups)])
    far = swap(near, "dp", 1)
    in_held.append(spread_over(after(in_chunks[1], near), "dp", 2))

    contexts = pl.pallas_call(
        functools.partial(attention_kernel, dp_count, exp_count),
        out_shape=[jax.ShapeDtypeStruct((frames, share), BF16)] * dp_count,
        in_specs=[SMEM, VMEM, VMEM] + [ANY] * exp_count,
        out_specs=[VMEM] * dp_count,
        scratch_shapes=[
            pltpu.VMEM((3, width, share), BF16),
            pltpu.SemaphoreType.DMA((exp_count,)),
        ],
        compiler_params=params(32),
        cost_estimate=cost(
            2 * frames * width * width * 3 + 16 * frames * frames * width, 5 << 20, frames * frames * 16
        ),
        name="attention",
    )(exp_index[None], near, far, *[qkv[k] for k in range(exp_count)])

    crossed = [swap(contexts[k], "dp", k) for k in range(1, dp_count)]

    proj_far = swap(after(proj_near, contexts), "dp", 1)

    in_far = [swap(after(expert_in, crossed), "dp", 1)]
    in_near = [expert_in]
    places = [(0, 0, width)]
    for k in range(2, dp_count, 2):
        for held, cut in zip(in_held, in_cuts):
            in_near.append(held[k])
            in_far.append(swap(after(held[k], crossed), "dp", 1))
            places.append((k // 2, *cut))
    out_near = spread_over(after(expert_out, crossed), "dp", 2)
    out_far = {0: swap(after(expert_out, in_far), "dp", 1)}

    cols = expert_ids[0]
    slots, mixed, gate = pl.pallas_call(
        functools.partial(mix_kernel, dp_count, exp_count, capacity),
        out_shape=(
            jax.ShapeDtypeStruct((slots_count, width), BF16),
            jax.ShapeDtypeStruct((frames, width), BF16),
            jax.ShapeDtypeStruct((frames, 128), F32),
        ),
        in_specs=[SMEM] + [VMEM] * (7 + dp_count),
        out_specs=(VMEM, VMEM, VMEM),
        scratch_shapes=[pltpu.VMEM((frames, width), F32)],
        compiler_params=params(32),
        cost_estimate=cost(2 * frames * width * (width + slots_count), 5 << 20),
        name="mix",
    )(me[None], stream, proj_near, proj_far, norm_gains, router, cols.T, cols, contexts[0], *crossed)

    arrived = lax.all_to_all(
        slots.reshape(exp_count, capacity, width), "expert", split_axis=0, concat_axis=0, tiled=True
    ).reshape(slots_count, width)


    def hidden_units(slots_in, held, name):
        return pl.pallas_call(
            functools.partial(hidden_kernel, places),
            out_shape=jax.ShapeDtypeStruct((groups, slots_count, inner), BF16),
            in_specs=[VMEM] + [HBM] * len(places),
            out_specs=VMEM,
            scratch_shapes=[
                pltpu.VMEM((groups, width, inner), BF16),
                pltpu.SemaphoreType.DMA((len(places),)),
            ],
            compiler_params=params(32),
            cost_estimate=cost(2 * slots_count * width * inner * groups, 8 << 20),
            name=name,
        )(slots_in, *held)

    hidden_near = hidden_units(arrived, in_near, "hidden_near")
    hidden_far = hidden_units(after(arrived, hidden_near), in_far, "hidden_far")
    distant = {k: block for k, block in out_near.items() if k}
    out_far.update(other_core(after(distant, hidden_near)))
    weights = [held[k] for held in (out_near, out_far) for k in sorted(held)]

    returned = []
    for c in range(2):
        answer = pl.pallas_call(
            functools.partial(answer_kernel, dp_count, c * rows),
            out_shape=jax.ShapeDtypeStruct((slots_count, rows), BF16),
            in_specs=[VMEM, VMEM] + [HBM] * dp_count,
            out_specs=VMEM,
            scratch_shapes=[
                pltpu.VMEM((dp_count, inner, rows), BF16),
                pltpu.VMEM((slots_count, rows), F32),
                pltpu.SemaphoreType.DMA((dp_count,)),
            ],
            compiler_params=params(32),
            cost_estimate=cost(2 * slots_count * rows * inner * dp_count, 10 << 20),
            name="answer",
        )(after(hidden_near, answer) if c else hidden_near, hidden_far, *weights)
        returned.append(
            lax.all_to_all(
                answer.reshape(exp_count, capacity, rows), "expert", split_axis=0, concat_axis=0, tiled=True
            ).reshape(slots_count, rows)
        )

    return pl.pallas_call(
        functools.partial(combine_kernel, exp_count, capacity, len(returned)),
        out_shape=jax.ShapeDtypeStruct((1, frames, width), BF16),
        in_specs=[VMEM] * (3 + len(returned)),
        out_specs=VMEM,
        compiler_params=params(32),
        cost_estimate=cost(4 * frames * slots_count * width, 3 << 20),
        name="combine",
    )(mixed, gate, cols, *returned)


def solution(mesh):
    return jax.shard_map(
        body,
        mesh=mesh,
        in_specs=(
            P(("dp", "expert"), None, None),
            P(),
            P(("dp", "expert"), None, None),
            P(),
            P(None, "expert", None),
            P("expert", None),
            P(),
            P("expert", None, "dp"),
            P("expert", "dp", None),
        ),
        out_specs=P(("dp", "expert"), None, None),
        check_vma=False,
    )
```

```python
import functools

import jax
import jax.numpy as jnp
from jax import lax
from jax.experimental import pallas as pl
from jax.experimental.pallas import tpu as pltpu
from jax.sharding import PartitionSpec as P

HEAD_DIM = 64
epsilon = 1e-05
BF16 = jnp.bfloat16
F32 = jnp.float32
VMEM = pl.BlockSpec(memory_space=pltpu.VMEM)
SMEM = pl.BlockSpec(memory_space=pltpu.SMEM)
ANY = pl.BlockSpec(memory_space=pl.ANY)
HBM = pl.BlockSpec(memory_space=pltpu.HBM)


def params(mib):
    return pltpu.CompilerParams(vmem_limit_bytes=mib << 20)


def cost(flops, moved, special=0):
    return pl.CostEstimate(flops=flops >> 8, bytes_accessed=moved >> 8, transcendentals=special >> 8)


def swap(block, axis, mask):
    count = lax.axis_size(axis)
    return lax.ppermute(block, axis, [(i, i ^ mask) for i in range(count)])


def layer_norm(values, gain):
    mean = jnp.mean(values, axis=-1, keepdims=True)
    centred = values - mean
    spread = jnp.mean(centred * centred, axis=-1, keepdims=True)
    return centred * lax.rsqrt(spread + epsilon) * gain


def norm_kernel(count, place_ref, gain_ref, *refs):
    raw, (normed_ref, own_ref) = refs[:count], refs[count:]
    gain = gain_ref[0:1, :]
    for k in range(count):
        where = place_ref[k]
        block = raw[k][0]
        normed_ref[where] = layer_norm(block.astype(F32), gain).astype(BF16)

        @pl.when(where == 0)
        def _():
            own_ref[...] = block


def attention_kernel(count, shards, me_ref, near_ref, far_ref, *refs):
    pieces, outs = refs[:shards], refs[shards : shards + count]
    weights, sems = refs[shards + count :]
    depth, cols = pieces[0].shape[1:]
    me = me_ref[0]
    copies = []
    for k in range(shards):
        rows = pl.ds(pl.multiple_of((me ^ k) * depth, depth), depth)
        copy = pltpu.make_async_copy(pieces[k], weights.at[:, rows, :], sems.at[k])
        copy.start()
        copies.append(copy)
    for copy in copies:
        copy.wait()
    frames = near_ref.shape[1]
    head = lax.broadcasted_iota(jnp.int32, (frames, cols), 1) // HEAD_DIM
    scale = HEAD_DIM**-0.5
    for k in range(count):
        x = (far_ref if k & 1 else near_ref)[k >> 1]
        q, key, val = [
            jnp.dot(x, weights[i], preferred_element_type=F32).astype(BF16) for i in range(3)
        ]
        q = q * jnp.asarray(scale, BF16)
        total = jnp.zeros((frames, cols), F32)
        for h in range(cols // HEAD_DIM):
            mine = head == h
            scores = lax.dot_general(
                jnp.where(mine, q, jnp.zeros_like(q)),
                key,
                (((1,), (1,)), ((), ())),
                preferred_element_type=F32,
            )
            exps = jnp.exp(scores - jnp.max(scores, axis=-1, keepdims=True))
            norm = 1.0 / jnp.sum(exps, axis=-1, keepdims=True)
            probs = (exps * norm).astype(BF16)
            total = jnp.where(mine, jnp.dot(probs, val, preferred_element_type=F32), total)
        outs[k][...] = total.astype(BF16)


def mix_kernel(
    count, experts, capacity, me_ref, own_ref, near_ref, far_ref, gain_ref, router_ref, rows_ref, cols_ref, *refs
):
    blocks, (slots_ref, mixed_ref, gate_ref), (wide,) = refs[:count], refs[count : count + 3], refs[count + 3 :]
    frames, depth = blocks[0].shape
    me = me_ref[0]
    part = near_ref.shape[1]
    for held, side in ((near_ref, me & 1), (far_ref, 1 - (me & 1))):
        total = jnp.zeros((frames, part), F32)
        for k in range(count):
            rows = pl.ds(pl.multiple_of((me ^ k) * depth, depth), depth)
            total += jnp.dot(blocks[k][...], held[rows, :], preferred_element_type=F32)
        wide[:, pl.ds(pl.multiple_of(side * part, part), part)] = total
    mixed = (own_ref[...].astype(F32) + wide[...]).astype(BF16)
    mixed_ref[...] = mixed
    normed = layer_norm(mixed.astype(F32), gain_ref[1:2, :]).astype(BF16)
    first, second = rows_ref[0:1, :], rows_ref[1:2, :]
    which = lax.broadcasted_iota(jnp.int32, (experts, frames), 0)
    named = ((which == first) | (which == second)).astype(F32)
    before = (
        lax.broadcasted_iota(jnp.int32, (frames, frames), 0)
        < lax.broadcasted_iota(jnp.int32, (frames, frames), 1)
    ).astype(F32)
    rank = jnp.dot(named, before, preferred_element_type=F32) + (which * capacity).astype(F32)
    slot = lax.broadcasted_iota(jnp.int32, (experts * capacity, frames), 0).astype(F32)
    place0 = jnp.sum(jnp.where(which == first, rank, 0.0), axis=0, keepdims=True)
    place1 = jnp.sum(jnp.where(which == second, rank, 0.0), axis=0, keepdims=True)
    spread = ((slot == place0) | (slot == place1)).astype(F32).astype(BF16)
    slots_ref[...] = jnp.dot(spread, normed, preferred_element_type=F32).astype(BF16)
    high = router_ref[...].astype(BF16)
    rest = router_ref[...] - high.astype(F32)
    middle = rest.astype(BF16)
    low = (rest - middle.astype(F32)).astype(BF16)
    logits = (
        jnp.dot(normed, low, preferred_element_type=F32)
        + jnp.dot(normed, middle, preferred_element_type=F32)
    ) + jnp.dot(normed, high, preferred_element_type=F32)
    lane = lax.broadcasted_iota(jnp.int32, (frames, experts), 1)
    ahead = jnp.sum(jnp.where(lane == cols_ref[:, 0:1], logits, 0.0), axis=1, keepdims=True)
    behind = jnp.sum(jnp.where(lane == cols_ref[:, 1:2], logits, 0.0), axis=1, keepdims=True)
    gate_ref[...] = jnp.broadcast_to(jax.nn.sigmoid(ahead - behind), gate_ref.shape)


def fetch(cuts, refs, buf, sems):
    copies = [[] for _ in range(buf.shape[0])]
    for k, (at, start, size) in enumerate(cuts):
        copy = pltpu.make_async_copy(
            refs[k].at[0], buf.at[at, pl.ds(start, size), :], sems.at[k]
        )
        copy.start()
        copies[at].append(copy)
    return copies


def hidden_kernel(cuts, slots_ref, *refs):
    hidden_ref, buf, sems = refs[len(cuts) :]
    count, _, inner = buf.shape
    copies = fetch(cuts, refs, buf, sems)
    step = min(512, inner)
    for at in range(count):
        for copy in copies[at]:
            copy.wait()
        for part in range(0, inner, step):
            half = 0.5 * jnp.dot(
                slots_ref[...], buf[at, :, part : part + step], preferred_element_type=F32
            )
            hidden_ref[at, :, part : part + step] = (half + half * jnp.tanh(half)).astype(BF16)


def answer_kernel(cuts, near_ref, far_ref, *refs):
    answer_ref, buf, total, sems = refs[len(cuts) :]
    near = near_ref.shape[0]
    count, _, width = buf.shape
    copies = fetch(cuts, refs, buf, sems)
    step = width // 2
    for at in range(count):
        for copy in copies[at]:
            copy.wait()
        hidden = near_ref[at] if at < near else far_ref[at - near]
        for part in range(0, width, step):
            where = slice(part, part + step)
            down = jnp.dot(hidden, buf[at, :, where], preferred_element_type=F32)
            if at == 0:
                total[:, where] = down
            elif at < count - 1:
                total[:, where] += down
            else:
                answer_ref[:, where] = (total[:, where] + down).astype(BF16)


def combine_kernel(experts, capacity, count, mixed_ref, gate_ref, cols_ref, *refs):
    answers, out_ref = refs[:count], refs[count]
    frames = mixed_ref.shape[0]
    first, second = cols_ref[:, 0:1], cols_ref[:, 1:2]
    lane = lax.broadcasted_iota(jnp.int32, (frames, experts), 1)
    named = ((lane == first) | (lane == second)).astype(F32)
    before = (
        lax.broadcasted_iota(jnp.int32, (frames, frames), 1)
        < lax.broadcasted_iota(jnp.int32, (frames, frames), 0)
    ).astype(F32)
    rank = jnp.dot(before, named, preferred_element_type=F32) + (lane * capacity).astype(F32)
    slot = lax.broadcasted_iota(jnp.int32, (frames, experts * capacity), 1).astype(F32)
    picks = []
    for chosen in (first, second):
        place = jnp.sum(jnp.where(lane == chosen, rank, 0.0), axis=1, keepdims=True)
        picks.append((slot == place).astype(F32).astype(BF16))
    gate = gate_ref[:, 0:1]
    cols = mixed_ref.shape[1] // count
    for c in range(count):
        where = slice(c * cols, (c + 1) * cols)
        back = [jnp.dot(pick, answers[c][...], preferred_element_type=F32) for pick in picks]
        result = mixed_ref[:, where].astype(F32) + gate * back[0] + (1.0 - gate) * back[1]
        out_ref[0, :, where] = result.astype(BF16)


def spread_over(block, axis, low):
    held = {0: block}
    bit = lax.axis_size(axis) // 2
    while bit >= low:
        for k in list(held):
            held[k | bit] = swap(held[k], axis, bit)
        bit //= 2
    return held


def cut(size, sixteenths):
    starts = [sum(sixteenths[:i]) * size // 16 for i in range(len(sixteenths) + 1)]
    return [(a, b - a) for a, b in zip(starts, starts[1:])]


def after(values, earlier):
    return lax.optimization_barrier((values, earlier))[0]


def body(
    frames_in, pit_order, expert_ids, norm_gains, attn_qkv, attn_out, router, expert_in, expert_out
):
    dp_count = lax.axis_size("dp")
    exp_count = lax.axis_size("expert")
    me = lax.axis_index("dp").astype(jnp.int32)
    exp_index = lax.axis_index("expert").astype(jnp.int32)
    frames, width = frames_in.shape[1:]
    top = expert_ids.shape[2]
    capacity = frames * top * 5 // (4 * exp_count)
    slots_count = exp_count * capacity
    half = dp_count // 2
    share = width // dp_count
    inner = expert_in.shape[2]

    raw = spread_over(frames_in, "dp", 2)

    qkv = {0: lax.dynamic_slice_in_dim(attn_qkv, me * share, share, axis=2)}
    for far in range(2, exp_count, 2):
        qkv[far] = swap(qkv[0], "expert", far)
    for far in range(0, exp_count, 2):
        qkv[far | 1] = swap(qkv[far], "expert", 1)

    rows = width // 2
    proj_near = lax.all_gather(
        lax.dynamic_slice_in_dim(attn_out, (me % 2) * rows, rows, axis=1),
        "expert",
        axis=0,
        tiled=True,
    )

    in_cuts = cut(width, (5, 8, 3))
    out_cuts = cut(inner, (3, 13))
    in_chunks = [lax.slice_in_dim(expert_in, a, a + n, axis=1) for a, n in in_cuts]
    out_chunks = [lax.slice_in_dim(expert_out, a, a + n, axis=1) for a, n in out_cuts]
    in_held = [spread_over(in_chunks[0], "dp", 2)]

    early = [qkv[1], *[qkv[k] for k in range(2, exp_count, 2)], qkv[3], in_held[0]]
    raw[half] = after(raw[half], early)

    groups = len(raw)
    member = jnp.arange(groups, dtype=jnp.int32) * 2
    meeting = ((me ^ member) % half) * exp_count + exp_index
    place = jnp.where(pit_order[meeting, 0] == 0, member, member ^ half) // 2

    near, stream = pl.pallas_call(
        functools.partial(norm_kernel, groups),
        out_shape=(
            jax.ShapeDtypeStruct((groups, frames, width), BF16),
            jax.ShapeDtypeStruct((frames, width), BF16),
        ),
        in_specs=[SMEM, VMEM] + [VMEM] * groups,
        out_specs=(VMEM, VMEM),
        compiler_params=params(32),
        cost_estimate=cost(groups * frames * width * 8, groups * frames * width * 4),
        name="norm",
    )(place, norm_gains, *[raw[2 * k] for k in range(groups)])
    far = swap(near, "dp", 1)
    in_held.append(spread_over(after(in_chunks[1], near), "dp", 2))
    far = after(far, in_held[1])
    in_held.append(spread_over(after(in_chunks[2], (in_held[1], far, qkv)), "dp", 2))

    contexts = pl.pallas_call(
        functools.partial(attention_kernel, dp_count, exp_count),
        out_shape=[jax.ShapeDtypeStruct((frames, share), BF16)] * dp_count,
        in_specs=[SMEM, VMEM, VMEM] + [ANY] * exp_count,
        out_specs=[VMEM] * dp_count,
        scratch_shapes=[
            pltpu.VMEM((3, width, share), BF16),
            pltpu.SemaphoreType.DMA((exp_count,)),
        ],
        compiler_params=params(32),
        cost_estimate=cost(
            2 * frames * width * width * 3 + 16 * frames * frames * width, 5 << 20, frames * frames * 16
        ),
        name="attention",
    )(exp_index[None], near, far, *[qkv[k] for k in range(exp_count)])

    contexts = after(contexts, in_held[2])
    crossed = [swap(contexts[k], "dp", k) for k in range(1, dp_count)]

    proj_far = swap(after(proj_near, contexts), "dp", 1)

    out_held = [spread_over(after(out_chunks[0], crossed), "dp", 2)]

    cols = expert_ids[0]
    slots, mixed, gate = pl.pallas_call(
        functools.partial(mix_kernel, dp_count, exp_count, capacity),
        out_shape=(
            jax.ShapeDtypeStruct((slots_count, width), BF16),
            jax.ShapeDtypeStruct((frames, width), BF16),
            jax.ShapeDtypeStruct((frames, 128), F32),
        ),
        in_specs=[SMEM] + [VMEM] * (7 + dp_count),
        out_specs=(VMEM, VMEM, VMEM),
        scratch_shapes=[pltpu.VMEM((frames, width), F32)],
        compiler_params=params(32),
        cost_estimate=cost(2 * frames * width * (width + slots_count), 5 << 20),
        name="mix",
    )(me[None], stream, proj_near, proj_far, norm_gains, router, cols.T, cols, contexts[0], *crossed)

    slots = after(slots, out_held[0])
    out_held.append(spread_over(after(out_chunks[1], (out_held[0], mixed)), "dp", 2))
    in_far, in_near, in_places = [swap(after(expert_in, mixed), "dp", 1)], [expert_in], [(0, 0, width)]
    out_far, out_near, out_places = [swap(after(expert_out, mixed), "dp", 1)], [expert_out], [(0, 0, inner)]
    for k in range(2, dp_count, 2):
        for held, place in zip(in_held, in_cuts):
            in_near.append(held[k])
            in_far.append(swap(after(held[k], mixed), "dp", 1))
            in_places.append((k // 2, *place))

    arrived = lax.all_to_all(
        slots.reshape(exp_count, capacity, width), "expert", split_axis=0, concat_axis=0, tiled=True
    ).reshape(slots_count, width)


    def hidden_units(slots_in, held, name):
        return pl.pallas_call(
            functools.partial(hidden_kernel, in_places),
            out_shape=jax.ShapeDtypeStruct((groups, slots_count, inner), BF16),
            in_specs=[VMEM] + [ANY] * len(in_places),
            out_specs=VMEM,
            scratch_shapes=[
                pltpu.VMEM((groups, width, inner), BF16),
                pltpu.SemaphoreType.DMA((len(in_places),)),
            ],
            compiler_params=params(48),
            cost_estimate=cost(2 * slots_count * width * inner * groups, 8 << 20),
            name=name,
        )(slots_in, *held)

    hidden_near = hidden_units(arrived, in_near, "hidden_near")
    hidden_far = hidden_units(after(arrived, hidden_near), in_far, "hidden_far")
    for k in range(2, dp_count, 2):
        for held, place in zip(out_held, out_cuts):
            out_near.append(held[k])
            out_far.append(swap(after(held[k], hidden_near), "dp", 1))
            out_places.append((k // 2, *place))
    out_places += [(groups + at, *place) for at, *place in out_places]

    answer = pl.pallas_call(
        functools.partial(answer_kernel, out_places),
        out_shape=jax.ShapeDtypeStruct((slots_count, width), BF16),
        in_specs=[VMEM, VMEM] + [ANY] * len(out_places),
        out_specs=VMEM,
        scratch_shapes=[
            pltpu.VMEM((dp_count, inner, width), BF16),
            pltpu.VMEM((slots_count, width), F32),
            pltpu.SemaphoreType.DMA((len(out_places),)),
        ],
        compiler_params=params(48),
        cost_estimate=cost(2 * slots_count * width * inner * dp_count, 10 << 20),
        name="answer",
    )(hidden_near, hidden_far, *out_near, *out_far)
    returned = lax.all_to_all(
        answer.reshape(exp_count, capacity, width), "expert", split_axis=0, concat_axis=0, tiled=True
    ).reshape(slots_count, width)

    return pl.pallas_call(
        functools.partial(combine_kernel, exp_count, capacity, 1),
        out_shape=jax.ShapeDtypeStruct((1, frames, width), BF16),
        in_specs=[VMEM] * 4,
        out_specs=VMEM,
        compiler_params=params(32),
        cost_estimate=cost(4 * frames * slots_count * width, 3 << 20),
        name="combine",
    )(mixed, gate, cols, returned)


def solution(mesh):
    return jax.shard_map(
        body,
        mesh=mesh,
        in_specs=(
            P(("dp", "expert"), None, None),
            P(),
            P(("dp", "expert"), None, None),
            P(),
            P(None, "expert", None),
            P("expert", None),
            P(),
            P("expert", None, "dp"),
            P("expert", "dp", None),
        ),
        out_specs=P(("dp", "expert"), None, None),
        check_vma=False,
    )
```

```python
import functools

import jax
import jax.numpy as jnp
from jax import lax
from jax.experimental import pallas as pl
from jax.experimental.pallas import tpu as pltpu
from jax.sharding import PartitionSpec as P

HEAD_DIM = 64
epsilon = 1e-05
BF16 = jnp.bfloat16
F32 = jnp.float32
VMEM = pl.BlockSpec(memory_space=pltpu.VMEM)
SMEM = pl.BlockSpec(memory_space=pltpu.SMEM)
ANY = pl.BlockSpec(memory_space=pl.ANY)
HBM = pl.BlockSpec(memory_space=pltpu.HBM)


def params(mib):
    return pltpu.CompilerParams(vmem_limit_bytes=mib << 20)


def cost(flops, moved, special=0):
    return pl.CostEstimate(flops=flops >> 8, bytes_accessed=moved >> 8, transcendentals=special >> 8)


def swap(block, axis, mask):
    count = lax.axis_size(axis)
    return lax.ppermute(block, axis, [(i, i ^ mask) for i in range(count)])


def layer_norm(values, gain):
    mean = jnp.mean(values, axis=-1, keepdims=True)
    centred = values - mean
    spread = jnp.mean(centred * centred, axis=-1, keepdims=True)
    return centred * lax.rsqrt(spread + epsilon) * gain


def norm_kernel(count, place_ref, gain_ref, *refs):
    raw, (normed_ref, own_ref) = refs[:count], refs[count:]
    gain = gain_ref[0:1, :]
    for k in range(count):
        where = place_ref[k]
        block = raw[k][0]
        normed_ref[where] = layer_norm(block.astype(F32), gain).astype(BF16)

        @pl.when(where == 0)
        def _():
            own_ref[...] = block


def attention_kernel(count, shards, me_ref, near_ref, far_ref, *refs):
    pieces, outs = refs[:shards], refs[shards : shards + count]
    weights, held, sems, out_sems = refs[shards + count :]
    depth, cols = pieces[0].shape[1:]
    me = me_ref[0]
    copies = []
    for k in range(shards):
        rows = pl.ds(pl.multiple_of((me ^ k) * depth, depth), depth)
        copy = pltpu.make_async_copy(pieces[k], weights.at[:, rows, :], sems.at[k])
        copy.start()
        copies.append(copy)
    for copy in copies:
        copy.wait()
    sent = []
    frames = near_ref.shape[1]
    head = lax.broadcasted_iota(jnp.int32, (frames, cols), 1) // HEAD_DIM
    scale = HEAD_DIM**-0.5
    for k in range(count):
        x = (far_ref if k & 1 else near_ref)[k >> 1]
        q, key, val = [
            jnp.dot(x, weights[i], preferred_element_type=F32).astype(BF16) for i in range(3)
        ]
        q = q * jnp.asarray(scale, BF16)
        total = jnp.zeros((frames, cols), F32)
        for h in range(cols // HEAD_DIM):
            mine = head == h
            scores = lax.dot_general(
                jnp.where(mine, q, jnp.zeros_like(q)),
                key,
                (((1,), (1,)), ((), ())),
                preferred_element_type=F32,
            )
            exps = jnp.exp(scores - jnp.max(scores, axis=-1, keepdims=True))
            norm = 1.0 / jnp.sum(exps, axis=-1, keepdims=True)
            probs = (exps * norm).astype(BF16)
            total = jnp.where(mine, jnp.dot(probs, val, preferred_element_type=F32), total)
        held[k] = total.astype(BF16)
        copy = pltpu.make_async_copy(held.at[k], outs[k], out_sems.at[k])
        copy.start()
        sent.append(copy)
    for copy in sent:
        copy.wait()


def mix_kernel(count, experts, capacity, me_ref, gain_ref, router_ref, rows_ref, cols_ref, *refs):
    sources, refs = refs[: count + 3], refs[count + 3 :]
    slots_out, mixed_out, gate_ref, own_ref, near_ref, far_ref, blocks, wide, slots_ref, mixed_ref, sems = refs
    places = [own_ref, near_ref, far_ref, *[blocks.at[k] for k in range(count)]]
    copies = [
        pltpu.make_async_copy(source, place, sems.at[k])
        for k, (source, place) in enumerate(zip(sources, places))
    ]
    for copy in copies:
        copy.start()
    _, frames, depth = blocks.shape
    me = me_ref[0]
    part = near_ref.shape[1]
    for copy in copies:
        copy.wait()
    for held, side in ((near_ref, me & 1), (far_ref, 1 - (me & 1))):
        total = jnp.zeros((frames, part), F32)
        for k in range(count):
            rows = pl.ds(pl.multiple_of((me ^ k) * depth, depth), depth)
            total += jnp.dot(blocks[k], held[rows, :], preferred_element_type=F32)
        wide[:, pl.ds(pl.multiple_of(side * part, part), part)] = total
    mixed = (own_ref[...].astype(F32) + wide[...]).astype(BF16)
    mixed_ref[...] = mixed
    mixed_copy = pltpu.make_async_copy(mixed_ref, mixed_out, sems.at[0])
    mixed_copy.start()
    normed = layer_norm(mixed.astype(F32), gain_ref[1:2, :]).astype(BF16)
    first, second = rows_ref[0:1, :], rows_ref[1:2, :]
    which = lax.broadcasted_iota(jnp.int32, (experts, frames), 0)
    named = ((which == first) | (which == second)).astype(F32)
    before = (
        lax.broadcasted_iota(jnp.int32, (frames, frames), 0)
        < lax.broadcasted_iota(jnp.int32, (frames, frames), 1)
    ).astype(F32)
    rank = jnp.dot(named, before, preferred_element_type=F32) + (which * capacity).astype(F32)
    slot = lax.broadcasted_iota(jnp.int32, (experts * capacity, frames), 0).astype(F32)
    place0 = jnp.sum(jnp.where(which == first, rank, 0.0), axis=0, keepdims=True)
    place1 = jnp.sum(jnp.where(which == second, rank, 0.0), axis=0, keepdims=True)
    spread = ((slot == place0) | (slot == place1)).astype(F32).astype(BF16)
    slots_ref[...] = jnp.dot(spread, normed, preferred_element_type=F32).astype(BF16)
    slots_copy = pltpu.make_async_copy(slots_ref, slots_out, sems.at[1])
    slots_copy.start()
    high = router_ref[...].astype(BF16)
    rest = router_ref[...] - high.astype(F32)
    middle = rest.astype(BF16)
    low = (rest - middle.astype(F32)).astype(BF16)
    logits = sum(
        lax.dot_general(normed, term, (((1,), (1,)), ((), ())), preferred_element_type=F32)
        for term in (low, middle, high)
    )
    lane = lax.broadcasted_iota(jnp.int32, (frames, experts), 1)
    ahead = jnp.sum(jnp.where(lane == cols_ref[:, 0:1], logits, 0.0), axis=1, keepdims=True)
    behind = jnp.sum(jnp.where(lane == cols_ref[:, 1:2], logits, 0.0), axis=1, keepdims=True)
    gate_ref[...] = jnp.broadcast_to(jax.nn.sigmoid(ahead - behind), gate_ref.shape)
    mixed_copy.wait()
    slots_copy.wait()


def split_kernel(cuts, whole_ref, *refs):
    outs, sems = refs[: len(cuts)], refs[len(cuts)]
    copies = [
        pltpu.make_async_copy(whole_ref.at[:, pl.ds(start, size), :], outs[k], sems.at[k])
        for k, (start, size) in enumerate(cuts)
    ]
    for copy in copies:
        copy.start()
    for copy in copies:
        copy.wait()


def fetch(cuts, step, refs, buf, sems):
    count, _, cols = buf.shape
    copies = {(at, part): [] for at in range(count) for part in range(0, cols, step)}
    for at, part in copies:
        for k, (of, start, size) in enumerate(cuts):
            if of == at:
                where = pl.ds(part, step)
                copy = pltpu.make_async_copy(
                    refs[k].at[0, :, where],
                    buf.at[at, pl.ds(start, size), where],
                    sems.at[k, part // step],
                )
                copy.start()
                copies[at, part].append(copy)
    return copies


def hidden_kernel(cuts, step, slots_ref, *refs):
    hidden_ref, buf, sems = refs[len(cuts) :]
    for (at, part), pieces in fetch(cuts, step, refs, buf, sems).items():
        for piece in pieces:
            piece.wait()
        where = slice(part, part + step)
        half = 0.5 * jnp.dot(slots_ref[...], buf[at, :, where], preferred_element_type=F32)
        hidden_ref[at, :, where] = (half + half * jnp.tanh(half)).astype(BF16)


def answer_kernel(slices, step, held, before, *refs):
    hidden, weights, refs = refs[:held], refs[held : held + len(slices)], refs[held + len(slices) :]
    total_ref = refs[0] if before else None
    answer_ref, buf, sems = refs[1:] if before else refs
    cuts = [(at, 0, buf.shape[1]) for at in range(len(slices))]
    copies = fetch(cuts, step, weights, buf, sems)
    for part in range(0, buf.shape[2], step):
        where = slice(part, part + step)
        total = total_ref[:, where] if before else 0.0
        for at, (of, place) in enumerate(slices):
            for piece in copies[at, part]:
                piece.wait()
            total += jnp.dot(hidden[of][place], buf[at, :, where], preferred_element_type=F32)
        answer_ref[:, where] = total.astype(answer_ref.dtype)


def combine_kernel(experts, capacity, gate_ref, cols_ref, mixed_in, answer_in, out_ref, mixed_ref, answer_ref, sems):
    copies = [
        pltpu.make_async_copy(answer_in, answer_ref, sems.at[0]),
        pltpu.make_async_copy(mixed_in, mixed_ref, sems.at[1]),
    ]
    for copy in copies:
        copy.start()
    frames = mixed_ref.shape[0]
    first, second = cols_ref[:, 0:1], cols_ref[:, 1:2]
    lane = lax.broadcasted_iota(jnp.int32, (frames, experts), 1)
    named = ((lane == first) | (lane == second)).astype(F32)
    before = (
        lax.broadcasted_iota(jnp.int32, (frames, frames), 1)
        < lax.broadcasted_iota(jnp.int32, (frames, frames), 0)
    ).astype(F32)
    rank = jnp.dot(before, named, preferred_element_type=F32) + (lane * capacity).astype(F32)
    slot = lax.broadcasted_iota(jnp.int32, (frames, experts * capacity), 1).astype(F32)
    picks = []
    for chosen in (first, second):
        place = jnp.sum(jnp.where(lane == chosen, rank, 0.0), axis=1, keepdims=True)
        picks.append((slot == place).astype(F32).astype(BF16))
    gate = gate_ref[:, 0:1]
    for copy in copies:
        copy.wait()
    step = mixed_ref.shape[1] // 2
    for part in range(0, 2 * step, step):
        where = slice(part, part + step)
        back = [jnp.dot(pick, answer_ref[:, where], preferred_element_type=F32) for pick in picks]
        result = mixed_ref[:, where].astype(F32) + gate * back[0] + (1.0 - gate) * back[1]
        out_ref[0, :, where] = result.astype(BF16)


def spread_over(block, axis, low):
    held = {0: block}
    bit = lax.axis_size(axis) // 2
    while bit >= low:
        for k in list(held):
            held[k | bit] = swap(held[k], axis, bit)
        bit //= 2
    return held


def cut(size, shares):
    starts = [sum(shares[:i]) * size // sum(shares) for i in range(len(shares) + 1)]
    return [(a, b - a) for a, b in zip(starts, starts[1:])]


def after(values, earlier):
    return lax.optimization_barrier((values, earlier))[0]


def body(
    frames_in, pit_order, expert_ids, norm_gains, attn_qkv, attn_out, router, expert_in, expert_out
):
    dp_count = lax.axis_size("dp")
    exp_count = lax.axis_size("expert")
    me = lax.axis_index("dp").astype(jnp.int32)
    exp_index = lax.axis_index("expert").astype(jnp.int32)
    frames, width = frames_in.shape[1:]
    top = expert_ids.shape[2]
    capacity = frames * top * 5 // (4 * exp_count)
    slots_count = exp_count * capacity
    half = dp_count // 2
    share = width // dp_count
    inner = expert_in.shape[2]

    raw = spread_over(frames_in, "dp", 2)

    qkv = {0: lax.dynamic_slice_in_dim(attn_qkv, me * share, share, axis=2)}
    for far in range(2, exp_count, 2):
        qkv[far] = swap(qkv[0], "expert", far)
    for far in range(0, exp_count, 2):
        qkv[far | 1] = swap(qkv[far], "expert", 1)

    rows = width // 2
    proj_near = lax.all_gather(
        lax.dynamic_slice_in_dim(attn_out, (me % 2) * rows, rows, axis=1),
        "expert",
        axis=0,
        tiled=True,
    )

    in_cuts = cut(width, (20, 23, 9, 12))
    in_chunks = pl.pallas_call(
        functools.partial(split_kernel, in_cuts),
        out_shape=[jax.ShapeDtypeStruct((1, n, inner), BF16) for _, n in in_cuts],
        in_specs=[HBM],
        out_specs=[HBM] * len(in_cuts),
        scratch_shapes=[pltpu.SemaphoreType.DMA((len(in_cuts),))],
        compiler_params=params(32),
        cost_estimate=cost(0, 4 << 20),
        name="split",
    )(expert_in)
    in_held = [spread_over(in_chunks[0], "dp", 2)]

    early = [qkv[1], *[qkv[k] for k in range(2, exp_count, 2)], qkv[3], in_held[0]]
    raw[half] = after(raw[half], early)

    groups = len(raw)
    member = jnp.arange(groups, dtype=jnp.int32) * 2
    meeting = ((me ^ member) % half) * exp_count + exp_index
    place = jnp.where(pit_order[meeting, 0] == 0, member, member ^ half) // 2

    near, stream = pl.pallas_call(
        functools.partial(norm_kernel, groups),
        out_shape=(
            jax.ShapeDtypeStruct((groups, frames, width), BF16),
            jax.ShapeDtypeStruct((frames, width), BF16),
        ),
        in_specs=[SMEM, VMEM] + [VMEM] * groups,
        out_specs=(VMEM, VMEM),
        compiler_params=params(32),
        cost_estimate=cost(groups * frames * width * 8, groups * frames * width * 4),
        name="norm",
    )(place, norm_gains, *[raw[2 * k] for k in range(groups)])
    far = swap(near, "dp", 1)
    in_held.append(spread_over(after(in_chunks[1], near), "dp", 2))
    far = after(far, in_held[1])
    in_held.append(spread_over(after(in_chunks[2], (in_held[1], far, qkv)), "dp", 2))

    contexts = pl.pallas_call(
        functools.partial(attention_kernel, dp_count, exp_count),
        out_shape=[jax.ShapeDtypeStruct((frames, share), BF16)] * dp_count,
        in_specs=[SMEM, VMEM, VMEM] + [ANY] * exp_count,
        out_specs=[ANY] * dp_count,
        scratch_shapes=[
            pltpu.VMEM((3, width, share), BF16),
            pltpu.VMEM((dp_count, frames, share), BF16),
            pltpu.SemaphoreType.DMA((exp_count,)),
            pltpu.SemaphoreType.DMA((dp_count,)),
        ],
        compiler_params=params(32),
        cost_estimate=cost(
            2 * frames * width * width * 3 + 16 * frames * frames * width, 5 << 20, frames * frames * 16
        ),
        name="attention",
    )(exp_index[None], near, far, *[qkv[k] for k in range(exp_count)])

    contexts = after(contexts, in_held[2])
    crossed = [swap(contexts[k], "dp", k) for k in range(1, dp_count)]

    proj_far = swap(after(proj_near, contexts), "dp", 1)

    in_held.append(spread_over(after(in_chunks[3], crossed), "dp", 2))

    cols = expert_ids[0]
    slots, mixed, gate = pl.pallas_call(
        functools.partial(mix_kernel, dp_count, exp_count, capacity),
        out_shape=(
            jax.ShapeDtypeStruct((slots_count, width), BF16),
            jax.ShapeDtypeStruct((frames, width), BF16),
            jax.ShapeDtypeStruct((frames, 128), F32),
        ),
        in_specs=[SMEM] + [VMEM] * 4 + [ANY] * (3 + dp_count),
        out_specs=(ANY, ANY, VMEM),
        scratch_shapes=[
            pltpu.VMEM((frames, width), BF16),
            pltpu.VMEM((width, rows), BF16),
            pltpu.VMEM((width, rows), BF16),
            pltpu.VMEM((dp_count, frames, share), BF16),
            pltpu.VMEM((frames, width), F32),
            pltpu.VMEM((slots_count, width), BF16),
            pltpu.VMEM((frames, width), BF16),
            pltpu.SemaphoreType.DMA((dp_count + 3,)),
        ],
        compiler_params=params(32),
        cost_estimate=cost(2 * frames * width * (width + slots_count), 5 << 20),
        name="mix",
    )(me[None], norm_gains, router.T, cols.T, cols, stream, proj_near, proj_far, contexts[0], *crossed)

    slots = after(slots, in_held[3])
    out_held = spread_over(after(expert_out, (in_held[3], mixed)), "dp", 2)
    in_far, in_near, in_places = [swap(after(expert_in, mixed), "dp", 1)], [expert_in], [(0, 0, width)]
    out_own = swap(after(expert_out, mixed), "dp", 1)
    for k in range(2, dp_count, 2):
        for held, place in zip(in_held, in_cuts):
            in_near.append(held[k])
            in_far.append(swap(after(held[k], mixed), "dp", 1))
            in_places.append((k // 2, *place))

    arrived = lax.all_to_all(
        slots.reshape(exp_count, capacity, width), "expert", split_axis=0, concat_axis=0, tiled=True
    ).reshape(slots_count, width)


    arrived = after(arrived, (in_far, out_own))
    step = min(256, inner)

    def hidden_units(slots_in, held, name):
        return pl.pallas_call(
            functools.partial(hidden_kernel, in_places, step),
            out_shape=jax.ShapeDtypeStruct((groups, slots_count, inner), BF16),
            in_specs=[VMEM] + [ANY] * len(in_places),
            out_specs=VMEM,
            scratch_shapes=[
                pltpu.VMEM((groups, width, inner), BF16),
                pltpu.SemaphoreType.DMA((len(in_places), inner // step)),
            ],
            compiler_params=params(48),
            cost_estimate=cost(2 * slots_count * width * inner * groups, 8 << 20),
            name=name,
        )(slots_in, *held)

    hidden = [hidden_units(arrived, in_near, "hidden_near")]
    hidden.append(hidden_units(after(arrived, hidden[0]), in_far, "hidden_far"))

    def answers(slices, weights, before, name):
        count = len(slices)
        used = sorted({of for of, _ in slices})
        slices = [(used.index(of), place) for of, place in slices]
        inputs = [hidden[of] for of in used]
        extra = [] if before is None else [before]
        return pl.pallas_call(
            functools.partial(answer_kernel, slices, 256, len(used), bool(extra)),
            out_shape=jax.ShapeDtypeStruct((slots_count, width), BF16 if name == "answer_far" else F32),
            in_specs=[VMEM] * len(used) + [ANY] * count + [VMEM] * len(extra),
            out_specs=VMEM,
            scratch_shapes=[
                pltpu.VMEM((count, inner, width), BF16),
                pltpu.SemaphoreType.DMA((count, width // 256)),
            ],
            compiler_params=params(40),
            cost_estimate=cost(2 * slots_count * width * inner * count, 10 << 20),
            name=name,
        )(*inputs, *weights, *extra)

    distant = range(1, groups)
    answer = answers([(0, 0), (1, 0)], [expert_out, out_own], None, "answer_own")
    out_near = [after(out_held[2 * k], hidden[1]) for k in distant]
    out_far = [swap(block, "dp", 1) for block in out_near]
    answer = answers([(0, k) for k in distant], out_near, answer, "answer_near")
    answer = answers([(1, k) for k in distant], out_far, answer, "answer_far")
    returned = lax.all_to_all(
        answer.reshape(exp_count, capacity, width), "expert", split_axis=0, concat_axis=0, tiled=True
    ).reshape(slots_count, width)

    return pl.pallas_call(
        functools.partial(combine_kernel, exp_count, capacity),
        out_shape=jax.ShapeDtypeStruct((1, frames, width), BF16),
        in_specs=[VMEM, VMEM, ANY, ANY],
        out_specs=VMEM,
        scratch_shapes=[
            pltpu.VMEM((frames, width), BF16),
            pltpu.VMEM((slots_count, width), BF16),
            pltpu.SemaphoreType.DMA((2,)),
        ],
        compiler_params=params(32),
        cost_estimate=cost(4 * frames * slots_count * width, 3 << 20),
        name="combine",
    )(gate, cols, mixed, returned)


def solution(mesh):
    return jax.shard_map(
        body,
        mesh=mesh,
        in_specs=(
            P(("dp", "expert"), None, None),
            P(),
            P(("dp", "expert"), None, None),
            P(),
            P(None, "expert", None),
            P("expert", None),
            P(),
            P("expert", None, "dp"),
            P("expert", "dp", None),
        ),
        out_specs=P(("dp", "expert"), None, None),
        check_vma=False,
    )
```

```python
import functools

import jax
import jax.numpy as jnp
from jax import lax
from jax.experimental import pallas as pl
from jax.experimental.pallas import tpu as pltpu
from jax.sharding import PartitionSpec as P

HEAD_DIM = 64
epsilon = 1e-05
BF16 = jnp.bfloat16
F32 = jnp.float32
VMEM = pl.BlockSpec(memory_space=pltpu.VMEM)
SMEM = pl.BlockSpec(memory_space=pltpu.SMEM)
ANY = pl.BlockSpec(memory_space=pl.ANY)
HBM = pl.BlockSpec(memory_space=pltpu.HBM)


def params(mib):
    return pltpu.CompilerParams(vmem_limit_bytes=mib << 20)


def cost(flops, moved, special=0):
    return pl.CostEstimate(flops=flops >> 8, bytes_accessed=moved >> 8, transcendentals=special >> 8)


def swap(block, axis, mask):
    count = lax.axis_size(axis)
    return lax.ppermute(block, axis, [(i, i ^ mask) for i in range(count)])


def layer_norm(values, gain):
    mean = jnp.mean(values, axis=-1, keepdims=True)
    centred = values - mean
    spread = jnp.mean(centred * centred, axis=-1, keepdims=True)
    return centred * lax.rsqrt(spread + epsilon) * gain


def norm_kernel(count, place_ref, gain_ref, *refs):
    raw, (normed_ref, own_ref) = refs[:count], refs[count:]
    gain = gain_ref[0:1, :]
    for k in range(count):
        where = place_ref[k]
        block = raw[k][0]
        normed_ref[where] = layer_norm(block.astype(F32), gain).astype(BF16)

        @pl.when(where == 0)
        def _():
            own_ref[...] = block


def attention_kernel(count, shards, me_ref, near_ref, far_ref, *refs):
    pieces, outs = refs[:shards], refs[shards : shards + count]
    weights, held, sems = refs[shards + count :]
    depth, cols = pieces[0].shape[1:]
    me = me_ref[0]
    for k in range(shards):
        weights[:, pl.ds(pl.multiple_of((me ^ k) * depth, depth), depth), :] = pieces[k][...]
    sent = []
    frames = near_ref.shape[1]
    head = lax.broadcasted_iota(jnp.int32, (frames, cols), 1) // HEAD_DIM
    scale = HEAD_DIM**-0.5
    for k in range(count):
        x = (far_ref if k & 1 else near_ref)[k >> 1]
        q, key, val = [
            jnp.dot(x, weights[i], preferred_element_type=F32).astype(BF16) for i in range(3)
        ]
        q = q * jnp.asarray(scale, BF16)
        total = jnp.zeros((frames, cols), F32)
        for h in range(cols // HEAD_DIM):
            mine = head == h
            scores = lax.dot_general(
                jnp.where(mine, q, jnp.zeros_like(q)),
                key,
                (((1,), (1,)), ((), ())),
                preferred_element_type=F32,
            )
            exps = jnp.exp(scores - jnp.max(scores, axis=-1, keepdims=True))
            norm = 1.0 / jnp.sum(exps, axis=-1, keepdims=True)
            probs = (exps * norm).astype(BF16)
            total = jnp.where(mine, jnp.dot(probs, val, preferred_element_type=F32), total)
        held[k] = total.astype(BF16)
        copy = pltpu.make_async_copy(held.at[k], outs[k], sems.at[k])
        copy.start()
        sent.append(copy)
    for copy in sent:
        copy.wait()


def mix_kernel(
    count, experts, capacity, me_ref, gain_ref, router_ref, rows_ref, cols_ref, own_ref, near_ref, far_ref, *refs
):
    blocks, (slots_out, mixed_out, gate_ref, wide, slots_ref, mixed_ref, sems) = refs[:count], refs[count:]
    frames, depth = blocks[0].shape
    me = me_ref[0]
    part = near_ref.shape[1]
    for held, side in ((near_ref, me & 1), (far_ref, 1 - (me & 1))):
        total = jnp.zeros((frames, part), F32)
        for k in range(count):
            rows = pl.ds(pl.multiple_of((me ^ k) * depth, depth), depth)
            total += jnp.dot(blocks[k][...], held[rows, :], preferred_element_type=F32)
        wide[:, pl.ds(pl.multiple_of(side * part, part), part)] = total
    mixed = (own_ref[...].astype(F32) + wide[...]).astype(BF16)
    mixed_ref[...] = mixed
    mixed_copy = pltpu.make_async_copy(mixed_ref, mixed_out, sems.at[0])
    mixed_copy.start()
    normed = layer_norm(mixed.astype(F32), gain_ref[1:2, :]).astype(BF16)
    first, second = rows_ref[0:1, :], rows_ref[1:2, :]
    which = lax.broadcasted_iota(jnp.int32, (experts, frames), 0)
    named = ((which == first) | (which == second)).astype(F32)
    before = (
        lax.broadcasted_iota(jnp.int32, (frames, frames), 0)
        < lax.broadcasted_iota(jnp.int32, (frames, frames), 1)
    ).astype(F32)
    rank = jnp.dot(named, before, preferred_element_type=F32) + (which * capacity).astype(F32)
    slot = lax.broadcasted_iota(jnp.int32, (experts * capacity, frames), 0).astype(F32)
    place0 = jnp.sum(jnp.where(which == first, rank, 0.0), axis=0, keepdims=True)
    place1 = jnp.sum(jnp.where(which == second, rank, 0.0), axis=0, keepdims=True)
    spread = ((slot == place0) | (slot == place1)).astype(F32).astype(BF16)
    slots_ref[...] = jnp.dot(spread, normed, preferred_element_type=F32).astype(BF16)
    slots_copy = pltpu.make_async_copy(slots_ref, slots_out, sems.at[1])
    slots_copy.start()
    high = router_ref[...].astype(BF16)
    rest = router_ref[...] - high.astype(F32)
    middle = rest.astype(BF16)
    low = (rest - middle.astype(F32)).astype(BF16)
    logits = sum(
        lax.dot_general(normed, term, (((1,), (1,)), ((), ())), preferred_element_type=F32)
        for term in (low, middle, high)
    )
    lane = lax.broadcasted_iota(jnp.int32, (frames, experts), 1)
    ahead = jnp.sum(jnp.where(lane == cols_ref[:, 0:1], logits, 0.0), axis=1, keepdims=True)
    behind = jnp.sum(jnp.where(lane == cols_ref[:, 1:2], logits, 0.0), axis=1, keepdims=True)
    gate_ref[...] = jnp.broadcast_to(jax.nn.sigmoid(ahead - behind), gate_ref.shape)
    mixed_copy.wait()
    slots_copy.wait()


def split_kernel(cuts, whole_ref, *refs):
    outs, sems = refs[: len(cuts)], refs[len(cuts)]
    copies = [
        pltpu.make_async_copy(whole_ref.at[:, :, pl.ds(start, size)], outs[k], sems.at[k])
        for k, (start, size) in enumerate(cuts)
    ]
    for copy in copies:
        copy.start()
    for copy in copies:
        copy.wait()


def hidden_kernel(cuts, step, slots_ref, *refs):
    hidden_ref = refs[len(cuts)]
    for weight, (at, start, size) in zip(refs, cuts):
        for part in range(0, size, step):
            end = min(part + step, size)
            half = 0.5 * jnp.dot(slots_ref[...], weight[0, :, part:end], preferred_element_type=F32)
            hidden_ref[at, :, start + part : start + end] = (half + half * jnp.tanh(half)).astype(BF16)


def answer_kernel(slices, step, held, before, *refs):
    hidden, weights, refs = refs[:held], refs[held : held + len(slices)], refs[held + len(slices) :]
    answer_ref = refs[-1]
    for part in range(0, answer_ref.shape[1], step):
        where = slice(part, part + step)
        total = refs[0][:, where] if before else 0.0
        for weight, (of, place) in zip(weights, slices):
            total += jnp.dot(hidden[of][place], weight[0, :, where], preferred_element_type=F32)
        answer_ref[:, where] = total.astype(answer_ref.dtype)


def combine_kernel(experts, capacity, gate_ref, cols_ref, answer_ref, mixed_in, out_ref, mixed_ref, sems):
    copy = pltpu.make_async_copy(mixed_in, mixed_ref, sems.at[0])
    copy.start()
    frames = mixed_ref.shape[0]
    first, second = cols_ref[:, 0:1], cols_ref[:, 1:2]
    lane = lax.broadcasted_iota(jnp.int32, (frames, experts), 1)
    named = ((lane == first) | (lane == second)).astype(F32)
    before = (
        lax.broadcasted_iota(jnp.int32, (frames, frames), 1)
        < lax.broadcasted_iota(jnp.int32, (frames, frames), 0)
    ).astype(F32)
    rank = jnp.dot(before, named, preferred_element_type=F32) + (lane * capacity).astype(F32)
    slot = lax.broadcasted_iota(jnp.int32, (frames, experts * capacity), 1).astype(F32)
    picks = []
    for chosen in (first, second):
        place = jnp.sum(jnp.where(lane == chosen, rank, 0.0), axis=1, keepdims=True)
        picks.append((slot == place).astype(F32).astype(BF16))
    gate = gate_ref[:, 0:1]
    copy.wait()
    step = mixed_ref.shape[1] // 2
    for part in range(0, 2 * step, step):
        where = slice(part, part + step)
        back = [jnp.dot(pick, answer_ref[:, where], preferred_element_type=F32) for pick in picks]
        result = mixed_ref[:, where].astype(F32) + gate * back[0] + (1.0 - gate) * back[1]
        out_ref[0, :, where] = result.astype(BF16)


def spread_over(block, axis, low):
    held = {0: block}
    bit = lax.axis_size(axis) // 2
    while bit >= low:
        for k in list(held):
            held[k | bit] = swap(held[k], axis, bit)
        bit //= 2
    return held


def cut(size, shares):
    starts = [round(sum(shares[:i]) * size / sum(shares) / 128) * 128 for i in range(len(shares) + 1)]
    return [(a, b - a) for a, b in zip(starts, starts[1:])]


def after(values, earlier):
    return lax.optimization_barrier((values, earlier))[0]


def body(
    frames_in, pit_order, expert_ids, norm_gains, attn_qkv, attn_out, router, expert_in, expert_out
):
    dp_count = lax.axis_size("dp")
    exp_count = lax.axis_size("expert")
    me = lax.axis_index("dp").astype(jnp.int32)
    exp_index = lax.axis_index("expert").astype(jnp.int32)
    frames, width = frames_in.shape[1:]
    top = expert_ids.shape[2]
    capacity = frames * top * 5 // (4 * exp_count)
    slots_count = exp_count * capacity
    half = dp_count // 2
    share = width // dp_count
    inner = expert_in.shape[2]

    raw = spread_over(frames_in, "dp", 2)

    qkv = {0: lax.dynamic_slice_in_dim(attn_qkv, me * share, share, axis=2)}
    for far in range(2, exp_count, 2):
        qkv[far] = swap(qkv[0], "expert", far)
    for far in range(0, exp_count, 2):
        qkv[far | 1] = swap(qkv[far], "expert", 1)

    rows = width // 2
    proj_near = lax.all_gather(
        lax.dynamic_slice_in_dim(attn_out, (me % 2) * rows, rows, axis=1),
        "expert",
        axis=0,
        tiled=True,
    )

    in_cuts = cut(inner, (2, 3, 1, 2))
    in_chunks = pl.pallas_call(
        functools.partial(split_kernel, in_cuts),
        out_shape=[jax.ShapeDtypeStruct((1, width, n), BF16) for _, n in in_cuts],
        in_specs=[HBM],
        out_specs=[HBM] * len(in_cuts),
        scratch_shapes=[pltpu.SemaphoreType.DMA((len(in_cuts),))],
        compiler_params=params(20),
        cost_estimate=cost(0, 4 << 20),
        name="split",
    )(expert_in)
    in_held = [spread_over(in_chunks[0], "dp", 2)]

    early = [qkv[1], *[qkv[k] for k in range(2, exp_count, 2)], qkv[3], in_held[0]]
    raw[half] = after(raw[half], early)

    groups = len(raw)
    member = jnp.arange(groups, dtype=jnp.int32) * 2
    meeting = ((me ^ member) % half) * exp_count + exp_index
    place = jnp.where(pit_order[meeting, 0] == 0, member, member ^ half) // 2

    near, stream = pl.pallas_call(
        functools.partial(norm_kernel, groups),
        out_shape=(
            jax.ShapeDtypeStruct((groups, frames, width), BF16),
            jax.ShapeDtypeStruct((frames, width), BF16),
        ),
        in_specs=[SMEM, VMEM] + [VMEM] * groups,
        out_specs=(VMEM, VMEM),
        compiler_params=params(20),
        cost_estimate=cost(groups * frames * width * 8, groups * frames * width * 4),
        name="norm",
    )(place, norm_gains, *[raw[2 * k] for k in range(groups)])
    far = swap(near, "dp", 1)
    in_held.append(spread_over(after(in_chunks[1], near), "dp", 2))
    far = after(far, in_held[1])
    in_held.append(spread_over(after(in_chunks[2], (in_held[1], far, qkv)), "dp", 2))

    contexts = pl.pallas_call(
        functools.partial(attention_kernel, dp_count, exp_count),
        out_shape=[jax.ShapeDtypeStruct((frames, share), BF16)] * dp_count,
        in_specs=[SMEM, VMEM, VMEM] + [VMEM] * exp_count,
        out_specs=[HBM] * dp_count,
        scratch_shapes=[
            pltpu.VMEM((3, width, share), BF16),
            pltpu.VMEM((dp_count, frames, share), BF16),
            pltpu.SemaphoreType.DMA((dp_count,)),
        ],
        compiler_params=params(20),
        cost_estimate=cost(
            2 * frames * width * width * 3 + 16 * frames * frames * width, 5 << 20, frames * frames * 16
        ),
        name="attention",
    )(exp_index[None], near, far, *[qkv[k] for k in range(exp_count)])

    contexts = after(contexts, in_held[2])
    crossed = [swap(contexts[k], "dp", k) for k in range(1, dp_count)]

    proj_far = swap(after(proj_near, contexts), "dp", 1)

    in_held.append(spread_over(after(in_chunks[3], crossed), "dp", 2))

    cols = expert_ids[0]
    slots, mixed, gate = pl.pallas_call(
        functools.partial(mix_kernel, dp_count, exp_count, capacity),
        out_shape=(
            jax.ShapeDtypeStruct((slots_count, width), BF16),
            jax.ShapeDtypeStruct((frames, width), BF16),
            jax.ShapeDtypeStruct((frames, 128), F32),
        ),
        in_specs=[SMEM] + [VMEM] * (7 + dp_count),
        out_specs=(HBM, HBM, VMEM),
        scratch_shapes=[
            pltpu.VMEM((frames, width), F32),
            pltpu.VMEM((slots_count, width), BF16),
            pltpu.VMEM((frames, width), BF16),
            pltpu.SemaphoreType.DMA((2,)),
        ],
        compiler_params=params(20),
        cost_estimate=cost(2 * frames * width * (width + slots_count), 5 << 20),
        name="mix",
    )(me[None], norm_gains, router.T, cols.T, cols, stream, proj_near, proj_far, contexts[0], *crossed)

    slots = after(slots, in_held[3])
    out_held = spread_over(after(expert_out, (in_held[3], mixed)), "dp", 2)
    in_far, in_near, in_places = [swap(after(expert_in, mixed), "dp", 1)], [expert_in], [(0, 0, inner)]
    out_own = swap(after(expert_out, mixed), "dp", 1)
    for k in range(2, dp_count, 2):
        for held, place in zip(in_held, in_cuts):
            in_near.append(held[k])
            in_far.append(swap(after(held[k], mixed), "dp", 1))
            in_places.append((k // 2, *place))

    arrived = lax.all_to_all(
        slots.reshape(exp_count, capacity, width), "expert", split_axis=0, concat_axis=0, tiled=True
    ).reshape(slots_count, width)


    arrived = after(arrived, (in_far, out_own))
    step = min(512, inner)

    def hidden_units(slots_in, held, name):
        return pl.pallas_call(
            functools.partial(hidden_kernel, in_places, step),
            out_shape=jax.ShapeDtypeStruct((groups, slots_count, inner), BF16),
            in_specs=[VMEM] + [VMEM] * len(in_places),
            out_specs=VMEM,
            compiler_params=params(16),
            cost_estimate=cost(2 * slots_count * width * inner * groups, 8 << 20),
            name=name,
        )(slots_in, *held)

    hidden = [hidden_units(arrived, in_near, "hidden_near")]
    hidden.append(hidden_units(after(arrived, hidden[0]), in_far, "hidden_far"))

    def answers(slices, weights, before, name):
        count = len(slices)
        used = sorted({of for of, _ in slices})
        slices = [(used.index(of), place) for of, place in slices]
        inputs = [hidden[of] for of in used]
        extra = [] if before is None else [before]
        return pl.pallas_call(
            functools.partial(answer_kernel, slices, rows, len(used), bool(extra)),
            out_shape=jax.ShapeDtypeStruct((slots_count, width), BF16 if name == "answer_far" else F32),
            in_specs=[VMEM] * (len(used) + count + len(extra)),
            out_specs=VMEM,
            compiler_params=params(16),
            cost_estimate=cost(2 * slots_count * width * inner * count, 10 << 20),
            name=name,
        )(*inputs, *weights, *extra)

    distant = range(1, groups)
    answer = answers([(0, 0), (1, 0)], [expert_out, out_own], None, "answer_own")
    out_near = [after(out_held[2 * k], hidden[1]) for k in distant]
    out_far = [swap(block, "dp", 1) for block in out_near]
    answer = answers([(0, k) for k in distant], out_near, answer, "answer_near")
    answer = answers([(1, k) for k in distant], out_far, answer, "answer_far")
    returned = lax.all_to_all(
        answer.reshape(exp_count, capacity, width), "expert", split_axis=0, concat_axis=0, tiled=True
    ).reshape(slots_count, width)

    return pl.pallas_call(
        functools.partial(combine_kernel, exp_count, capacity),
        out_shape=jax.ShapeDtypeStruct((1, frames, width), BF16),
        in_specs=[VMEM, VMEM, VMEM, HBM],
        out_specs=VMEM,
        scratch_shapes=[pltpu.VMEM((frames, width), BF16), pltpu.SemaphoreType.DMA((1,))],
        compiler_params=params(20),
        cost_estimate=cost(4 * frames * slots_count * width, 3 << 20),
        name="combine",
    )(gate, cols, returned, mixed)


def solution(mesh):
    return jax.shard_map(
        body,
        mesh=mesh,
        in_specs=(
            P(("dp", "expert"), None, None),
            P(),
            P(("dp", "expert"), None, None),
            P(),
            P(None, "expert", None),
            P("expert", None),
            P(),
            P("expert", None, "dp"),
            P("expert", "dp", None),
        ),
        out_specs=P(("dp", "expert"), None, None),
        check_vma=False,
    )
```

```python
import functools

import jax
import jax.numpy as jnp
from jax import lax
from jax.experimental import pallas as pl
from jax.experimental.pallas import tpu as pltpu
from jax.sharding import PartitionSpec as P

HEAD_DIM = 64
epsilon = 1e-05
BF16 = jnp.bfloat16
F32 = jnp.float32
VMEM = pl.BlockSpec(memory_space=pltpu.VMEM)
SMEM = pl.BlockSpec(memory_space=pltpu.SMEM)
ANY = pl.BlockSpec(memory_space=pl.ANY)
HBM = pl.BlockSpec(memory_space=pltpu.HBM)


def params(mib):
    return pltpu.CompilerParams(vmem_limit_bytes=mib << 20)


def cost(flops, moved, special=0):
    return pl.CostEstimate(flops=flops >> 8, bytes_accessed=moved >> 8, transcendentals=special >> 8)


def swap(block, axis, mask):
    count = lax.axis_size(axis)
    return lax.ppermute(block, axis, [(i, i ^ mask) for i in range(count)])


def layer_norm(values, gain):
    mean = jnp.mean(values, axis=-1, keepdims=True)
    centred = values - mean
    spread = jnp.mean(centred * centred, axis=-1, keepdims=True)
    return centred * lax.rsqrt(spread + epsilon) * gain


def norm_kernel(count, place_ref, gain_ref, *refs):
    raw, (normed_ref, own_ref) = refs[:count], refs[count:]
    gain = gain_ref[0:1, :]
    for k in range(count):
        where = place_ref[k]
        block = raw[k][0]
        normed_ref[where] = layer_norm(block.astype(F32), gain).astype(BF16)

        @pl.when(where == 0)
        def _():
            own_ref[...] = block


def attention_kernel(count, shards, me_ref, near_ref, far_ref, *refs):
    pieces, outs = refs[:shards], refs[shards : shards + count]
    weights, held, sems = refs[shards + count :]
    depth, cols = pieces[0].shape[1:]
    me = me_ref[0]
    for k in range(shards):
        weights[:, pl.ds(pl.multiple_of((me ^ k) * depth, depth), depth), :] = pieces[k][...]
    sent = []
    frames = near_ref.shape[1]
    head = lax.broadcasted_iota(jnp.int32, (frames, cols), 1) // HEAD_DIM
    scale = HEAD_DIM**-0.5
    for k in range(count):
        x = (far_ref if k & 1 else near_ref)[k >> 1]
        q, key, val = [
            jnp.dot(x, weights[i], preferred_element_type=F32).astype(BF16) for i in range(3)
        ]
        q = q * jnp.asarray(scale, BF16)
        total = jnp.zeros((frames, cols), F32)
        for h in range(cols // HEAD_DIM):
            mine = head == h
            scores = lax.dot_general(
                jnp.where(mine, q, jnp.zeros_like(q)),
                key,
                (((1,), (1,)), ((), ())),
                preferred_element_type=F32,
            )
            exps = jnp.exp(scores - jnp.max(scores, axis=-1, keepdims=True))
            norm = 1.0 / jnp.sum(exps, axis=-1, keepdims=True)
            probs = (exps * norm).astype(BF16)
            total = jnp.where(mine, jnp.dot(probs, val, preferred_element_type=F32), total)
        held[k] = total.astype(BF16)
        copy = pltpu.make_async_copy(held.at[k], outs[k], sems.at[k])
        copy.start()
        sent.append(copy)
    for copy in sent:
        copy.wait()


def mix_kernel(
    count, experts, capacity, me_ref, gain_ref, router_ref, rows_ref, cols_ref, own_ref, near_ref, far_ref, *refs
):
    blocks, (slots_out, mixed_out, gate_ref, wide, slots_ref, mixed_ref, sems) = refs[:count], refs[count:]
    frames, depth = blocks[0].shape
    me = me_ref[0]
    part = near_ref.shape[1]
    for held, side in ((near_ref, me & 1), (far_ref, 1 - (me & 1))):
        total = jnp.zeros((frames, part), F32)
        for k in range(count):
            rows = pl.ds(pl.multiple_of((me ^ k) * depth, depth), depth)
            total += jnp.dot(blocks[k][...], held[rows, :], preferred_element_type=F32)
        wide[:, pl.ds(pl.multiple_of(side * part, part), part)] = total
    mixed = (own_ref[...].astype(F32) + wide[...]).astype(BF16)
    mixed_ref[...] = mixed
    mixed_copy = pltpu.make_async_copy(mixed_ref, mixed_out, sems.at[0])
    mixed_copy.start()
    normed = layer_norm(mixed.astype(F32), gain_ref[1:2, :]).astype(BF16)
    first, second = rows_ref[0:1, :], rows_ref[1:2, :]
    which = lax.broadcasted_iota(jnp.int32, (experts, frames), 0)
    named = ((which == first) | (which == second)).astype(F32)
    before = (
        lax.broadcasted_iota(jnp.int32, (frames, frames), 0)
        < lax.broadcasted_iota(jnp.int32, (frames, frames), 1)
    ).astype(F32)
    rank = jnp.dot(named, before, preferred_element_type=F32) + (which * capacity).astype(F32)
    slot = lax.broadcasted_iota(jnp.int32, (experts * capacity, frames), 0).astype(F32)
    place0 = jnp.sum(jnp.where(which == first, rank, 0.0), axis=0, keepdims=True)
    place1 = jnp.sum(jnp.where(which == second, rank, 0.0), axis=0, keepdims=True)
    spread = ((slot == place0) | (slot == place1)).astype(F32).astype(BF16)
    slots_ref[...] = jnp.dot(spread, normed, preferred_element_type=F32).astype(BF16)
    slots_copy = pltpu.make_async_copy(slots_ref, slots_out, sems.at[1])
    slots_copy.start()
    high = router_ref[...].astype(BF16)
    rest = router_ref[...] - high.astype(F32)
    middle = rest.astype(BF16)
    low = (rest - middle.astype(F32)).astype(BF16)
    logits = sum(
        lax.dot_general(normed, term, (((1,), (1,)), ((), ())), preferred_element_type=F32)
        for term in (low, middle, high)
    )
    lane = lax.broadcasted_iota(jnp.int32, (frames, experts), 1)
    ahead = jnp.sum(jnp.where(lane == cols_ref[:, 0:1], logits, 0.0), axis=1, keepdims=True)
    behind = jnp.sum(jnp.where(lane == cols_ref[:, 1:2], logits, 0.0), axis=1, keepdims=True)
    gate_ref[...] = jnp.broadcast_to(jax.nn.sigmoid(ahead - behind), gate_ref.shape)
    mixed_copy.wait()
    slots_copy.wait()


def split_kernel(cuts, whole_ref, *refs):
    outs, sems = refs[: len(cuts)], refs[len(cuts)]
    copies = [
        pltpu.make_async_copy(whole_ref.at[:, :, pl.ds(start, size)], outs[k], sems.at[k])
        for k, (start, size) in enumerate(cuts)
    ]
    for copy in copies:
        copy.start()
    for copy in copies:
        copy.wait()


def hidden_kernel(cuts, step, slots_ref, *refs):
    hidden_ref = refs[len(cuts)]
    for weight, (at, start, size) in zip(refs, cuts):
        for part in range(0, size, step):
            end = min(part + step, size)
            half = 0.5 * jnp.dot(slots_ref[...], weight[0, :, part:end], preferred_element_type=F32)
            hidden_ref[at, :, start + part : start + end] = (half + half * jnp.tanh(half)).astype(BF16)


def answer_kernel(slices, step, held, before, *refs):
    hidden, weights, refs = refs[:held], refs[held : held + len(slices)], refs[held + len(slices) :]
    answer_ref = refs[-1]
    for part in range(0, answer_ref.shape[1], step):
        where = slice(part, part + step)
        total = refs[0][:, where] if before else 0.0
        for weight, (of, place) in zip(weights, slices):
            total += jnp.dot(hidden[of][place], weight[0, :, where], preferred_element_type=F32)
        answer_ref[:, where] = total.astype(answer_ref.dtype)


def last_answer_kernel(slices, step, held, blocks, *refs):
    me_ref, refs = refs[0], refs[1:]
    inputs, outs, total_ref = refs[: -blocks - 1], refs[-blocks - 1 : -1], refs[-1]
    answer_kernel(slices, step, held, True, *inputs, total_ref)
    size = outs[0].shape[0]
    for k, out in enumerate(outs):
        out[...] = total_ref[pl.ds(pl.multiple_of((me_ref[0] ^ k) * size, size), size), :]


def combine_kernel(experts, capacity, me_ref, gate_ref, cols_ref, mixed_in, *refs):
    blocks, (out_ref, mixed_ref, answer_ref, sems) = refs[:experts], refs[experts:]
    copy = pltpu.make_async_copy(mixed_in, mixed_ref, sems.at[0])
    copy.start()
    for k, block in enumerate(blocks):
        answer_ref[k * capacity : (k + 1) * capacity, :] = block[...]
    frames = mixed_ref.shape[0]
    first, second = cols_ref[:, 0:1], cols_ref[:, 1:2]
    lane = lax.broadcasted_iota(jnp.int32, (frames, experts), 1)
    named = ((lane == first) | (lane == second)).astype(F32)
    before = (
        lax.broadcasted_iota(jnp.int32, (frames, frames), 1)
        < lax.broadcasted_iota(jnp.int32, (frames, frames), 0)
    ).astype(F32)
    rank = jnp.dot(before, named, preferred_element_type=F32) + ((lane ^ me_ref[0]) * capacity).astype(F32)
    slot = lax.broadcasted_iota(jnp.int32, (frames, experts * capacity), 1).astype(F32)
    picks = []
    for chosen in (first, second):
        place = jnp.sum(jnp.where(lane == chosen, rank, 0.0), axis=1, keepdims=True)
        picks.append((slot == place).astype(F32).astype(BF16))
    gate = gate_ref[:, 0:1]
    copy.wait()
    step = mixed_ref.shape[1] // 2
    for part in range(0, 2 * step, step):
        where = slice(part, part + step)
        back = [jnp.dot(pick, answer_ref[:, where], preferred_element_type=F32) for pick in picks]
        result = mixed_ref[:, where].astype(F32) + gate * back[0] + (1.0 - gate) * back[1]
        out_ref[0, :, where] = result.astype(BF16)


def spread_over(block, axis, low):
    held = {0: block}
    bit = lax.axis_size(axis) // 2
    while bit >= low:
        for k in list(held):
            held[k | bit] = swap(held[k], axis, bit)
        bit //= 2
    return held


def cut(size, shares):
    starts, tiles, count = [0], size // 128, len(shares)
    for i in range(1, count + 1):
        wanted = round(sum(shares[:i]) * tiles / sum(shares))
        starts.append(min(max(wanted, starts[-1] + 1), tiles - (count - i)))
    return [(a * 128, (b - a) * 128) for a, b in zip(starts, starts[1:])]


def after(values, earlier):
    return lax.optimization_barrier((values, earlier))[0]


def body(
    frames_in, pit_order, expert_ids, norm_gains, attn_qkv, attn_out, router, expert_in, expert_out
):
    dp_count = lax.axis_size("dp")
    exp_count = lax.axis_size("expert")
    me = lax.axis_index("dp").astype(jnp.int32)
    exp_index = lax.axis_index("expert").astype(jnp.int32)
    frames, width = frames_in.shape[1:]
    top = expert_ids.shape[2]
    capacity = -(-frames * top * 5 // (4 * exp_count * 16)) * 16
    slots_count = exp_count * capacity
    half = dp_count // 2
    share = width // dp_count
    inner = expert_in.shape[2]

    raw = spread_over(frames_in, "dp", 2)

    qkv = {0: lax.dynamic_slice_in_dim(attn_qkv, me * share, share, axis=2)}
    for far in range(2, exp_count, 2):
        qkv[far] = swap(qkv[0], "expert", far)
    for far in range(0, exp_count, 2):
        qkv[far | 1] = swap(qkv[far], "expert", 1)

    rows = width // 2
    proj_near = lax.all_gather(
        lax.dynamic_slice_in_dim(attn_out, (me % 2) * rows, rows, axis=1),
        "expert",
        axis=0,
        tiled=True,
    )

    in_cuts = cut(inner, (3, 1, 2, 2))
    in_chunks = pl.pallas_call(
        functools.partial(split_kernel, in_cuts),
        out_shape=[jax.ShapeDtypeStruct((1, width, n), BF16) for _, n in in_cuts],
        in_specs=[HBM],
        out_specs=[HBM] * len(in_cuts),
        scratch_shapes=[pltpu.SemaphoreType.DMA((len(in_cuts),))],
        compiler_params=params(20),
        cost_estimate=cost(0, 4 << 20),
        name="split",
    )(expert_in)
    in_held = [spread_over(after(in_chunks[0], qkv[1]), "dp", 2)]
    in_held.append(spread_over(after(in_chunks[1], (in_held[0], qkv[exp_count - 2])), "dp", 2))
    raw[half] = after(raw[half], (qkv, in_held[1]))

    groups = len(raw)
    member = jnp.arange(groups, dtype=jnp.int32) * 2
    meeting = ((me ^ member) % half) * exp_count + exp_index
    place = jnp.where(pit_order[meeting, 0] == 0, member, member ^ half) // 2

    near, stream = pl.pallas_call(
        functools.partial(norm_kernel, groups),
        out_shape=(
            jax.ShapeDtypeStruct((groups, frames, width), BF16),
            jax.ShapeDtypeStruct((frames, width), BF16),
        ),
        in_specs=[SMEM, VMEM] + [VMEM] * groups,
        out_specs=(VMEM, VMEM),
        compiler_params=params(20),
        cost_estimate=cost(groups * frames * width * 8, groups * frames * width * 4),
        name="norm",
    )(place, norm_gains, *[raw[2 * k] for k in range(groups)])
    far = swap(near, "dp", 1)
    in_held.append(spread_over(after(in_chunks[2], near), "dp", 2))

    contexts = pl.pallas_call(
        functools.partial(attention_kernel, dp_count, exp_count),
        out_shape=[jax.ShapeDtypeStruct((frames, share), BF16)] * dp_count,
        in_specs=[SMEM, VMEM, VMEM] + [VMEM] * exp_count,
        out_specs=[HBM] * dp_count,
        scratch_shapes=[
            pltpu.VMEM((3, width, share), BF16),
            pltpu.VMEM((dp_count, frames, share), BF16),
            pltpu.SemaphoreType.DMA((dp_count,)),
        ],
        compiler_params=params(20),
        cost_estimate=cost(
            2 * frames * width * width * 3 + 16 * frames * frames * width, 5 << 20, frames * frames * 16
        ),
        name="attention",
    )(exp_index[None], near, far, *[qkv[k] for k in range(exp_count)])

    contexts = after(contexts, in_held[2])
    crossed = [swap(contexts[k], "dp", k) for k in range(1, dp_count)]

    proj_far = swap(after(proj_near, contexts), "dp", 1)

    in_held.append(spread_over(after(in_chunks[3], crossed), "dp", 2))

    cols = expert_ids[0]
    slots, mixed, gate = pl.pallas_call(
        functools.partial(mix_kernel, dp_count, exp_count, capacity),
        out_shape=(
            jax.ShapeDtypeStruct((slots_count, width), BF16),
            jax.ShapeDtypeStruct((frames, width), BF16),
            jax.ShapeDtypeStruct((frames, 128), F32),
        ),
        in_specs=[SMEM] + [VMEM] * (7 + dp_count),
        out_specs=(HBM, HBM, VMEM),
        scratch_shapes=[
            pltpu.VMEM((frames, width), F32),
            pltpu.VMEM((slots_count, width), BF16),
            pltpu.VMEM((frames, width), BF16),
            pltpu.SemaphoreType.DMA((2,)),
        ],
        compiler_params=params(20),
        cost_estimate=cost(2 * frames * width * (width + slots_count), 5 << 20),
        name="mix",
    )(me[None], norm_gains, router.T, cols.T, cols, stream, proj_near, proj_far, contexts[0], *crossed)

    slots = after(slots, in_held[3])
    out_held = spread_over(after(expert_out, (in_held[3], mixed)), "dp", 2)
    in_far, in_near, in_places = [swap(after(expert_in, mixed), "dp", 1)], [expert_in], [(0, 0, inner)]
    out_own = swap(after(expert_out, mixed), "dp", 1)
    for k in range(2, dp_count, 2):
        for held, place in zip(in_held, in_cuts):
            in_near.append(held[k])
            in_far.append(swap(after(held[k], mixed), "dp", 1))
            in_places.append((k // 2, *place))

    arrived = lax.all_to_all(
        slots.reshape(exp_count, capacity, width), "expert", split_axis=0, concat_axis=0, tiled=True
    ).reshape(slots_count, width)


    arrived = after(arrived, (in_far, out_own))
    step = min(512, inner)

    def hidden_units(slots_in, held, name):
        return pl.pallas_call(
            functools.partial(hidden_kernel, in_places, step),
            out_shape=jax.ShapeDtypeStruct((groups, slots_count, inner), BF16),
            in_specs=[VMEM] + [VMEM] * len(in_places),
            out_specs=VMEM,
            compiler_params=params(16),
            cost_estimate=cost(2 * slots_count * width * inner * groups, 8 << 20),
            name=name,
        )(slots_in, *held)

    hidden = [hidden_units(arrived, in_near, "hidden_near")]
    hidden.append(hidden_units(after(arrived, hidden[0]), in_far, "hidden_far"))

    def answers(slices, weights, before, name):
        count = len(slices)
        used = sorted({of for of, _ in slices})
        slices = [(used.index(of), place) for of, place in slices]
        inputs = [hidden[of] for of in used]
        extra = [] if before is None else [before]
        if name == "answer_far":
            return pl.pallas_call(
                functools.partial(last_answer_kernel, slices, rows, len(used), exp_count),
                out_shape=[jax.ShapeDtypeStruct((capacity, width), BF16)] * exp_count,
                in_specs=[SMEM] + [VMEM] * (len(used) + count + len(extra)),
                out_specs=[VMEM] * exp_count,
                scratch_shapes=[pltpu.VMEM((slots_count, width), BF16)],
                compiler_params=params(16),
                cost_estimate=cost(2 * slots_count * width * inner * count, 10 << 20),
                name=name,
            )(exp_index[None], *inputs, *weights, *extra)
        return pl.pallas_call(
            functools.partial(answer_kernel, slices, rows, len(used), bool(extra)),
            out_shape=jax.ShapeDtypeStruct((slots_count, width), F32),
            in_specs=[VMEM] * (len(used) + count + len(extra)),
            out_specs=VMEM,
            compiler_params=params(16),
            cost_estimate=cost(2 * slots_count * width * inner * count, 10 << 20),
            name=name,
        )(*inputs, *weights, *extra)

    distant = range(1, groups)
    answer = answers([(0, 0), (1, 0)], [expert_out, out_own], None, "answer_own")
    out_near = [after(out_held[2 * k], hidden[1]) for k in distant]
    out_far = [swap(block, "dp", 1) for block in out_near]
    answer = answers([(0, k) for k in distant], out_near, answer, "answer_near")
    answer = answers([(1, k) for k in distant], out_far, answer, "answer_far")
    returned = {k: swap(answer[k], "expert", k) for k in reversed(range(1, exp_count))}
    returned[0] = answer[0]

    return pl.pallas_call(
        functools.partial(combine_kernel, exp_count, capacity),
        out_shape=jax.ShapeDtypeStruct((1, frames, width), BF16),
        in_specs=[SMEM, VMEM, VMEM, HBM] + [VMEM] * exp_count,
        out_specs=VMEM,
        scratch_shapes=[
            pltpu.VMEM((frames, width), BF16),
            pltpu.VMEM((slots_count, width), BF16),
            pltpu.SemaphoreType.DMA((1,)),
        ],
        compiler_params=params(20),
        cost_estimate=cost(4 * frames * slots_count * width, 3 << 20),
        name="combine",
    )(exp_index[None], gate, cols, mixed, *[returned[k] for k in range(exp_count)])


def solution(mesh):
    return jax.shard_map(
        body,
        mesh=mesh,
        in_specs=(
            P(("dp", "expert"), None, None),
            P(),
            P(("dp", "expert"), None, None),
            P(),
            P(None, "expert", None),
            P("expert", None),
            P(),
            P("expert", None, "dp"),
            P("expert", "dp", None),
        ),
        out_specs=P(("dp", "expert"), None, None),
        check_vma=False,
    )
```

```python
import functools

import jax
import jax.numpy as jnp
from jax import lax
from jax.experimental import pallas as pl
from jax.experimental.pallas import tpu as pltpu
from jax.sharding import PartitionSpec as P

HEAD_DIM = 64
epsilon = 1e-05
BF16 = jnp.bfloat16
F32 = jnp.float32
VMEM = pl.BlockSpec(memory_space=pltpu.VMEM)
SMEM = pl.BlockSpec(memory_space=pltpu.SMEM)
ANY = pl.BlockSpec(memory_space=pl.ANY)
HBM = pl.BlockSpec(memory_space=pltpu.HBM)


def params(mib):
    return pltpu.CompilerParams(vmem_limit_bytes=mib << 20)


def cost(flops, moved, special=0):
    return pl.CostEstimate(flops=flops >> 8, bytes_accessed=moved >> 8, transcendentals=special >> 8)


def swap(block, axis, mask):
    count = lax.axis_size(axis)
    return lax.ppermute(block, axis, [(i, i ^ mask) for i in range(count)])


def layer_norm(values, gain):
    mean = jnp.mean(values, axis=-1, keepdims=True)
    centred = values - mean
    spread = jnp.mean(centred * centred, axis=-1, keepdims=True)
    return centred * lax.rsqrt(spread + epsilon) * gain


def norm_kernel(count, place_ref, gain_ref, *refs):
    raw, (normed_ref, own_ref) = refs[:count], refs[count:]
    gain = gain_ref[0:1, :]
    for k in range(count):
        where = place_ref[k]
        block = raw[k][0]
        normed_ref[where] = layer_norm(block.astype(F32), gain).astype(BF16)

        @pl.when(where == 0)
        def _():
            own_ref[...] = block


def attention_kernel(count, shards, me_ref, near_ref, far_ref, *refs):
    pieces, outs = refs[:shards], refs[shards : shards + count]
    weights, held, sems = refs[shards + count :]
    depth, cols = pieces[0].shape[1:]
    me = me_ref[0]
    for k in range(shards):
        weights[:, pl.ds(pl.multiple_of((me ^ k) * depth, depth), depth), :] = pieces[k][...]
    sent = []
    frames = near_ref.shape[1]
    head = lax.broadcasted_iota(jnp.int32, (frames, cols), 1) // HEAD_DIM
    scale = HEAD_DIM**-0.5
    for k in range(count):
        x = (far_ref if k & 1 else near_ref)[k >> 1]
        q, key, val = [
            jnp.dot(x, weights[i], preferred_element_type=F32).astype(BF16) for i in range(3)
        ]
        q = q * jnp.asarray(scale, BF16)
        total = jnp.zeros((frames, cols), F32)
        for h in range(cols // HEAD_DIM):
            mine = head == h
            scores = lax.dot_general(
                jnp.where(mine, q, jnp.zeros_like(q)),
                key,
                (((1,), (1,)), ((), ())),
                preferred_element_type=F32,
            )
            exps = jnp.exp(scores - jnp.max(scores, axis=-1, keepdims=True))
            norm = 1.0 / jnp.sum(exps, axis=-1, keepdims=True)
            probs = (exps * norm).astype(BF16)
            total = jnp.where(mine, jnp.dot(probs, val, preferred_element_type=F32), total)
        held[k] = total.astype(BF16)
        copy = pltpu.make_async_copy(held.at[k], outs[k], sems.at[k])
        copy.start()
        sent.append(copy)
    for copy in sent:
        copy.wait()


def mix_kernel(
    count, experts, capacity, me_ref, gain_ref, router_ref, rows_ref, cols_ref, own_ref, near_ref, far_ref, *refs
):
    blocks, (slots_out, mixed_out, gate_ref, wide, slots_ref, mixed_ref, sems) = refs[:count], refs[count:]
    frames, depth = blocks[0].shape
    me = me_ref[0]
    part = near_ref.shape[1]
    for held, side in ((near_ref, me & 1), (far_ref, 1 - (me & 1))):
        total = jnp.zeros((frames, part), F32)
        for k in range(count):
            rows = pl.ds(pl.multiple_of((me ^ k) * depth, depth), depth)
            total += jnp.dot(blocks[k][...], held[rows, :], preferred_element_type=F32)
        wide[:, pl.ds(pl.multiple_of(side * part, part), part)] = total
    mixed = (own_ref[...].astype(F32) + wide[...]).astype(BF16)
    mixed_ref[...] = mixed
    mixed_copy = pltpu.make_async_copy(mixed_ref, mixed_out, sems.at[0])
    mixed_copy.start()
    normed = layer_norm(mixed.astype(F32), gain_ref[1:2, :]).astype(BF16)
    first, second = rows_ref[0:1, :], rows_ref[1:2, :]
    which = lax.broadcasted_iota(jnp.int32, (experts, frames), 0)
    named = ((which == first) | (which == second)).astype(F32)
    before = (
        lax.broadcasted_iota(jnp.int32, (frames, frames), 0)
        < lax.broadcasted_iota(jnp.int32, (frames, frames), 1)
    ).astype(F32)
    rank = jnp.dot(named, before, preferred_element_type=F32) + (which * capacity).astype(F32)
    slot = lax.broadcasted_iota(jnp.int32, (experts * capacity, frames), 0).astype(F32)
    place0 = jnp.sum(jnp.where(which == first, rank, 0.0), axis=0, keepdims=True)
    place1 = jnp.sum(jnp.where(which == second, rank, 0.0), axis=0, keepdims=True)
    spread = ((slot == place0) | (slot == place1)).astype(F32).astype(BF16)
    slots_ref[...] = jnp.dot(spread, normed, preferred_element_type=F32).astype(BF16)
    slots_copy = pltpu.make_async_copy(slots_ref, slots_out, sems.at[1])
    slots_copy.start()
    high = router_ref[...].astype(BF16)
    rest = router_ref[...] - high.astype(F32)
    middle = rest.astype(BF16)
    low = (rest - middle.astype(F32)).astype(BF16)
    logits = sum(
        lax.dot_general(normed, term, (((1,), (1,)), ((), ())), preferred_element_type=F32)
        for term in (low, middle, high)
    )
    lane = lax.broadcasted_iota(jnp.int32, (frames, experts), 1)
    ahead = jnp.sum(jnp.where(lane == cols_ref[:, 0:1], logits, 0.0), axis=1, keepdims=True)
    behind = jnp.sum(jnp.where(lane == cols_ref[:, 1:2], logits, 0.0), axis=1, keepdims=True)
    gate_ref[...] = jnp.broadcast_to(jax.nn.sigmoid(ahead - behind), gate_ref.shape)
    mixed_copy.wait()
    slots_copy.wait()


def split_kernel(cuts, whole_ref, *refs):
    outs, sems = refs[: len(cuts)], refs[len(cuts)]
    copies = [
        pltpu.make_async_copy(whole_ref.at[:, pl.ds(start, size), :], outs[k], sems.at[k])
        for k, (start, size) in enumerate(cuts)
    ]
    for copy in copies:
        copy.start()
    for copy in copies:
        copy.wait()


def hidden_kernel(step, slots_ref, *refs):
    hidden_ref = refs[-1]
    for at, weight in enumerate(refs[:-1]):
        for part in range(0, weight.shape[2], step):
            where = slice(part, part + step)
            half = 0.5 * jnp.dot(slots_ref[...], weight[0, :, where], preferred_element_type=F32)
            hidden_ref[at, :, where] = (half + half * jnp.tanh(half)).astype(BF16)


def answer_kernel(slices, step, held, before, *refs):
    hidden, weights, refs = refs[:held], refs[held : held + len(slices)], refs[held + len(slices) :]
    answer_ref = refs[-1]
    for part in range(0, answer_ref.shape[1], step):
        where = slice(part, part + step)
        total = refs[0][:, where] if before else 0.0
        for weight, (of, place, start) in zip(weights, slices):
            units = hidden[of][place, :, start : start + weight.shape[1]]
            total += jnp.dot(units, weight[0, :, where], preferred_element_type=F32)
        answer_ref[:, where] = total.astype(answer_ref.dtype)


def last_answer_kernel(slices, step, held, blocks, *refs):
    me_ref, refs = refs[0], refs[1:]
    inputs, outs, total_ref = refs[: -blocks - 1], refs[-blocks - 1 : -1], refs[-1]
    answer_kernel(slices, step, held, True, *inputs, total_ref)
    size = outs[0].shape[0]
    for k, out in enumerate(outs):
        out[...] = total_ref[pl.ds(pl.multiple_of((me_ref[0] ^ k) * size, size), size), :]


def combine_kernel(experts, capacity, me_ref, gate_ref, cols_ref, mixed_in, *refs):
    blocks, (out_ref, mixed_ref, answer_ref, sems) = refs[:experts], refs[experts:]
    copy = pltpu.make_async_copy(mixed_in, mixed_ref, sems.at[0])
    copy.start()
    for k, block in enumerate(blocks):
        answer_ref[k * capacity : (k + 1) * capacity, :] = block[...]
    frames = mixed_ref.shape[0]
    first, second = cols_ref[:, 0:1], cols_ref[:, 1:2]
    lane = lax.broadcasted_iota(jnp.int32, (frames, experts), 1)
    named = ((lane == first) | (lane == second)).astype(F32)
    before = (
        lax.broadcasted_iota(jnp.int32, (frames, frames), 1)
        < lax.broadcasted_iota(jnp.int32, (frames, frames), 0)
    ).astype(F32)
    rank = jnp.dot(before, named, preferred_element_type=F32) + ((lane ^ me_ref[0]) * capacity).astype(F32)
    slot = lax.broadcasted_iota(jnp.int32, (frames, experts * capacity), 1).astype(F32)
    picks = []
    for chosen in (first, second):
        place = jnp.sum(jnp.where(lane == chosen, rank, 0.0), axis=1, keepdims=True)
        picks.append((slot == place).astype(F32).astype(BF16))
    gate = gate_ref[:, 0:1]
    copy.wait()
    step = mixed_ref.shape[1] // 2
    for part in range(0, 2 * step, step):
        where = slice(part, part + step)
        back = [jnp.dot(pick, answer_ref[:, where], preferred_element_type=F32) for pick in picks]
        result = mixed_ref[:, where].astype(F32) + gate * back[0] + (1.0 - gate) * back[1]
        out_ref[0, :, where] = result.astype(BF16)


def spread_over(block, axis, low):
    held = {0: block}
    bit = lax.axis_size(axis) // 2
    while bit >= low:
        for k in list(held):
            held[k | bit] = swap(held[k], axis, bit)
        bit //= 2
    return held


def cut(size, shares):
    starts, tiles, count = [0], size // 128, len(shares)
    for i in range(1, count + 1):
        wanted = round(sum(shares[:i]) * tiles / sum(shares))
        starts.append(min(max(wanted, starts[-1] + 1), tiles - (count - i)))
    return [(a * 128, (b - a) * 128) for a, b in zip(starts, starts[1:])]


def after(values, earlier):
    return lax.optimization_barrier((values, earlier))[0]


def body(
    frames_in, pit_order, expert_ids, norm_gains, attn_qkv, attn_out, router, expert_in, expert_out
):
    dp_count = lax.axis_size("dp")
    exp_count = lax.axis_size("expert")
    me = lax.axis_index("dp").astype(jnp.int32)
    exp_index = lax.axis_index("expert").astype(jnp.int32)
    frames, width = frames_in.shape[1:]
    top = expert_ids.shape[2]
    capacity = -(-frames * top * 5 // (4 * exp_count * 16)) * 16
    slots_count = exp_count * capacity
    half = dp_count // 2
    share = width // dp_count
    inner = expert_in.shape[2]

    raw = spread_over(frames_in, "dp", 2)

    qkv = {0: lax.dynamic_slice_in_dim(attn_qkv, me * share, share, axis=2)}
    for far in range(2, exp_count, 2):
        qkv[far] = swap(qkv[0], "expert", far)
    for far in range(0, exp_count, 2):
        qkv[far | 1] = swap(qkv[far], "expert", 1)

    rows = width // 2
    proj_near = lax.all_gather(
        lax.dynamic_slice_in_dim(attn_out, (me % 2) * rows, rows, axis=1),
        "expert",
        axis=0,
        tiled=True,
    )

    in_near = spread_over(after(expert_in, (raw[half], qkv[1], qkv[2], qkv[4])), "dp", 2)

    raw[half] = after(raw[half], qkv)

    groups = len(raw)
    member = jnp.arange(groups, dtype=jnp.int32) * 2
    meeting = ((me ^ member) % half) * exp_count + exp_index
    place = jnp.where(pit_order[meeting, 0] == 0, member, member ^ half) // 2

    near, stream = pl.pallas_call(
        functools.partial(norm_kernel, groups),
        out_shape=(
            jax.ShapeDtypeStruct((groups, frames, width), BF16),
            jax.ShapeDtypeStruct((frames, width), BF16),
        ),
        in_specs=[SMEM, VMEM] + [VMEM] * groups,
        out_specs=(VMEM, VMEM),
        compiler_params=params(20),
        cost_estimate=cost(groups * frames * width * 8, groups * frames * width * 4),
        name="norm",
    )(place, norm_gains, *[raw[2 * k] for k in range(groups)])
    far = swap(near, "dp", 1)

    contexts = pl.pallas_call(
        functools.partial(attention_kernel, dp_count, exp_count),
        out_shape=[jax.ShapeDtypeStruct((frames, share), BF16)] * dp_count,
        in_specs=[SMEM, VMEM, VMEM] + [VMEM] * exp_count,
        out_specs=[HBM] * dp_count,
        scratch_shapes=[
            pltpu.VMEM((3, width, share), BF16),
            pltpu.VMEM((dp_count, frames, share), BF16),
            pltpu.SemaphoreType.DMA((dp_count,)),
        ],
        compiler_params=params(20),
        cost_estimate=cost(
            2 * frames * width * width * 3 + 16 * frames * frames * width, 5 << 20, frames * frames * 16
        ),
        name="attention",
    )(exp_index[None], near, far, *[qkv[k] for k in range(exp_count)])

    contexts = [*contexts[:-1], after(contexts[-1], in_near)]
    crossed = [swap(contexts[k], "dp", k) for k in range(1, dp_count)]

    proj_far = swap(after(proj_near, contexts), "dp", 1)

    out_cuts = cut(inner, (1, 3))
    out_chunks = pl.pallas_call(
        functools.partial(split_kernel, out_cuts),
        out_shape=[jax.ShapeDtypeStruct((1, n, width), BF16) for _, n in out_cuts],
        in_specs=[HBM],
        out_specs=[HBM] * len(out_cuts),
        scratch_shapes=[pltpu.SemaphoreType.DMA((len(out_cuts),))],
        compiler_params=params(20),
        cost_estimate=cost(0, 4 << 20),
        name="split",
    )(after(expert_out, qkv))
    out_held = [spread_over(after(out_chunks[0], crossed), "dp", 2)]

    cols = expert_ids[0]
    slots, mixed, gate = pl.pallas_call(
        functools.partial(mix_kernel, dp_count, exp_count, capacity),
        out_shape=(
            jax.ShapeDtypeStruct((slots_count, width), BF16),
            jax.ShapeDtypeStruct((frames, width), BF16),
            jax.ShapeDtypeStruct((frames, 128), F32),
        ),
        in_specs=[SMEM] + [VMEM] * (7 + dp_count),
        out_specs=(HBM, HBM, VMEM),
        scratch_shapes=[
            pltpu.VMEM((frames, width), F32),
            pltpu.VMEM((slots_count, width), BF16),
            pltpu.VMEM((frames, width), BF16),
            pltpu.SemaphoreType.DMA((2,)),
        ],
        compiler_params=params(20),
        cost_estimate=cost(2 * frames * width * (width + slots_count), 5 << 20),
        name="mix",
    )(me[None], norm_gains, router.T, cols.T, cols, stream, proj_near, proj_far, contexts[0], *crossed)

    slots = after(slots, out_held[0])
    out_held.append(spread_over(after(out_chunks[1], (out_held[0], gate)), "dp", 2))
    in_far = {k: swap(after(block, gate), "dp", 1) for k, block in in_near.items()}
    out_own = swap(after(expert_out, gate), "dp", 1)

    arrived = lax.all_to_all(
        slots.reshape(exp_count, capacity, width), "expert", split_axis=0, concat_axis=0, tiled=True
    ).reshape(slots_count, width)


    out_first = {k: swap(after(block, gate), "dp", 1) for k, block in out_held[0].items() if k}
    arrived = after(arrived, (in_far, out_own, out_first))
    step = min(512, inner)

    def hidden_units(slots_in, held, name):
        return pl.pallas_call(
            functools.partial(hidden_kernel, step),
            out_shape=jax.ShapeDtypeStruct((groups, slots_count, inner), BF16),
            in_specs=[VMEM] * (1 + groups),
            out_specs=VMEM,
            compiler_params=params(16),
            cost_estimate=cost(2 * slots_count * width * inner * groups, 8 << 20),
            name=name,
        )(slots_in, *[held[k] for k in sorted(held)])

    hidden = [hidden_units(arrived, in_near, "hidden_near")]
    hidden.append(hidden_units(after(arrived, hidden[0]), in_far, "hidden_far"))

    def answers(slices, weights, before, name):
        count = len(slices)
        used = sorted({of for of, _, _ in slices})
        slices = [(used.index(of), place, start) for of, place, start in slices]
        inputs = [hidden[of] for of in used]
        extra = [] if before is None else [before]
        if name == "answer_far":
            return pl.pallas_call(
                functools.partial(last_answer_kernel, slices, rows, len(used), exp_count),
                out_shape=[jax.ShapeDtypeStruct((capacity, width), BF16)] * exp_count,
                in_specs=[SMEM] + [VMEM] * (len(used) + count + len(extra)),
                out_specs=[VMEM] * exp_count,
                scratch_shapes=[pltpu.VMEM((slots_count, width), BF16)],
                compiler_params=params(16),
                cost_estimate=cost(2 * slots_count * width * inner * count, 10 << 20),
                name=name,
            )(exp_index[None], *inputs, *weights, *extra)
        return pl.pallas_call(
            functools.partial(answer_kernel, slices, rows, len(used), bool(extra)),
            out_shape=jax.ShapeDtypeStruct((slots_count, width), F32),
            in_specs=[VMEM] * (len(used) + count + len(extra)),
            out_specs=VMEM,
            compiler_params=params(16),
            cost_estimate=cost(2 * slots_count * width * inner * count, 10 << 20),
            name=name,
        )(*inputs, *weights, *extra)

    distant = range(1, groups)
    (_, _), (rest, _) = out_cuts
    answer = answers(
        [(0, 0, 0), (1, 0, 0)] + [(of, k, 0) for of in (0, 1) for k in distant],
        [expert_out, out_own] + [held[2 * k] for held in (out_held[0], out_first) for k in distant],
        None,
        "answer_first",
    )
    out_near = [after(out_held[1][2 * k], hidden[0]) for k in distant]
    out_far = [swap(block, "dp", 1) for block in out_near]
    answer = answers([(0, k, rest) for k in distant], out_near, answer, "answer_near")
    answer = answers([(1, k, rest) for k in distant], out_far, answer, "answer_far")
    returned = {k: swap(answer[k], "expert", k) for k in reversed(range(1, exp_count))}
    returned[0] = answer[0]

    return pl.pallas_call(
        functools.partial(combine_kernel, exp_count, capacity),
        out_shape=jax.ShapeDtypeStruct((1, frames, width), BF16),
        in_specs=[SMEM, VMEM, VMEM, HBM] + [VMEM] * exp_count,
        out_specs=VMEM,
        scratch_shapes=[
            pltpu.VMEM((frames, width), BF16),
            pltpu.VMEM((slots_count, width), BF16),
            pltpu.SemaphoreType.DMA((1,)),
        ],
        compiler_params=params(20),
        cost_estimate=cost(4 * frames * slots_count * width, 3 << 20),
        name="combine",
    )(exp_index[None], gate, cols, mixed, *[returned[k] for k in range(exp_count)])


def solution(mesh):
    return jax.shard_map(
        body,
        mesh=mesh,
        in_specs=(
            P(("dp", "expert"), None, None),
            P(),
            P(("dp", "expert"), None, None),
            P(),
            P(None, "expert", None),
            P("expert", None),
            P(),
            P("expert", None, "dp"),
            P("expert", "dp", None),
        ),
        out_specs=P(("dp", "expert"), None, None),
        check_vma=False,
    )
```

```python
import functools

import jax
import jax.numpy as jnp
from jax import lax
from jax.experimental import pallas as pl
from jax.experimental.pallas import tpu as pltpu
from jax.sharding import PartitionSpec as P

HEAD_DIM = 64
epsilon = 1e-05
BF16 = jnp.bfloat16
F32 = jnp.float32
VMEM = pl.BlockSpec(memory_space=pltpu.VMEM)
SMEM = pl.BlockSpec(memory_space=pltpu.SMEM)
ANY = pl.BlockSpec(memory_space=pl.ANY)
HBM = pl.BlockSpec(memory_space=pltpu.HBM)


def params(mib):
    return pltpu.CompilerParams(vmem_limit_bytes=mib << 20)


def cost(flops, moved, special=0):
    return pl.CostEstimate(flops=flops >> 8, bytes_accessed=moved >> 8, transcendentals=special >> 8)


def swap(block, axis, mask):
    count = lax.axis_size(axis)
    return lax.ppermute(block, axis, [(i, i ^ mask) for i in range(count)])


def layer_norm(values, gain):
    mean = jnp.mean(values, axis=-1, keepdims=True)
    centred = values - mean
    spread = jnp.mean(centred * centred, axis=-1, keepdims=True)
    return centred * lax.rsqrt(spread + epsilon) * gain


def norm_kernel(count, place_ref, gain_ref, *refs):
    raw, (normed_ref, own_ref) = refs[:count], refs[count:]
    gain = gain_ref[0:1, :]
    for k in range(count):
        where = place_ref[k]
        block = raw[k][0]
        normed_ref[where] = layer_norm(block.astype(F32), gain).astype(BF16)

        @pl.when(where == 0)
        def _():
            own_ref[...] = block


def attention_kernel(count, shards, me_ref, near_ref, far_ref, *refs):
    pieces, outs = refs[:shards], refs[shards : shards + count]
    weights, held, sems = refs[shards + count :]
    depth, cols = pieces[0].shape[1:]
    me = me_ref[0]
    for k in range(shards):
        weights[:, pl.ds(pl.multiple_of((me ^ k) * depth, depth), depth), :] = pieces[k][...]
    sent = []
    frames = near_ref.shape[1]
    head = lax.broadcasted_iota(jnp.int32, (frames, cols), 1) // HEAD_DIM
    scale = HEAD_DIM**-0.5
    for k in range(count):
        x = (far_ref if k & 1 else near_ref)[k >> 1]
        q, key, val = [
            jnp.dot(x, weights[i], preferred_element_type=F32).astype(BF16) for i in range(3)
        ]
        q = q * jnp.asarray(scale, BF16)
        total = jnp.zeros((frames, cols), F32)
        for h in range(cols // HEAD_DIM):
            mine = head == h
            scores = lax.dot_general(
                jnp.where(mine, q, jnp.zeros_like(q)),
                key,
                (((1,), (1,)), ((), ())),
                preferred_element_type=F32,
            )
            exps = jnp.exp(scores - jnp.max(scores, axis=-1, keepdims=True))
            norm = 1.0 / jnp.sum(exps, axis=-1, keepdims=True)
            probs = (exps * norm).astype(BF16)
            total = jnp.where(mine, jnp.dot(probs, val, preferred_element_type=F32), total)
        held[k] = total.astype(BF16)
        copy = pltpu.make_async_copy(held.at[k], outs[k], sems.at[k])
        copy.start()
        sent.append(copy)
    for copy in sent:
        copy.wait()


def mix_kernel(
    count, experts, capacity, me_ref, gain_ref, router_ref, rows_ref, cols_ref, own_ref, near_ref, far_ref, *refs
):
    blocks, refs = refs[:count], refs[count:]
    slots_out, (mixed_out, gate_ref, wide, slots_ref, mixed_ref, sems) = refs[:experts], refs[experts:]
    frames, depth = blocks[0].shape
    me = me_ref[0]
    part = near_ref.shape[1]
    for held, side in ((near_ref, me & 1), (far_ref, 1 - (me & 1))):
        total = jnp.zeros((frames, part), F32)
        for k in range(count):
            rows = pl.ds(pl.multiple_of((me ^ k) * depth, depth), depth)
            total += jnp.dot(blocks[k][...], held[rows, :], preferred_element_type=F32)
        wide[:, pl.ds(pl.multiple_of(side * part, part), part)] = total
    mixed = (own_ref[...].astype(F32) + wide[...]).astype(BF16)
    mixed_ref[...] = mixed
    mixed_copy = pltpu.make_async_copy(mixed_ref, mixed_out, sems.at[0])
    mixed_copy.start()
    normed = layer_norm(mixed.astype(F32), gain_ref[1:2, :]).astype(BF16)
    first, second = rows_ref[0:1, :], rows_ref[1:2, :]
    which = lax.broadcasted_iota(jnp.int32, (experts, frames), 0)
    named = ((which == first) | (which == second)).astype(F32)
    before = (
        lax.broadcasted_iota(jnp.int32, (frames, frames), 0)
        < lax.broadcasted_iota(jnp.int32, (frames, frames), 1)
    ).astype(F32)
    rank = jnp.dot(named, before, preferred_element_type=F32) + (which * capacity).astype(F32)
    slot = lax.broadcasted_iota(jnp.int32, (experts * capacity, frames), 0).astype(F32)
    place0 = jnp.sum(jnp.where(which == first, rank, 0.0), axis=0, keepdims=True)
    place1 = jnp.sum(jnp.where(which == second, rank, 0.0), axis=0, keepdims=True)
    spread = ((slot == place0) | (slot == place1)).astype(F32).astype(BF16)
    slots_ref[...] = jnp.dot(spread, normed, preferred_element_type=F32).astype(BF16)
    for k, out in enumerate(slots_out):
        out[...] = slots_ref[pl.ds(pl.multiple_of((me_ref[1] ^ k) * capacity, capacity), capacity), :]
    high = router_ref[...].astype(BF16)
    rest = router_ref[...] - high.astype(F32)
    middle = rest.astype(BF16)
    low = (rest - middle.astype(F32)).astype(BF16)
    logits = sum(
        lax.dot_general(normed, term, (((1,), (1,)), ((), ())), preferred_element_type=F32)
        for term in (low, middle, high)
    )
    lane = lax.broadcasted_iota(jnp.int32, (frames, experts), 1)
    ahead = jnp.sum(jnp.where(lane == cols_ref[:, 0:1], logits, 0.0), axis=1, keepdims=True)
    behind = jnp.sum(jnp.where(lane == cols_ref[:, 1:2], logits, 0.0), axis=1, keepdims=True)
    gate_ref[...] = jnp.broadcast_to(jax.nn.sigmoid(ahead - behind), gate_ref.shape)
    mixed_copy.wait()


def split_kernel(cuts, whole_ref, *refs):
    outs, sems = refs[: len(cuts)], refs[len(cuts)]
    copies = [
        pltpu.make_async_copy(whole_ref.at[:, :, pl.ds(start, size)], outs[k], sems.at[k])
        for k, (start, size) in enumerate(cuts)
    ]
    for copy in copies:
        copy.start()
    for copy in copies:
        copy.wait()


def hidden_kernel(places, blocks, step, _, *refs):
    hidden_ref, slots_ref = refs[-2:]
    size = refs[0].shape[0]
    for k in range(blocks):
        slots_ref[k * size : (k + 1) * size, :] = refs[k][...]
    for weight, (at, start) in zip(refs[blocks:], places):
        size = weight.shape[2]
        for part in range(0, size, step):
            end = min(part + step, size)
            half = 0.5 * jnp.dot(slots_ref[...], weight[0, :, part:end], preferred_element_type=F32)
            hidden_ref[at, :, start + part : start + end] = (half + half * jnp.tanh(half)).astype(BF16)


def answer_kernel(slices, step, held, before, *refs):
    hidden, weights, refs = refs[:held], refs[held : held + len(slices)], refs[held + len(slices) :]
    answer_ref = refs[-1]
    for part in range(0, answer_ref.shape[1], step):
        where = slice(part, part + step)
        total = refs[0][:, where] if before else 0.0
        for weight, (of, place, start) in zip(weights, slices):
            units = hidden[of][place, :, start : start + weight.shape[1]]
            total += jnp.dot(units, weight[0, :, where], preferred_element_type=F32)
        answer_ref[:, where] = total.astype(answer_ref.dtype)


def last_answer_kernel(slices, step, held, blocks, *refs):
    inputs, outs, total_ref = refs[: -blocks - 1], refs[-blocks - 1 : -1], refs[-1]
    answer_kernel(slices, step, held, True, *inputs, total_ref)
    size = outs[0].shape[0]
    for k, out in enumerate(outs):
        out[...] = total_ref[k * size : (k + 1) * size, :]


def combine_kernel(experts, capacity, me_ref, gate_ref, cols_ref, mixed_in, *refs):
    blocks, (out_ref, mixed_ref, answer_ref, sems) = refs[:experts], refs[experts:]
    copy = pltpu.make_async_copy(mixed_in, mixed_ref, sems.at[0])
    copy.start()
    for k, block in enumerate(blocks):
        answer_ref[k * capacity : (k + 1) * capacity, :] = block[...]
    frames = mixed_ref.shape[0]
    first, second = cols_ref[:, 0:1], cols_ref[:, 1:2]
    lane = lax.broadcasted_iota(jnp.int32, (frames, experts), 1)
    named = ((lane == first) | (lane == second)).astype(F32)
    before = (
        lax.broadcasted_iota(jnp.int32, (frames, frames), 1)
        < lax.broadcasted_iota(jnp.int32, (frames, frames), 0)
    ).astype(F32)
    rank = jnp.dot(before, named, preferred_element_type=F32) + ((lane ^ me_ref[0]) * capacity).astype(F32)
    slot = lax.broadcasted_iota(jnp.int32, (frames, experts * capacity), 1).astype(F32)
    picks = []
    for chosen in (first, second):
        place = jnp.sum(jnp.where(lane == chosen, rank, 0.0), axis=1, keepdims=True)
        picks.append((slot == place).astype(F32).astype(BF16))
    gate = gate_ref[:, 0:1]
    copy.wait()
    step = mixed_ref.shape[1] // 2
    for part in range(0, 2 * step, step):
        where = slice(part, part + step)
        back = [jnp.dot(pick, answer_ref[:, where], preferred_element_type=F32) for pick in picks]
        result = mixed_ref[:, where].astype(F32) + gate * back[0] + (1.0 - gate) * back[1]
        out_ref[0, :, where] = result.astype(BF16)


def spread_over(block, axis, low):
    held = {0: block}
    bit = lax.axis_size(axis) // 2
    while bit >= low:
        for k in list(held):
            held[k | bit] = swap(held[k], axis, bit)
        bit //= 2
    return held


def cut(size, shares):
    starts, tiles, count = [0], size // 128, len(shares)
    for i in range(1, count + 1):
        wanted = round(sum(shares[:i]) * tiles / sum(shares))
        starts.append(min(max(wanted, starts[-1] + 1), tiles - (count - i)))
    return [(a * 128, (b - a) * 128) for a, b in zip(starts, starts[1:])]


def after(values, earlier):
    return lax.optimization_barrier((values, earlier))[0]


def body(
    frames_in, pit_order, expert_ids, norm_gains, attn_qkv, attn_out, router, expert_in, expert_out
):
    dp_count = lax.axis_size("dp")
    exp_count = lax.axis_size("expert")
    me = lax.axis_index("dp").astype(jnp.int32)
    exp_index = lax.axis_index("expert").astype(jnp.int32)
    frames, width = frames_in.shape[1:]
    top = expert_ids.shape[2]
    capacity = -(-frames * top * 5 // (4 * exp_count * 16)) * 16
    slots_count = exp_count * capacity
    half = dp_count // 2
    share = width // dp_count
    inner = expert_in.shape[2]

    raw = spread_over(frames_in, "dp", 2)

    qkv = {0: lax.dynamic_slice_in_dim(attn_qkv, me * share, share, axis=2)}
    for far in range(2, exp_count, 2):
        qkv[far] = swap(qkv[0], "expert", far)
    for far in range(0, exp_count, 2):
        qkv[far | 1] = swap(qkv[far], "expert", 1)

    rows = width // 2
    proj_near = lax.all_gather(
        lax.dynamic_slice_in_dim(attn_out, (me % 2) * rows, rows, axis=1),
        "expert",
        axis=0,
        tiled=True,
    )

    in_cuts = cut(inner, (4, 2, 2))
    in_chunks = pl.pallas_call(
        functools.partial(split_kernel, in_cuts),
        out_shape=[jax.ShapeDtypeStruct((1, width, n), BF16) for _, n in in_cuts],
        in_specs=[HBM],
        out_specs=[HBM] * len(in_cuts),
        scratch_shapes=[pltpu.SemaphoreType.DMA((len(in_cuts),))],
        compiler_params=params(1),
        cost_estimate=cost(0, 4 << 20),
        name="split",
    )(expert_in)
    first = after(in_chunks[0], (raw[half], qkv[1], qkv[2], qkv[4]))
    in_held = [spread_over(first, "dp", 2)]

    raw[half] = after(raw[half], (qkv, in_held[0]))

    groups = len(raw)
    member = jnp.arange(groups, dtype=jnp.int32) * 2
    meeting = ((me ^ member) % half) * exp_count + exp_index
    place = jnp.where(pit_order[meeting, 0] == 0, member, member ^ half) // 2

    near, stream = pl.pallas_call(
        functools.partial(norm_kernel, groups),
        out_shape=(
            jax.ShapeDtypeStruct((groups, frames, width), BF16),
            jax.ShapeDtypeStruct((frames, width), BF16),
        ),
        in_specs=[SMEM, VMEM] + [VMEM] * groups,
        out_specs=(VMEM, VMEM),
        compiler_params=params(20),
        cost_estimate=cost(groups * frames * width * 8, groups * frames * width * 4),
        name="norm",
    )(place, norm_gains, *[raw[2 * k] for k in range(groups)])
    far = swap(near, "dp", 1)
    in_held.append(spread_over(after(in_chunks[1], near), "dp", 2))
    in_core, out_own = [swap(block, "dp", 1) for block in after((expert_in, expert_out), (far, qkv))]

    contexts = pl.pallas_call(
        functools.partial(attention_kernel, dp_count, exp_count),
        out_shape=[jax.ShapeDtypeStruct((frames, share), BF16)] * dp_count,
        in_specs=[SMEM, VMEM, VMEM] + [VMEM] * exp_count,
        out_specs=[HBM] * dp_count,
        scratch_shapes=[
            pltpu.VMEM((3, width, share), BF16),
            pltpu.VMEM((dp_count, frames, share), BF16),
            pltpu.SemaphoreType.DMA((dp_count,)),
        ],
        compiler_params=params(20),
        cost_estimate=cost(
            2 * frames * width * width * 3 + 16 * frames * frames * width, 5 << 20, frames * frames * 16
        ),
        name="attention",
    )(exp_index[None], near, far, *[qkv[k] for k in range(exp_count)])

    contexts = [*contexts[:-1], after(contexts[-1], (in_held[1], in_core, out_own, proj_near))]
    crossed = [swap(contexts[k], "dp", k) for k in range(1, dp_count)]

    proj_far = swap(after(proj_near, contexts), "dp", 1)

    in_held.append(spread_over(after(in_chunks[2], crossed), "dp", 2))
    in_hop = [
        {k: swap(after(block, crossed), "dp", 1) for k, block in held.items() if k} for held in in_held[:2]
    ]

    cols = expert_ids[0]
    *slots, mixed, gate = pl.pallas_call(
        functools.partial(mix_kernel, dp_count, exp_count, capacity),
        out_shape=[jax.ShapeDtypeStruct((capacity, width), BF16)] * exp_count
        + [
            jax.ShapeDtypeStruct((frames, width), BF16),
            jax.ShapeDtypeStruct((frames, 128), F32),
        ],
        in_specs=[SMEM] + [VMEM] * (7 + dp_count),
        out_specs=[VMEM] * exp_count + [HBM, VMEM],
        scratch_shapes=[
            pltpu.VMEM((frames, width), F32),
            pltpu.VMEM((slots_count, width), BF16),
            pltpu.VMEM((frames, width), BF16),
            pltpu.SemaphoreType.DMA((1,)),
        ],
        compiler_params=params(20),
        cost_estimate=cost(2 * frames * width * (width + slots_count), 5 << 20),
        name="mix",
    )(after(jnp.stack([me, exp_index]), (in_held[2], in_hop)), norm_gains, router.T, cols.T, cols, stream, proj_near, proj_far, contexts[0], *crossed)

    out_near = spread_over(after(expert_out, in_held[2]), "dp", 2)
    long = range(exp_count // 2, exp_count)
    arrived = {k: swap(slots[k], "expert", k) for k in long}
    for k in range(1, long[0]):
        arrived[k] = swap(after(slots[k], arrived[long[0]]), "expert", k)
    arrived[0] = slots[0]
    turn = [arrived[k] for k in long]
    in_hop.append({k: swap(after(block, turn), "dp", 1) for k, block in in_held[2].items() if k})
    in_near, in_far, places = [expert_in], [in_core], [(0, 0)]
    for k in range(2, dp_count, 2):
        for held, hop, (start, _) in zip(in_held, in_hop, in_cuts):
            in_near.append(held[k])
            in_far.append(hop[k])
            places.append((k // 2, start))

    step = min(512, inner)

    def hidden_units(order, held, name):
        return pl.pallas_call(
            functools.partial(hidden_kernel, places, exp_count, step),
            out_shape=jax.ShapeDtypeStruct((groups, slots_count, inner), BF16),
            in_specs=[SMEM] + [VMEM] * (exp_count + len(held)),
            out_specs=VMEM,
            scratch_shapes=[pltpu.VMEM((slots_count, width), BF16)],
            compiler_params=params(16),
            cost_estimate=cost(2 * slots_count * width * inner * groups, 8 << 20),
            name=name,
        )(order, *[arrived[k] for k in range(exp_count)], *held)

    hidden = [hidden_units(me[None], in_near, "hidden_near")]
    hidden.append(hidden_units(after(me[None], hidden[0]), in_far, "hidden_far"))

    def answers(slices, weights, before, name):
        count = len(slices)
        used = sorted({of for of, _, _ in slices})
        slices = [(used.index(of), place, start) for of, place, start in slices]
        inputs = [hidden[of] for of in used]
        extra = [] if before is None else [before]
        if name == "answer_far":
            return pl.pallas_call(
                functools.partial(last_answer_kernel, slices, rows, len(used), exp_count),
                out_shape=[jax.ShapeDtypeStruct((capacity, width), BF16)] * exp_count,
                in_specs=[VMEM] * (len(used) + count + len(extra)),
                out_specs=[VMEM] * exp_count,
                scratch_shapes=[pltpu.VMEM((slots_count, width), BF16)],
                compiler_params=params(16),
                cost_estimate=cost(2 * slots_count * width * inner * count, 10 << 20),
                name=name,
            )(*inputs, *weights, *extra)
        return pl.pallas_call(
            functools.partial(answer_kernel, slices, rows, len(used), bool(extra)),
            out_shape=jax.ShapeDtypeStruct((slots_count, width), F32),
            in_specs=[VMEM] * (len(used) + count + len(extra)),
            out_specs=VMEM,
            compiler_params=params(16),
            cost_estimate=cost(2 * slots_count * width * inner * count, 10 << 20),
            name=name,
        )(*inputs, *weights, *extra)

    distant = range(1, groups)
    answer = answers([(0, 0, 0), (1, 0, 0)], [expert_out, out_own], None, "answer_own")
    near_weights = [after(out_near[2 * k], hidden[0]) for k in distant]
    far_weights = [swap(block, "dp", 1) for block in near_weights]
    answer = answers([(0, k, 0) for k in distant], near_weights, answer, "answer_near")
    answer = answers([(1, k, 0) for k in distant], far_weights, answer, "answer_far")
    returned = {k: swap(answer[k], "expert", k) for k in reversed(range(1, exp_count))}
    returned[0] = answer[0]

    return pl.pallas_call(
        functools.partial(combine_kernel, exp_count, capacity),
        out_shape=jax.ShapeDtypeStruct((1, frames, width), BF16),
        in_specs=[SMEM, VMEM, VMEM, HBM] + [VMEM] * exp_count,
        out_specs=VMEM,
        scratch_shapes=[
            pltpu.VMEM((frames, width), BF16),
            pltpu.VMEM((slots_count, width), BF16),
            pltpu.SemaphoreType.DMA((1,)),
        ],
        compiler_params=params(20),
        cost_estimate=cost(4 * frames * slots_count * width, 3 << 20),
        name="combine",
    )(exp_index[None], gate, cols, mixed, *[returned[k] for k in range(exp_count)])


def solution(mesh):
    return jax.shard_map(
        body,
        mesh=mesh,
        in_specs=(
            P(("dp", "expert"), None, None),
            P(),
            P(("dp", "expert"), None, None),
            P(),
            P(None, "expert", None),
            P("expert", None),
            P(),
            P("expert", None, "dp"),
            P("expert", "dp", None),
        ),
        out_specs=P(("dp", "expert"), None, None),
        check_vma=False,
    )
```

```python
import functools

import jax
import jax.numpy as jnp
from jax import lax
from jax.experimental import pallas as pl
from jax.experimental.pallas import tpu as pltpu
from jax.sharding import PartitionSpec as P

HEAD_DIM = 64
epsilon = 1e-05
BF16 = jnp.bfloat16
F32 = jnp.float32
VMEM = pl.BlockSpec(memory_space=pltpu.VMEM)
SMEM = pl.BlockSpec(memory_space=pltpu.SMEM)
ANY = pl.BlockSpec(memory_space=pl.ANY)
HBM = pl.BlockSpec(memory_space=pltpu.HBM)


def params(mib):
    return pltpu.CompilerParams(vmem_limit_bytes=mib << 20)


def cost(flops, moved, special=0):
    return pl.CostEstimate(flops=flops >> 8, bytes_accessed=moved >> 8, transcendentals=special >> 8)


def swap(block, axis, mask):
    count = lax.axis_size(axis)
    return lax.ppermute(block, axis, [(i, i ^ mask) for i in range(count)])


def layer_norm(values, gain):
    mean = jnp.mean(values, axis=-1, keepdims=True)
    centred = values - mean
    spread = jnp.mean(centred * centred, axis=-1, keepdims=True)
    return centred * lax.rsqrt(spread + epsilon) * gain


def norm_kernel(count, place_ref, gain_ref, *refs):
    raw, (normed_ref, own_ref) = refs[:count], refs[count:]
    gain = gain_ref[0:1, :]
    for k in range(count):
        where = place_ref[k]
        block = raw[k][0]
        normed_ref[where] = layer_norm(block.astype(F32), gain).astype(BF16)

        @pl.when(where == 0)
        def _():
            own_ref[...] = block


def attention_kernel(count, shards, me_ref, near_ref, far_ref, *refs):
    pieces, outs = refs[:shards], refs[shards : shards + count]
    weights, held, sems = refs[shards + count :]
    depth, cols = pieces[0].shape[1:]
    me = me_ref[0]
    for k in range(shards):
        weights[:, pl.ds(pl.multiple_of((me ^ k) * depth, depth), depth), :] = pieces[k][...]
    sent = []
    frames = near_ref.shape[1]
    head = lax.broadcasted_iota(jnp.int32, (frames, cols), 1) // HEAD_DIM
    scale = HEAD_DIM**-0.5
    for k in range(count):
        x = (far_ref if k & 1 else near_ref)[k >> 1]
        q, key, val = [
            jnp.dot(x, weights[i], preferred_element_type=F32).astype(BF16) for i in range(3)
        ]
        q = q * jnp.asarray(scale, BF16)
        total = jnp.zeros((frames, cols), F32)
        for h in range(cols // HEAD_DIM):
            mine = head == h
            scores = lax.dot_general(
                jnp.where(mine, q, jnp.zeros_like(q)),
                key,
                (((1,), (1,)), ((), ())),
                preferred_element_type=F32,
            )
            exps = jnp.exp(scores - jnp.max(scores, axis=-1, keepdims=True))
            norm = 1.0 / jnp.sum(exps, axis=-1, keepdims=True)
            probs = (exps * norm).astype(BF16)
            total = jnp.where(mine, jnp.dot(probs, val, preferred_element_type=F32), total)
        held[k] = total.astype(BF16)
        copy = pltpu.make_async_copy(held.at[k], outs[k], sems.at[k])
        copy.start()
        sent.append(copy)
    for copy in sent:
        copy.wait()


def mix_kernel(
    count, experts, capacity, me_ref, gain_ref, router_ref, rows_ref, cols_ref, own_ref, near_ref, far_ref, *refs
):
    blocks, (slots_out, mixed_out, gate_ref, wide, slots_ref, mixed_ref, sems) = refs[:count], refs[count:]
    frames, depth = blocks[0].shape
    me = me_ref[0]
    part = near_ref.shape[1]
    for held, side in ((near_ref, me & 1), (far_ref, 1 - (me & 1))):
        total = jnp.zeros((frames, part), F32)
        for k in range(count):
            rows = pl.ds(pl.multiple_of((me ^ k) * depth, depth), depth)
            total += jnp.dot(blocks[k][...], held[rows, :], preferred_element_type=F32)
        wide[:, pl.ds(pl.multiple_of(side * part, part), part)] = total
    mixed = (own_ref[...].astype(F32) + wide[...]).astype(BF16)
    mixed_ref[...] = mixed
    mixed_copy = pltpu.make_async_copy(mixed_ref, mixed_out, sems.at[0])
    mixed_copy.start()
    normed = layer_norm(mixed.astype(F32), gain_ref[1:2, :]).astype(BF16)
    first, second = rows_ref[0:1, :], rows_ref[1:2, :]
    which = lax.broadcasted_iota(jnp.int32, (experts, frames), 0)
    named = ((which == first) | (which == second)).astype(F32)
    before = (
        lax.broadcasted_iota(jnp.int32, (frames, frames), 0)
        < lax.broadcasted_iota(jnp.int32, (frames, frames), 1)
    ).astype(F32)
    rank = jnp.dot(named, before, preferred_element_type=F32) + (which * capacity).astype(F32)
    slot = lax.broadcasted_iota(jnp.int32, (experts * capacity, frames), 0).astype(F32)
    place0 = jnp.sum(jnp.where(which == first, rank, 0.0), axis=0, keepdims=True)
    place1 = jnp.sum(jnp.where(which == second, rank, 0.0), axis=0, keepdims=True)
    spread = ((slot == place0) | (slot == place1)).astype(F32).astype(BF16)
    slots_ref[...] = jnp.dot(spread, normed, preferred_element_type=F32).astype(BF16)
    slots_copy = pltpu.make_async_copy(slots_ref, slots_out, sems.at[1])
    slots_copy.start()
    high = router_ref[...].astype(BF16)
    rest = router_ref[...] - high.astype(F32)
    middle = rest.astype(BF16)
    low = (rest - middle.astype(F32)).astype(BF16)
    logits = sum(
        lax.dot_general(normed, term, (((1,), (1,)), ((), ())), preferred_element_type=F32)
        for term in (low, middle, high)
    )
    lane = lax.broadcasted_iota(jnp.int32, (frames, experts), 1)
    ahead = jnp.sum(jnp.where(lane == cols_ref[:, 0:1], logits, 0.0), axis=1, keepdims=True)
    behind = jnp.sum(jnp.where(lane == cols_ref[:, 1:2], logits, 0.0), axis=1, keepdims=True)
    gate_ref[...] = jnp.broadcast_to(jax.nn.sigmoid(ahead - behind), gate_ref.shape)
    mixed_copy.wait()
    slots_copy.wait()


def split_kernel(cuts, axis, whole_ref, *refs):
    outs, sems = refs[: len(cuts)], refs[len(cuts)]
    copies = [
        pltpu.make_async_copy(whole_ref.at[(slice(None),) * axis + (pl.ds(start, size),)], outs[k], sems.at[k])
        for k, (start, size) in enumerate(cuts)
    ]
    for copy in copies:
        copy.start()
    for copy in copies:
        copy.wait()


def hidden_kernel(places, step, slots_ref, *refs):
    hidden_ref = refs[-1]
    for weight, (at, start) in zip(refs, places):
        size = weight.shape[2]
        for part in range(0, size, step):
            end = min(part + step, size)
            half = 0.5 * jnp.dot(slots_ref[...], weight[0, :, part:end], preferred_element_type=F32)
            hidden_ref[at, :, start + part : start + end] = (half + half * jnp.tanh(half)).astype(BF16)


def answer_kernel(slices, step, held, before, *refs):
    hidden, weights, refs = refs[:held], refs[held : held + len(slices)], refs[held + len(slices) :]
    answer_ref = refs[-1]
    for part in range(0, answer_ref.shape[1], step):
        where = slice(part, part + step)
        total = refs[0][:, where] if before else 0.0
        for weight, (of, place, start) in zip(weights, slices):
            units = hidden[of][place, :, start : start + weight.shape[1]]
            total += jnp.dot(units, weight[0, :, where], preferred_element_type=F32)
        answer_ref[:, where] = total.astype(answer_ref.dtype)


def last_answer_kernel(slices, step, held, blocks, *refs):
    me_ref, refs = refs[0], refs[1:]
    inputs, outs, total_ref = refs[: -blocks - 1], refs[-blocks - 1 : -1], refs[-1]
    answer_kernel(slices, step, held, True, *inputs, total_ref)
    size = outs[0].shape[0]
    for k, out in enumerate(outs):
        out[...] = total_ref[pl.ds(pl.multiple_of((me_ref[0] ^ k) * size, size), size), :]


def combine_kernel(experts, capacity, me_ref, gate_ref, cols_ref, mixed_in, *refs):
    blocks, (out_ref, mixed_ref, answer_ref, sems) = refs[:experts], refs[experts:]
    copy = pltpu.make_async_copy(mixed_in, mixed_ref, sems.at[0])
    copy.start()
    for k, block in enumerate(blocks):
        answer_ref[k * capacity : (k + 1) * capacity, :] = block[...]
    frames = mixed_ref.shape[0]
    first, second = cols_ref[:, 0:1], cols_ref[:, 1:2]
    lane = lax.broadcasted_iota(jnp.int32, (frames, experts), 1)
    named = ((lane == first) | (lane == second)).astype(F32)
    before = (
        lax.broadcasted_iota(jnp.int32, (frames, frames), 1)
        < lax.broadcasted_iota(jnp.int32, (frames, frames), 0)
    ).astype(F32)
    rank = jnp.dot(before, named, preferred_element_type=F32) + ((lane ^ me_ref[0]) * capacity).astype(F32)
    slot = lax.broadcasted_iota(jnp.int32, (frames, experts * capacity), 1).astype(F32)
    picks = []
    for chosen in (first, second):
        place = jnp.sum(jnp.where(lane == chosen, rank, 0.0), axis=1, keepdims=True)
        picks.append((slot == place).astype(F32).astype(BF16))
    gate = gate_ref[:, 0:1]
    copy.wait()
    step = mixed_ref.shape[1] // 2
    for part in range(0, 2 * step, step):
        where = slice(part, part + step)
        back = [jnp.dot(pick, answer_ref[:, where], preferred_element_type=F32) for pick in picks]
        result = mixed_ref[:, where].astype(F32) + gate * back[0] + (1.0 - gate) * back[1]
        out_ref[0, :, where] = result.astype(BF16)


def spread_over(block, axis, low):
    held = {0: block}
    bit = lax.axis_size(axis) // 2
    while bit >= low:
        for k in list(held):
            held[k | bit] = swap(held[k], axis, bit)
        bit //= 2
    return held


def cut(size, shares):
    starts, tiles, count = [0], size // 128, len(shares)
    for i in range(1, count + 1):
        wanted = round(sum(shares[:i]) * tiles / sum(shares))
        starts.append(min(max(wanted, starts[-1] + 1), tiles - (count - i)))
    return [(a * 128, (b - a) * 128) for a, b in zip(starts, starts[1:])]


def after(values, earlier):
    return lax.optimization_barrier((values, earlier))[0]


def body(
    frames_in, pit_order, expert_ids, norm_gains, attn_qkv, attn_out, router, expert_in, expert_out
):
    dp_count = lax.axis_size("dp")
    exp_count = lax.axis_size("expert")
    me = lax.axis_index("dp").astype(jnp.int32)
    exp_index = lax.axis_index("expert").astype(jnp.int32)
    frames, width = frames_in.shape[1:]
    top = expert_ids.shape[2]
    capacity = -(-frames * top * 5 // (4 * exp_count * 16)) * 16
    slots_count = exp_count * capacity
    half = dp_count // 2
    share = width // dp_count
    inner = expert_in.shape[2]

    raw = spread_over(frames_in, "dp", 2)

    qkv = {0: lax.dynamic_slice_in_dim(attn_qkv, me * share, share, axis=2)}
    for far in range(2, exp_count, 2):
        qkv[far] = swap(qkv[0], "expert", far)
    for far in range(0, exp_count, 2):
        qkv[far | 1] = swap(qkv[far], "expert", 1)

    rows = width // 2
    proj_near = lax.all_gather(
        lax.dynamic_slice_in_dim(attn_out, (me % 2) * rows, rows, axis=1),
        "expert",
        axis=0,
        tiled=True,
    )

    in_cuts = cut(inner, (7, 1))
    in_chunks = pl.pallas_call(
        functools.partial(split_kernel, in_cuts, 2),
        out_shape=[jax.ShapeDtypeStruct((1, width, n), BF16) for _, n in in_cuts],
        in_specs=[HBM],
        out_specs=[HBM] * len(in_cuts),
        scratch_shapes=[pltpu.SemaphoreType.DMA((len(in_cuts),))],
        compiler_params=params(1),
        cost_estimate=cost(0, 4 << 20),
        name="split_in",
    )(expert_in)
    first = after(in_chunks[0], (raw[half], qkv[1], qkv[2], qkv[4]))
    in_held = [spread_over(first, "dp", 2)]

    raw[half] = after(raw[half], qkv)

    groups = len(raw)
    member = jnp.arange(groups, dtype=jnp.int32) * 2
    meeting = ((me ^ member) % half) * exp_count + exp_index
    place = jnp.where(pit_order[meeting, 0] == 0, member, member ^ half) // 2

    near, stream = pl.pallas_call(
        functools.partial(norm_kernel, groups),
        out_shape=(
            jax.ShapeDtypeStruct((groups, frames, width), BF16),
            jax.ShapeDtypeStruct((frames, width), BF16),
        ),
        in_specs=[SMEM, VMEM] + [VMEM] * groups,
        out_specs=(VMEM, VMEM),
        compiler_params=params(20),
        cost_estimate=cost(groups * frames * width * 8, groups * frames * width * 4),
        name="norm",
    )(place, norm_gains, *[raw[2 * k] for k in range(groups)])
    far = swap(near, "dp", 1)

    contexts = pl.pallas_call(
        functools.partial(attention_kernel, dp_count, exp_count),
        out_shape=[jax.ShapeDtypeStruct((frames, share), BF16)] * dp_count,
        in_specs=[SMEM, VMEM, VMEM] + [VMEM] * exp_count,
        out_specs=[HBM] * dp_count,
        scratch_shapes=[
            pltpu.VMEM((3, width, share), BF16),
            pltpu.VMEM((dp_count, frames, share), BF16),
            pltpu.SemaphoreType.DMA((dp_count,)),
        ],
        compiler_params=params(20),
        cost_estimate=cost(
            2 * frames * width * width * 3 + 16 * frames * frames * width, 5 << 20, frames * frames * 16
        ),
        name="attention",
    )(exp_index[None], near, far, *[qkv[k] for k in range(exp_count)])

    contexts = [*contexts[:-1], after(contexts[-1], in_held[0])]
    crossed = [swap(contexts[k], "dp", k) for k in range(1, dp_count)]

    proj_far = swap(after(proj_near, contexts), "dp", 1)

    in_held.append(spread_over(after(in_chunks[1], crossed), "dp", 2))

    out_cuts = cut(inner, (1, 3))
    out_chunks = pl.pallas_call(
        functools.partial(split_kernel, out_cuts, 1),
        out_shape=[jax.ShapeDtypeStruct((1, n, width), BF16) for _, n in out_cuts],
        in_specs=[HBM],
        out_specs=[HBM] * len(out_cuts),
        scratch_shapes=[pltpu.SemaphoreType.DMA((len(out_cuts),))],
        compiler_params=params(1),
        cost_estimate=cost(0, 4 << 20),
        name="split_out",
    )(after(expert_out, qkv))
    out_held = [spread_over(after(out_chunks[0], in_held[1]), "dp", 2)]

    cols = expert_ids[0]
    slots, mixed, gate = pl.pallas_call(
        functools.partial(mix_kernel, dp_count, exp_count, capacity),
        out_shape=(
            jax.ShapeDtypeStruct((slots_count, width), BF16),
            jax.ShapeDtypeStruct((frames, width), BF16),
            jax.ShapeDtypeStruct((frames, 128), F32),
        ),
        in_specs=[SMEM] + [VMEM] * (7 + dp_count),
        out_specs=(HBM, HBM, VMEM),
        scratch_shapes=[
            pltpu.VMEM((frames, width), F32),
            pltpu.VMEM((slots_count, width), BF16),
            pltpu.VMEM((frames, width), BF16),
            pltpu.SemaphoreType.DMA((2,)),
        ],
        compiler_params=params(20),
        cost_estimate=cost(2 * frames * width * (width + slots_count), 5 << 20),
        name="mix",
    )(after(me[None], in_held[1]), norm_gains, router.T, cols.T, cols, stream, proj_near, proj_far, contexts[0], *crossed)

    slots = after(slots, out_held[0])
    out_held.append(spread_over(after(out_chunks[1], (out_held[0], gate)), "dp", 2))
    in_near, in_far, places = [expert_in], [swap(after(expert_in, gate), "dp", 1)], [(0, 0)]
    for k in range(2, dp_count, 2):
        for held, (start, _) in zip(in_held, in_cuts):
            in_near.append(held[k])
            in_far.append(swap(after(held[k], gate), "dp", 1))
            places.append((k // 2, start))
    out_own = swap(after(expert_out, gate), "dp", 1)

    arrived = lax.all_to_all(
        slots.reshape(exp_count, capacity, width), "expert", split_axis=0, concat_axis=0, tiled=True
    ).reshape(slots_count, width)


    out_first = {k: swap(after(block, gate), "dp", 1) for k, block in out_held[0].items() if k}
    arrived = after(arrived, (in_far, out_own, out_first))
    step = min(512, inner)

    def hidden_units(slots_in, held, name):
        return pl.pallas_call(
            functools.partial(hidden_kernel, places, step),
            out_shape=jax.ShapeDtypeStruct((groups, slots_count, inner), BF16),
            in_specs=[VMEM] * (1 + len(places)),
            out_specs=VMEM,
            compiler_params=params(16),
            cost_estimate=cost(2 * slots_count * width * inner * groups, 8 << 20),
            name=name,
        )(slots_in, *held)

    hidden = [hidden_units(arrived, in_near, "hidden_near")]
    hidden.append(hidden_units(after(arrived, hidden[0]), in_far, "hidden_far"))

    def answers(slices, weights, before, name):
        count = len(slices)
        used = sorted({of for of, _, _ in slices})
        slices = [(used.index(of), place, start) for of, place, start in slices]
        inputs = [hidden[of] for of in used]
        extra = [] if before is None else [before]
        if name == "answer_far":
            return pl.pallas_call(
                functools.partial(last_answer_kernel, slices, rows, len(used), exp_count),
                out_shape=[jax.ShapeDtypeStruct((capacity, width), BF16)] * exp_count,
                in_specs=[SMEM] + [VMEM] * (len(used) + count + len(extra)),
                out_specs=[VMEM] * exp_count,
                scratch_shapes=[pltpu.VMEM((slots_count, width), BF16)],
                compiler_params=params(16),
                cost_estimate=cost(2 * slots_count * width * inner * count, 10 << 20),
                name=name,
            )(exp_index[None], *inputs, *weights, *extra)
        return pl.pallas_call(
            functools.partial(answer_kernel, slices, rows, len(used), bool(extra)),
            out_shape=jax.ShapeDtypeStruct((slots_count, width), F32),
            in_specs=[VMEM] * (len(used) + count + len(extra)),
            out_specs=VMEM,
            compiler_params=params(16),
            cost_estimate=cost(2 * slots_count * width * inner * count, 10 << 20),
            name=name,
        )(*inputs, *weights, *extra)

    distant = range(1, groups)
    (_, _), (rest, _) = out_cuts
    answer = answers(
        [(0, 0, 0), (1, 0, 0)] + [(of, k, 0) for of in (0, 1) for k in distant],
        [expert_out, out_own] + [held[2 * k] for held in (out_held[0], out_first) for k in distant],
        None,
        "answer_first",
    )
    out_near = [after(out_held[1][2 * k], hidden[0]) for k in distant]
    out_far = [swap(block, "dp", 1) for block in out_near]
    answer = answers([(0, k, rest) for k in distant], out_near, answer, "answer_near")
    answer = answers([(1, k, rest) for k in distant], out_far, answer, "answer_far")
    returned = {k: swap(answer[k], "expert", k) for k in reversed(range(1, exp_count))}
    returned[0] = answer[0]

    return pl.pallas_call(
        functools.partial(combine_kernel, exp_count, capacity),
        out_shape=jax.ShapeDtypeStruct((1, frames, width), BF16),
        in_specs=[SMEM, VMEM, VMEM, HBM] + [VMEM] * exp_count,
        out_specs=VMEM,
        scratch_shapes=[
            pltpu.VMEM((frames, width), BF16),
            pltpu.VMEM((slots_count, width), BF16),
            pltpu.SemaphoreType.DMA((1,)),
        ],
        compiler_params=params(20),
        cost_estimate=cost(4 * frames * slots_count * width, 3 << 20),
        name="combine",
    )(exp_index[None], gate, cols, mixed, *[returned[k] for k in range(exp_count)])


def solution(mesh):
    return jax.shard_map(
        body,
        mesh=mesh,
        in_specs=(
            P(("dp", "expert"), None, None),
            P(),
            P(("dp", "expert"), None, None),
            P(),
            P(None, "expert", None),
            P("expert", None),
            P(),
            P("expert", None, "dp"),
            P("expert", "dp", None),
        ),
        out_specs=P(("dp", "expert"), None, None),
        check_vma=False,
    )
```
